32 devices in a mesh: groups: 2 (over y), dp: 16 (over z, x, core).
Axes of the slice: x: 2, y: 2, z: 4, core: 2. Of those that a mesh axis runs over, the one named last changes fastest.
Arguments:
- tokens: bfloat16 [24576, 768], P(('groups', 'dp')), parts along dimension 0, may hold values from -6 to 6
- lengths: int32 [128], P(('groups', 'dp')), parts along dimension 0, may hold values from 32 to 512, as said below
- norm_gains: float32 [3, 768], replicated, may hold values from 0.1 to 1.9
- query_key_value: bfloat16 [768, 2304], replicated, may hold values from -6 to 6
- attention_out: bfloat16 [768, 768], replicated, may hold values from -0.21875 to 0.21875
- expand_weight: bfloat16 [2, 768, 2048], P(None, None, 'dp'), may hold values from -0.21875 to 0.21875
- contract_weight: bfloat16 [2048, 768], P('dp'), may hold values from -0.125 to 0.125
- pool_weight: bfloat16 [768, 768], replicated, may hold values from -0.21875 to 0.21875
- queries: bfloat16 [4096, 768], P(('groups', 'dp')), parts along dimension 0, may hold values from -6 to 6
- list_ids: int32 [4096], P(('groups', 'dp')), parts along dimension 0, may hold values from 0 to 1
- labels: int32 [4096, 32], P(('groups', 'dp')), parts along dimension 0, may hold values from 0 to 8, as said below
Outputs:
- item_vectors: float32 [128, 768], P(('groups', 'dp')), parts along dimension 0
- query_loss: float32 [4096], P(('groups', 'dp')), parts along dimension 0
The draws below stay inside these ranges and needn't reach their ends.
There are 2 independent parts, one for each index of `groups`. The reference program is written for one: setup_inputs(seed, part) draws one part's arguments, and reference() takes and returns one part's arrays. A program takes and returns all parts, laid end to end along the dimension named above; an argument that names none is the same for every part. Nothing has to cross between parts.
Inputs may be any that keep to these rules, and one draw needn't show every extreme that they name: One device's lengths sum to at most 768, and some device's to exactly 768; over all devices they sum to 256 times the number of devices of dp; some item has exactly 512 tokens. `lengths`: counting the tokens of all devices in order, the first token of device i has a rank from (i - 2) * 256 to (i + 2) * 256. `labels`: each query has exactly one candidate of relevance 8; all its other candidates have relevance 0 to 3.
All inputs are finite; a program needn't handle non-finite values.
Results may differ from the reference program's by a relative error of at most 0.0085.
Values may be sent and summed in bfloat16 or wider, within the bound.
No kernel may reach another device: no remote copies, remote signals or barrier semaphores. Data moves between devices by JAX's collectives and lax.ppermute only.
A program may use at most 128 MiB of HBM per device.

```python
import jax
import jax.numpy as jnp
from jax import lax

D = 768
HEAD = 64
FF = 2048
TOK_DEV = 256
ITEM_MIN = 32
ITEM_MAX = 512
LISTS = 2
ITEMS_DEV = 4
HOME_TOK = 768
ITEMS = 64
CAND = 32
QUERIES = 2048
N_DP = 16


def item_lengths(key):
    group_count = N_DP // 8
    light_count = 7 * ITEMS_DEV
    light_extra = 5 * TOK_DEV - light_count * ITEM_MIN
    light_base = light_extra // light_count
    light_rest = light_extra - light_base * light_count
    heavy_extra = 3 * TOK_DEV - ITEM_MAX - (ITEMS_DEV - 1) * ITEM_MIN
    heavy_base = heavy_extra // (ITEMS_DEV - 1)
    heavy_rest = heavy_extra - heavy_base * (ITEMS_DEV - 1)
    subkeys = jax.random.split(key, 5)
    ordering = jax.vmap(lambda one_key: jax.random.permutation(one_key, light_count))(jax.random.split(subkeys[0], group_count))
    bumped = (ordering < light_rest).astype(jnp.int32)
    swings = jax.random.randint(subkeys[1], (group_count, light_count // 2), -light_base, light_base + 1)
    swings = jnp.stack([swings, -swings], axis=-1).reshape(group_count, light_count)
    light_rows = (ITEM_MIN + light_base + bumped + swings).reshape(group_count, 7, ITEMS_DEV)
    heavy_tail = jnp.full((group_count, ITEMS_DEV - 1), ITEM_MIN + heavy_base, jnp.int32)
    heavy_tail = heavy_tail.at[:, 0].add(heavy_rest)
    if ITEMS_DEV >= 3:
        tilted = jax.random.randint(subkeys[2], (group_count,), -heavy_base, heavy_base + 1)
        heavy_tail = heavy_tail.at[:, 0].add(tilted).at[:, 1].add(-tilted)
    heavy_row = jnp.concatenate([jnp.full((group_count, 1), ITEM_MAX, jnp.int32), heavy_tail], axis=1)
    shuffle = jax.vmap(lambda one_key: jax.random.permutation(one_key, ITEMS_DEV))(jax.random.split(subkeys[3], group_count))
    heavy_row = jnp.take_along_axis(heavy_row, shuffle, axis=1)
    full_at = jax.random.randint(subkeys[4], (group_count,), 0, 8)
    slot_index = jnp.arange(8, dtype=jnp.int32)[None, :]
    light_index = jnp.clip(slot_index - (slot_index > full_at[:, None]).astype(jnp.int32), 0, 6)
    light_index = jnp.broadcast_to(light_index[:, :, None], (group_count, 8, ITEMS_DEV))
    spread = jnp.take_along_axis(light_rows, light_index, axis=1)
    placed = jnp.where((slot_index == full_at[:, None])[:, :, None], heavy_row[:, None, :], spread)
    return placed.reshape(N_DP * ITEMS_DEV).astype(jnp.int32)


def draw_lengths(key, part):
    key = jax.random.fold_in(key, 3)
    return item_lengths(key)


def draw_query_key_value(key, part):
    key = jax.random.fold_in(key, 11)
    deviation = D ** (-0.5)
    values = jnp.clip(jax.random.normal(key, (D, 3 * D), jnp.float32), -6.0, 6.0) * deviation
    return values.astype(jnp.bfloat16)


def draw_labels(key, part):
    key = jax.random.fold_in(key, 5)
    lower_key, chosen_key = jax.random.split(key)
    background = jax.random.randint(lower_key, (QUERIES, CAND), 0, 4)
    chosen = jax.random.randint(chosen_key, (QUERIES,), 0, CAND)
    marked = jnp.arange(CAND, dtype=jnp.int32)[None, :] == chosen[:, None]
    return jnp.where(marked, 8, background).astype(jnp.int32)


def with_ends(array, key, low, top_value):
    extent = array.shape
    spot = [jax.random.randint(jax.random.fold_in(key, axis), (), 0, extent[axis]) for axis in range(len(extent))]
    array = array.at[tuple(spot)].set(low)
    longest = extent.index(max(extent))
    spot[longest] = (spot[longest] + 1) % extent[longest]
    return array.at[tuple(spot)].set(top_value)


def block_levels(key, dims, cuts, least, top_value):
    factor_of = 1.0
    for dim, shards_of in cuts:
        steps = jax.random.uniform(jax.random.fold_in(jax.random.fold_in(key, 6), dim), (shards_of,), jnp.float32, least / len(cuts), top_value / len(cuts))
        factor_of = factor_of * jnp.repeat(jnp.exp(steps), dims[dim] // shards_of).reshape((-1,) + (1,) * (len(dims) - 1 - dim))
    return factor_of


def normal_values(stream_key, extent, scale, reach, cuts=(), kind=jnp.bfloat16):
    entries = jax.random.normal(stream_key, extent, jnp.float32) * scale
    if len(cuts) > 0:
        entries = block_levels(stream_key, extent, cuts, -0.22, 0.18) * entries
    return jnp.clip(entries, min=-reach, max=reach).astype(kind)


def setup_inputs(seed: int = 0, part: int = 0) -> dict:
    arg_keys = jax.random.split(jax.random.key(seed), 12)
    part_keys = jax.random.split(jax.random.fold_in(arg_keys[11], part), 12)
    tokens = normal_values(part_keys[0], (N_DP * HOME_TOK, D), 1.0, 6.0, ((0, 16),))
    lengths = draw_lengths(jax.random.fold_in(jax.random.fold_in(arg_keys[11], part), 71), part)
    norm_gains = jnp.clip(1.0 + 0.18 * jax.random.normal(arg_keys[2], (3, D), jnp.float32), 0.1, 1.9)
    query_key_value = draw_query_key_value(jax.random.fold_in(arg_keys[11], 71), part)
    attention_out = normal_values(arg_keys[4], (D, D), D ** -0.5, 0.21875)
    expand_weight = normal_values(arg_keys[5], (2, D, FF), D ** -0.5, 0.21875, ((2, 16),))
    contract_weight = normal_values(arg_keys[6], (FF, D), FF ** -0.5, 0.125, ((0, 16),))
    pool_weight = normal_values(arg_keys[7], (D, D), D ** -0.5, 0.21875)
    queries = normal_values(part_keys[8], (QUERIES, D), 1.0, 6.0, ((0, 16),))
    list_ids = with_ends(jax.random.randint(part_keys[9], (QUERIES,), 0, LISTS), jax.random.fold_in(part_keys[9], 1), 0, LISTS - 1).astype(jnp.int32)
    labels = draw_labels(jax.random.fold_in(jax.random.fold_in(arg_keys[11], part), 71), part)
    return dict(tokens=tokens, lengths=lengths, norm_gains=norm_gains, query_key_value=query_key_value, attention_out=attention_out, expand_weight=expand_weight, contract_weight=contract_weight, pool_weight=pool_weight, queries=queries, list_ids=list_ids, labels=labels)


epsilon = 1e-06
score_scale = 32.0

def rms_scale(values, gain_row):
    widened = values.astype(jnp.float32)
    factor = lax.rsqrt(lax.optimization_barrier(jnp.mean(widened * widened, axis=-1, keepdims=True)) + epsilon)
    return widened * factor * gain_row.astype(jnp.float32)

def unit_scale(values):
    widened = values.astype(jnp.float32)
    return widened * lax.rsqrt(lax.optimization_barrier(jnp.mean(widened * widened, axis=-1, keepdims=True)) + epsilon)

def segment_table(item_counts, row_count):
    item_ends = jnp.cumsum(item_counts.astype(jnp.int32))
    position = jnp.arange(row_count, dtype=jnp.int32)
    return lax.optimization_barrier(jnp.sum((position[:, None] >= item_ends[None, :]).astype(jnp.int32), axis=1))

def attention_block(block_tokens, segment, gain_row, query_key_value, attention_out):
    row_count = block_tokens.shape[0]
    head_count = attention_out.shape[0] // HEAD
    normed = rms_scale(block_tokens, gain_row).astype(jnp.bfloat16)
    projected = jnp.dot(normed, query_key_value, preferred_element_type=jnp.float32).astype(jnp.bfloat16)
    by_head = projected.reshape(row_count, 3, head_count, HEAD).transpose(1, 2, 0, 3)
    same_item = segment[:, None] == segment[None, :]

    def one_head(operands):
        query_rows, key_rows, value_rows = operands
        logits = jnp.dot(query_rows, key_rows.T, preferred_element_type=jnp.float32) * HEAD ** (-0.5)
        logits = jnp.where(same_item, logits, -jnp.inf)
        highest = lax.optimization_barrier(jnp.max(logits, axis=1, keepdims=True))
        weights = jnp.exp(logits - highest)
        weights = (weights / lax.optimization_barrier(jnp.sum(weights, axis=1, keepdims=True))).astype(jnp.bfloat16)
        return jnp.dot(weights, value_rows, preferred_element_type=jnp.float32).astype(jnp.bfloat16)
    mixed_heads = lax.map(one_head, (by_head[0], by_head[1], by_head[2]))
    mixed_heads = mixed_heads.transpose(1, 0, 2).reshape(row_count, head_count * HEAD)
    attended = jnp.dot(mixed_heads, attention_out, preferred_element_type=jnp.float32)
    return (block_tokens.astype(jnp.float32) + attended).astype(jnp.bfloat16)

def feed_forward(residual, gain_row, expand_weight, contract_weight):
    normed = rms_scale(residual, gain_row).astype(jnp.bfloat16)
    gate_part = jnp.dot(normed, expand_weight[0], preferred_element_type=jnp.float32)
    up_part = jnp.dot(normed, expand_weight[1], preferred_element_type=jnp.float32)
    active = (jax.nn.gelu(gate_part, approximate=True) * up_part).astype(jnp.bfloat16)
    grown_rows = jnp.dot(active, contract_weight, preferred_element_type=jnp.float32)
    return (residual.astype(jnp.float32) + grown_rows).astype(jnp.bfloat16)

def pool_items(finished, segment, item_counts, gain_row):
    final_rows = rms_scale(finished, gain_row).astype(jnp.bfloat16)
    member = (segment[None, :] == jnp.arange(item_counts.shape[0], dtype=jnp.int32)[:, None]).astype(jnp.bfloat16)
    summed = jnp.dot(member, final_rows, preferred_element_type=jnp.float32)
    return summed / item_counts.astype(jnp.float32)[:, None]

def project_items(pooled, pool_weight):
    return unit_scale(jnp.dot(pooled.astype(jnp.bfloat16), pool_weight, preferred_element_type=jnp.float32))

def list_loss(all_logits, list_ids, labels):
    per_list = all_logits.reshape(all_logits.shape[0], LISTS, -1)
    chosen = jnp.take_along_axis(per_list, list_ids.astype(jnp.int32)[:, None, None], axis=1)[:, 0, :]
    chosen = chosen * (score_scale / D)
    target = jnp.exp(labels.astype(jnp.float32))
    target = target / lax.optimization_barrier(jnp.sum(target, axis=1, keepdims=True))
    log_total = jnp.log(lax.optimization_barrier(jnp.sum(jnp.exp(chosen), axis=1)))
    return log_total - lax.optimization_barrier(jnp.sum(target * chosen, axis=1))

def reference(tokens, lengths, norm_gains, query_key_value, attention_out, expand_weight, contract_weight, pool_weight, queries, list_ids, labels):
    blocks = tokens.reshape(N_DP, HOME_TOK, D)
    count_rows = lengths.reshape(N_DP, ITEMS_DEV)

    def one_device(operands):
        block_tokens, item_counts = operands
        segment = segment_table(item_counts, HOME_TOK)
        residual = attention_block(block_tokens, segment, norm_gains[0], query_key_value, attention_out)
        finished = feed_forward(residual, norm_gains[1], expand_weight, contract_weight)
        return pool_items(finished, segment, item_counts, norm_gains[2])
    pooled = lax.map(one_device, (blocks, count_rows)).reshape(ITEMS, D)
    item_vectors = project_items(pooled, pool_weight)
    candidates = item_vectors.astype(jnp.bfloat16)
    query_unit = unit_scale(queries).astype(jnp.bfloat16)
    all_logits = jnp.dot(query_unit, candidates.T, preferred_element_type=jnp.float32)
    return (item_vectors, list_loss(all_logits, list_ids, labels))
```

```python
import functools

import jax
import jax.numpy as jnp
from jax import lax
from jax.experimental import pallas as pl
from jax.experimental.pallas import tpu as pltpu
from jax.sharding import PartitionSpec as P

D = 768
HEAD = 64
LISTS = 2
OUTER = 4
CHUNK = 256
HEADS_STEP = 4

epsilon = 1e-06
score_scale = 32.0
MIB = 1024 * 1024


def inverse_rms(widened):
    return lax.rsqrt(jnp.mean(widened * widened, axis=-1, keepdims=True) + epsilon)


def nt_dot(left, right):
    return lax.dot_general(
        left, right, (((1,), (1,)), ((), ())), preferred_element_type=jnp.float32
    )


def attention_kernel(
    items, lengths, tokens, gains, wq, wk, wv, wo, residual, normed, bias, total
):
    step = pl.program_id(0)
    rows = tokens.shape[0]
    wide = HEADS_STEP * HEAD

    @pl.when(step == 0)
    def _():
        widened = tokens[...].astype(jnp.float32)
        normed[...] = (widened * inverse_rms(widened) * gains[0:1, :]).astype(jnp.bfloat16)
        down = lax.broadcasted_iota(jnp.int32, (rows, 1), 0)
        across = lax.broadcasted_iota(jnp.int32, (1, rows), 1)
        seg_down = jnp.zeros((rows, 1), jnp.int32)
        seg_across = jnp.zeros((1, rows), jnp.int32)
        end = 0
        for item in range(items):
            end = end + lengths[item]
            seg_down += (down >= end).astype(jnp.int32)
            seg_across += (across >= end).astype(jnp.int32)
        bias[...] = jnp.where(seg_down == seg_across, 0.0, -1e30)

    x = normed[...]
    q = jnp.dot(x, wq[...], preferred_element_type=jnp.float32).astype(jnp.bfloat16)
    k = jnp.dot(x, wk[...], preferred_element_type=jnp.float32).astype(jnp.bfloat16)
    v = jnp.dot(x, wv[...], preferred_element_type=jnp.float32).astype(jnp.bfloat16)
    q = q * jnp.bfloat16(HEAD ** (-0.5))
    lane = lax.broadcasted_iota(jnp.int32, (1, wide), 1) // HEAD
    tile = 256 if rows % 256 == 0 else rows
    for start in range(0, rows, tile):
        mixed = jnp.zeros((tile, wide), jnp.float32)
        for head in range(HEADS_STEP):
            mine = lane == head
            qh = jnp.where(mine, q[start : start + tile], jnp.bfloat16(0))
            vh = jnp.where(mine, v, jnp.bfloat16(1))
            logits = nt_dot(qh, k) + bias[start : start + tile, :]
            highest = jnp.max(logits, axis=1, keepdims=True)
            weights = jnp.exp(logits - highest).astype(jnp.bfloat16)
            out = jnp.dot(weights, vh, preferred_element_type=jnp.float32)
            other = ((head + 1) % HEADS_STEP) * HEAD
            mixed = jnp.where(mine, out / out[:, other : other + 1], mixed)
        part = jnp.dot(
            mixed.astype(jnp.bfloat16), wo[...], preferred_element_type=jnp.float32
        )

        @pl.when(step == 0)
        def _():
            total[start : start + tile, :] = part

        @pl.when(step > 0)
        def _():
            total[start : start + tile, :] += part

    @pl.when(step == pl.num_programs(0) - 1)
    def _():
        residual[...] = (tokens[...].astype(jnp.float32) + total[...]).astype(jnp.bfloat16)


def attention(tokens, lengths, norm_gains, query_key_value, attention_out):
    rows = tokens.shape[0]
    wide = HEADS_STEP * HEAD
    steps = D // wide
    return pl.pallas_call(
        functools.partial(attention_kernel, lengths.shape[0]),
        grid=(steps,),
        out_shape=jax.ShapeDtypeStruct((rows, D), jnp.bfloat16),
        in_specs=[
            pl.BlockSpec(memory_space=pltpu.SMEM),
            pl.BlockSpec((rows, D), lambda h: (0, 0)),
            pl.BlockSpec(norm_gains.shape, lambda h: (0, 0)),
            pl.BlockSpec((D, wide), lambda h: (0, h)),
            pl.BlockSpec((D, wide), lambda h: (0, steps + h)),
            pl.BlockSpec((D, wide), lambda h: (0, 2 * steps + h)),
            pl.BlockSpec((wide, D), lambda h: (h, 0)),
        ],
        out_specs=pl.BlockSpec((rows, D), lambda h: (0, 0)),
        scratch_shapes=[
            pltpu.VMEM((rows, D), jnp.bfloat16),
            pltpu.VMEM((rows, rows), jnp.float32),
            pltpu.VMEM((rows, D), jnp.float32),
        ],
        compiler_params=pltpu.CompilerParams(vmem_limit_bytes=40 * MIB),
        cost_estimate=pl.CostEstimate(
            flops=20_000_000_000, bytes_accessed=6_000_000, transcendentals=7_000_000
        ),
        name="attention",
    )(
        lengths,
        tokens,
        norm_gains,
        query_key_value,
        query_key_value,
        query_key_value,
        attention_out,
    )


def feed_forward_kernel(
    items, lengths, residual, gains, wg, wu, wd, pool, vectors, candidates, normed, total
):
    step = pl.program_id(0)
    rows = residual.shape[0]

    @pl.when(step == 0)
    def _():
        widened = residual[...].astype(jnp.float32)
        normed[...] = (widened * inverse_rms(widened) * gains[1:2, :]).astype(jnp.bfloat16)
        total[...] = widened

    x = normed[...]
    gate = nt_dot(x, wg[...].reshape(CHUNK, D))
    up = nt_dot(x, wu[...].reshape(CHUNK, D))
    active = (jax.nn.gelu(gate, approximate=True) * up).astype(jnp.bfloat16)
    total[...] += jnp.dot(active, wd[...].reshape(CHUNK, D), preferred_element_type=jnp.float32)

    @pl.when(step == pl.num_programs(0) - 1)
    def _():
        finished = total[...].astype(jnp.bfloat16).astype(jnp.float32)
        final_rows = (finished * inverse_rms(finished) * gains[2:3, :]).astype(jnp.bfloat16)
        slots = 16
        across = lax.broadcasted_iota(jnp.int32, (slots, rows), 1)
        slot = lax.broadcasted_iota(jnp.int32, (slots, rows), 0)
        slot_column = lax.broadcasted_iota(jnp.int32, (slots, 1), 0)
        member = jnp.zeros((slots, rows), jnp.float32)
        counts = jnp.ones((slots, 1), jnp.float32)
        begin = 0
        for item in range(items):
            end = begin + lengths[item]
            inside = (slot == item) & (across >= begin) & (across < end)
            member = jnp.where(inside, 1.0, member)
            counts = jnp.where(slot_column == item, lengths[item].astype(jnp.float32), counts)
            begin = end
        summed = jnp.dot(
            member.astype(jnp.bfloat16), final_rows, preferred_element_type=jnp.float32
        )
        pooled = (summed / counts).astype(jnp.bfloat16)
        e = jnp.dot(pooled, pool[...], preferred_element_type=jnp.float32)
        e = e * inverse_rms(e)
        vectors[...] = e[:items, :]
        candidates[...] = e[:items, :].astype(jnp.bfloat16)


def feed_forward(residual, lengths, norm_gains, gathered, pool_weight):
    rows = residual.shape[0]
    items = lengths.shape[0]
    pieces, _, width, _ = gathered.shape
    each = CHUNK // width
    steps = pieces // each

    def weight(which):
        return pl.BlockSpec((each, 1, width, D), lambda c: (c, which, 0, 0))

    return pl.pallas_call(
        functools.partial(feed_forward_kernel, items),
        grid=(steps,),
        out_shape=(
            jax.ShapeDtypeStruct((items, D), jnp.float32),
            jax.ShapeDtypeStruct((items, D), jnp.bfloat16),
        ),
        in_specs=[
            pl.BlockSpec(memory_space=pltpu.SMEM),
            pl.BlockSpec((rows, D), lambda c: (0, 0)),
            pl.BlockSpec(norm_gains.shape, lambda c: (0, 0)),
            weight(0),
            weight(1),
            weight(2),
            pl.BlockSpec((D, D), lambda c: (0, 0)),
        ],
        out_specs=(
            pl.BlockSpec((items, D), lambda c: (0, 0)),
            pl.BlockSpec((items, D), lambda c: (0, 0)),
        ),
        scratch_shapes=[
            pltpu.VMEM((rows, D), jnp.bfloat16),
            pltpu.VMEM((rows, D), jnp.float32),
        ],
        compiler_params=pltpu.CompilerParams(vmem_limit_bytes=40 * MIB),
        cost_estimate=pl.CostEstimate(
            flops=8_000_000_000, bytes_accessed=12_000_000, transcendentals=1_600_000
        ),
        name="feed_forward",
    )(lengths, residual, norm_gains, gathered, gathered, gathered, pool_weight)


def loss_kernel(queries, list_ids, labels, candidates, loss):
    widened = queries[...].astype(jnp.float32)
    query_unit = (widened * inverse_rms(widened)).astype(jnp.bfloat16)
    each = labels.shape[0]
    chosen = None
    for which in range(LISTS):
        scores = nt_dot(candidates[which * each : (which + 1) * each, :], query_unit)
        if chosen is None:
            chosen = scores
        else:
            chosen = jnp.where(list_ids[...] == which, scores, chosen)
    chosen = chosen * (score_scale / D)
    target = jnp.exp(labels[...].astype(jnp.float32))
    target = target / jnp.sum(target, axis=0, keepdims=True)
    log_total = jnp.log(jnp.sum(jnp.exp(chosen), axis=0, keepdims=True))
    loss[...] = log_total - jnp.sum(target * chosen, axis=0, keepdims=True)


def list_loss(queries, list_ids, labels, candidates):
    count = queries.shape[0]
    return pl.pallas_call(
        loss_kernel,
        out_shape=jax.ShapeDtypeStruct((1, count), jnp.float32),
        compiler_params=pltpu.CompilerParams(vmem_limit_bytes=16 * MIB),
        name="list_loss",
    )(queries, list_ids.reshape(1, count), labels.T, candidates).reshape(count)


def shifted(value, count, mapping):
    return lax.ppermute(value, "dp", [(i, mapping(i)) for i in range(count)])


def gather_candidates(mine, count):
    inner = count // OUTER
    me = lax.axis_index("dp")
    near = [mine] + [
        shifted(mine, count, lambda i, s=s: i // inner * inner + (i % inner + s) % inner)
        for s in range(1, inner)
    ]
    near = jnp.stack(near)
    order = (me % inner - jnp.arange(inner)) % inner
    block = near[order]
    far = [block] + [
        shifted(block, count, lambda i, s=s: (i + s * inner) % count) for s in range(1, OUTER)
    ]
    order = (me // inner - jnp.arange(OUTER)) % OUTER
    return jnp.stack(far)[order].reshape(count * mine.shape[0], D)


def local(
    count,
    planes,
    tokens,
    lengths,
    norm_gains,
    query_key_value,
    attention_out,
    expand_weight,
    contract_weight,
    pool_weight,
    queries,
    list_ids,
    labels,
):
    packed = jnp.concatenate([expand_weight.transpose(0, 2, 1), contract_weight[None]], axis=0)
    width = packed.shape[1]
    if width % (16 * planes) == 0:
        width = width // planes
        packed = lax.dynamic_slice_in_dim(packed, lax.axis_index("groups") * width, width, axis=1)
        gathered = lax.all_gather(packed, ("groups", "dp"), axis=0)
    else:
        gathered = lax.all_gather(packed, "dp", axis=0)
    residual = attention(tokens, lengths, norm_gains, query_key_value, attention_out)
    item_vectors, candidates = feed_forward(
        residual, lengths, norm_gains, gathered, pool_weight
    )
    every = gather_candidates(candidates, count)
    return item_vectors, list_loss(queries, list_ids, labels, every)


def solution(mesh):
    return jax.shard_map(
        functools.partial(local, mesh.shape["dp"], mesh.shape["groups"]),
        mesh=mesh,
        in_specs=(
            P(("groups", "dp"), None),
            P(("groups", "dp")),
            P(),
            P(),
            P(),
            P(None, None, "dp"),
            P("dp", None),
            P(),
            P(("groups", "dp"), None),
            P(("groups", "dp")),
            P(("groups", "dp"), None),
        ),
        out_specs=(P(("groups", "dp"), None), P(("groups", "dp"))),
        check_vma=False,
    )
```

```python
import functools

import jax
import jax.numpy as jnp
from jax import lax
from jax.experimental import pallas as pl
from jax.experimental.pallas import tpu as pltpu
from jax.sharding import PartitionSpec as P

D = 768
HEAD = 64
LISTS = 2
OUTER = 4
CHUNK = 256
HEADS_STEP = 4

epsilon = 1e-06
score_scale = 32.0
MIB = 1024 * 1024


def inverse_rms(widened):
    return lax.rsqrt(jnp.mean(widened * widened, axis=-1, keepdims=True) + epsilon)


def nt_dot(left, right):
    return lax.dot_general(
        left, right, (((1,), (1,)), ((), ())), preferred_element_type=jnp.float32
    )


def pack_kernel(expand, contract, mine, other):
    width = mine.shape[1]
    plane = lax.axis_index("groups")

    def put(target, start):
        for which in range(2):
            target[which] = expand[which].T[start : start + width, :]
        target[2] = contract[start : start + width, :]

    @pl.when(plane == 0)
    def _():
        put(mine, 0)
        put(other, width)

    @pl.when(plane != 0)
    def _():
        put(mine, width)
        put(other, 0)


def pack_halves(expand_weight, contract_weight):
    half = jax.ShapeDtypeStruct((3, contract_weight.shape[0] // 2, D), jnp.bfloat16)
    return pl.pallas_call(
        pack_kernel,
        out_shape=(half, half),
        compiler_params=pltpu.CompilerParams(vmem_limit_bytes=8 * MIB),
        name="pack_halves",
    )(expand_weight, contract_weight)


def segments(items, lengths, rows):
    down = lax.broadcasted_iota(jnp.int32, (rows, 1), 0)
    across = lax.broadcasted_iota(jnp.int32, (1, rows), 1)
    seg_down = jnp.zeros((rows, 1), jnp.int32)
    seg_across = jnp.zeros((1, rows), jnp.int32)
    end = 0
    for item in range(items):
        end = end + lengths[item]
        seg_down += (down >= end).astype(jnp.int32)
        seg_across += (across >= end).astype(jnp.int32)
    return seg_down, seg_across


def heads_kernel(items, lengths, tokens, gains, wq, wk, wv, mixed_heads):
    rows = tokens.shape[0]
    wide = mixed_heads.shape[1]
    widened = tokens[...].astype(jnp.float32)
    x = (widened * inverse_rms(widened) * gains[0:1, :]).astype(jnp.bfloat16)
    seg_down, seg_across = segments(items, lengths, rows)
    q = jnp.dot(x, wq[...], preferred_element_type=jnp.float32).astype(jnp.bfloat16)
    k = jnp.dot(x, wk[...], preferred_element_type=jnp.float32).astype(jnp.bfloat16)
    v = jnp.dot(x, wv[...], preferred_element_type=jnp.float32).astype(jnp.bfloat16)
    q = q * jnp.bfloat16(HEAD ** (-0.5))
    lane = lax.broadcasted_iota(jnp.int32, (1, wide), 1) // HEAD
    tile = 256 if rows % 256 == 0 else rows
    for start in range(0, rows, tile):
        mixed = jnp.zeros((tile, wide), jnp.float32)
        bias = jnp.where(seg_down[start : start + tile] == seg_across, 0.0, -1e30)
        for head in range(HEADS_STEP):
            mine = lane == head
            qh = jnp.where(mine, q[start : start + tile], jnp.bfloat16(0))
            vh = jnp.where(mine, v, jnp.bfloat16(1))
            logits = nt_dot(qh, k) + bias
            highest = jnp.max(logits, axis=1, keepdims=True)
            weights = jnp.exp(logits - highest).astype(jnp.bfloat16)
            out = jnp.dot(weights, vh, preferred_element_type=jnp.float32)
            other = ((head + 1) % HEADS_STEP) * HEAD
            inverse = 1.0 / out[:, other : other + 1]
            mixed = jnp.where(mine, out * inverse, mixed)
        mixed_heads[start : start + tile, :] = mixed.astype(jnp.bfloat16)


def heads(group, tokens, lengths, norm_gains, query_key_value):
    rows = tokens.shape[0]
    wide = HEADS_STEP * HEAD
    steps = D // wide
    return pl.pallas_call(
        functools.partial(heads_kernel, lengths.shape[0]),
        grid=(1,),
        out_shape=jax.ShapeDtypeStruct((rows, wide), jnp.bfloat16),
        in_specs=[
            pl.BlockSpec(memory_space=pltpu.SMEM),
            pl.BlockSpec((rows, D), lambda i: (0, 0)),
            pl.BlockSpec(norm_gains.shape, lambda i: (0, 0)),
            pl.BlockSpec((D, wide), lambda i: (0, group)),
            pl.BlockSpec((D, wide), lambda i: (0, steps + group)),
            pl.BlockSpec((D, wide), lambda i: (0, 2 * steps + group)),
        ],
        out_specs=pl.BlockSpec((rows, wide), lambda i: (0, 0)),
        compiler_params=pltpu.CompilerParams(vmem_limit_bytes=24 * MIB),
        cost_estimate=pl.CostEstimate(
            flops=6_000_000_000, bytes_accessed=3_000_000, transcendentals=2_400_000
        ),
        name="heads",
    )(lengths, tokens, norm_gains, query_key_value, query_key_value, query_key_value)


def join_kernel(tokens, gains, wo, *refs):
    parts, (residual, normed) = refs[:-2], refs[-2:]
    wide = parts[0].shape[1]
    total = tokens[...].astype(jnp.float32)
    for group, part in enumerate(parts):
        total += jnp.dot(
            part[...], wo[group * wide : (group + 1) * wide, :], preferred_element_type=jnp.float32
        )
    rounded = total.astype(jnp.bfloat16)
    residual[...] = rounded
    widened = rounded.astype(jnp.float32)
    normed[...] = (widened * inverse_rms(widened) * gains[1:2, :]).astype(jnp.bfloat16)


def join_heads(tokens, norm_gains, attention_out, parts):
    rows = jax.ShapeDtypeStruct(tokens.shape, jnp.bfloat16)
    return pl.pallas_call(
        join_kernel,
        out_shape=(rows, rows),
        compiler_params=pltpu.CompilerParams(vmem_limit_bytes=24 * MIB),
        cost_estimate=pl.CostEstimate(
            flops=1_000_000_000, bytes_accessed=6_000_000, transcendentals=1_000
        ),
        name="join_heads",
    )(tokens, norm_gains, attention_out, *parts)


def hidden_kernel(count, resumed, x, *refs):
    blocks = refs[:count]
    before = refs[count] if resumed else None
    total = refs[-1]
    rows = x.shape[0]
    tile = 256 if rows % 256 == 0 else rows

    def weight(which, part):
        return jnp.concatenate([block[which] for block in part], axis=0)

    each = max(1, CHUNK // blocks[0].shape[1])
    groups = [blocks[i : i + each] for i in range(0, count, each)]
    for start in range(0, rows, tile):
        here = x[start : start + tile, :]
        grown = None
        for part in groups:
            gate = nt_dot(here, weight(0, part))
            up = nt_dot(here, weight(1, part))
            active = (jax.nn.gelu(gate, approximate=True) * up).astype(jnp.bfloat16)
            term = jnp.dot(active, weight(2, part), preferred_element_type=jnp.float32)
            grown = term if grown is None else grown + term
        if before is not None:
            grown = grown + before[start : start + tile, :]
        total[start : start + tile, :] = grown.astype(total.dtype)


def hidden(normed, blocks, before, kind):
    units = sum(block.shape[1] for block in blocks)
    extra = () if before is None else (before,)
    return pl.pallas_call(
        functools.partial(hidden_kernel, len(blocks), before is not None),
        out_shape=jax.ShapeDtypeStruct(normed.shape, kind),
        compiler_params=pltpu.CompilerParams(vmem_limit_bytes=28 * MIB),
        cost_estimate=pl.CostEstimate(
            flops=6 * units * normed.size, bytes_accessed=6_000_000, transcendentals=1_000_000
        ),
        name="hidden",
    )(normed, *blocks, *extra)


def pool_kernel(items, count, lengths, gains, residual, pool, *refs):
    sums, (vectors, candidates) = refs[:count], refs[count:]
    rows = residual.shape[0]
    total = residual[...].astype(jnp.float32)
    for part in sums:
        total += part[...].astype(jnp.float32)
    finished = total.astype(jnp.bfloat16).astype(jnp.float32)
    final_rows = (finished * inverse_rms(finished) * gains[2:3, :]).astype(jnp.bfloat16)
    slots = 16
    across = lax.broadcasted_iota(jnp.int32, (slots, rows), 1)
    slot = lax.broadcasted_iota(jnp.int32, (slots, rows), 0)
    slot_column = lax.broadcasted_iota(jnp.int32, (slots, 1), 0)
    member = jnp.zeros((slots, rows), jnp.float32)
    counts = jnp.ones((slots, 1), jnp.float32)
    begin = 0
    for item in range(items):
        end = begin + lengths[item]
        inside = (slot == item) & (across >= begin) & (across < end)
        member = jnp.where(inside, 1.0, member)
        counts = jnp.where(slot_column == item, lengths[item].astype(jnp.float32), counts)
        begin = end
    summed = jnp.dot(member.astype(jnp.bfloat16), final_rows, preferred_element_type=jnp.float32)
    pooled = (summed / counts).astype(jnp.bfloat16)
    e = jnp.dot(pooled, pool[...], preferred_element_type=jnp.float32)
    e = e * inverse_rms(e)
    vectors[...] = e[:items, :]
    candidates[...] = e[:items, :].astype(jnp.bfloat16)


def pool_items(lengths, norm_gains, residual, pool_weight, sums):
    items = lengths.shape[0]
    whole = pl.BlockSpec(memory_space=pltpu.VMEM)
    return pl.pallas_call(
        functools.partial(pool_kernel, items, len(sums)),
        out_shape=(
            jax.ShapeDtypeStruct((items, D), jnp.float32),
            jax.ShapeDtypeStruct((items, D), jnp.bfloat16),
        ),
        in_specs=[pl.BlockSpec(memory_space=pltpu.SMEM)] + [whole] * (3 + len(sums)),
        out_specs=(whole, whole),
        compiler_params=pltpu.CompilerParams(vmem_limit_bytes=24 * MIB),
        cost_estimate=pl.CostEstimate(
            flops=500_000_000, bytes_accessed=6_000_000, transcendentals=1_000
        ),
        name="pool_items",
    )(lengths, norm_gains, residual, pool_weight, *sums)


def loss_kernel(queries, list_ids, labels, candidates, loss):
    widened = queries[...].astype(jnp.float32)
    query_unit = (widened * inverse_rms(widened)).astype(jnp.bfloat16)
    each = labels.shape[0]
    chosen = None
    for which in range(LISTS):
        scores = nt_dot(candidates[which * each : (which + 1) * each, :], query_unit)
        if chosen is None:
            chosen = scores
        else:
            chosen = jnp.where(list_ids[...] == which, scores, chosen)
    chosen = chosen * (score_scale / D)
    target = jnp.exp(labels[...].astype(jnp.float32))
    target = target / jnp.sum(target, axis=0, keepdims=True)
    log_total = jnp.log(jnp.sum(jnp.exp(chosen), axis=0, keepdims=True))
    loss[...] = log_total - jnp.sum(target * chosen, axis=0, keepdims=True)


def list_loss(queries, list_ids, labels, candidates):
    count = queries.shape[0]
    return pl.pallas_call(
        loss_kernel,
        out_shape=jax.ShapeDtypeStruct((1, count), jnp.float32),
        compiler_params=pltpu.CompilerParams(vmem_limit_bytes=16 * MIB),
        name="list_loss",
    )(queries, list_ids.reshape(1, count), labels.T, candidates).reshape(count)


def swapped(value, count, bit):
    return lax.ppermute(value, "dp", [(i, i ^ bit) for i in range(count)])


def gather_candidates(mine, count):
    me = lax.axis_index("dp")
    block = mine
    bit = 1
    while bit < count:
        theirs = swapped(block, count, bit)
        upper = (me & bit) != 0
        block = jnp.concatenate(
            [jnp.where(upper, theirs, block), jnp.where(upper, block, theirs)], axis=0
        )
        bit *= 2
    return block


def after(value, *earlier):
    return lax.optimization_barrier((value, earlier))[0]


def local(
    count,
    planes,
    tokens,
    lengths,
    norm_gains,
    query_key_value,
    attention_out,
    expand_weight,
    contract_weight,
    pool_weight,
    queries,
    list_ids,
    labels,
):
    inner = count // OUTER
    width = contract_weight.shape[0]
    head_groups = D // (HEADS_STEP * HEAD)

    if planes == 2 and inner == 4 and width % 32 == 0:

        def along(value):
            return lax.ppermute(value, "dp", [(i, (i + inner) % count) for i in range(count)])

        def side(value):
            return swapped(value, count, 2)

        def plane(value):
            return lax.ppermute(value, "groups", [(0, 1), (1, 0)])

        mine, other = pack_halves(expand_weight, contract_weight)
        a1, b0 = along(mine), side(mine)
        part0 = heads(0, tokens, lengths, norm_gains, query_key_value)
        a2, b1, c1 = along(a1), side(a1), plane(a1)
        part1 = heads(1, after(tokens, a1, b0, part0), lengths, norm_gains, query_key_value)
        a3, b2, e1 = along(a2), side(a2), plane(b1)
        part2 = heads(2, after(tokens, a2, b1, c1, part1), lengths, norm_gains, query_key_value)
        c2, b3, e2 = along(c1), side(a3), plane(b2)
        residual, normed = join_heads(
            after(tokens, a3, b2, e1, part2), norm_gains, attention_out, (part0, part1, part2)
        )
        theirs = swapped(normed, count, 1)
        first = (mine, other, a1, b0, a2, b1, c1, a3)
        own_sum = hidden(normed, first, None, jnp.float32)
        c2, b3, e2, theirs = after((c2, b3, e2, theirs), own_sum)
        e0, c3, e3 = side(other), along(c2), plane(b3)
        second = (b2, e1, c2, b3)
        third = (e2, e0, c3, e3)
        their_sum = hidden(theirs, first, None, jnp.float32)
        own_sum = hidden(normed, second, own_sum, jnp.float32)
        their_sum = hidden(theirs, second, their_sum, jnp.float32)
        their_sum = hidden(theirs, third, their_sum, jnp.bfloat16)
        back = swapped(their_sum, count, 1)
        own_sum = hidden(after(normed, their_sum), third, own_sum, jnp.float32)
        sums = (own_sum, back)
    else:
        packed = jnp.concatenate([expand_weight.transpose(0, 2, 1), contract_weight[None]], axis=0)
        gathered = lax.all_gather(packed, "dp", axis=1, tiled=True)
        parts = [
            heads(group, tokens, lengths, norm_gains, query_key_value)
            for group in range(head_groups)
        ]
        residual, normed = join_heads(tokens, norm_gains, attention_out, parts)
        total = None
        for start in range(0, gathered.shape[1], 2 * CHUNK):
            total = hidden(normed, (gathered[:, start : start + 2 * CHUNK],), total, jnp.float32)
        sums = (total,)

    item_vectors, candidates = pool_items(lengths, norm_gains, residual, pool_weight, sums)
    every = gather_candidates(candidates, count)
    return item_vectors, list_loss(queries, list_ids, labels, every)


def solution(mesh):
    return jax.shard_map(
        functools.partial(local, mesh.shape["dp"], mesh.shape["groups"]),
        mesh=mesh,
        in_specs=(
            P(("groups", "dp"), None),
            P(("groups", "dp")),
            P(),
            P(),
            P(),
            P(None, None, "dp"),
            P("dp", None),
            P(),
            P(("groups", "dp"), None),
            P(("groups", "dp")),
            P(("groups", "dp"), None),
        ),
        out_specs=(P(("groups", "dp"), None), P(("groups", "dp"))),
        check_vma=False,
    )
```

```python
import functools

import jax
import jax.numpy as jnp
from jax import lax
from jax.experimental import pallas as pl
from jax.experimental.pallas import tpu as pltpu
from jax.sharding import PartitionSpec as P

D = 768
HEAD = 64
LISTS = 2
OUTER = 4
CHUNK = 256

epsilon = 1e-06
score_scale = 32.0
MIB = 1024 * 1024
SHORT = pl.CostEstimate(flops=1000, bytes_accessed=1000, transcendentals=0)


def inverse_rms(widened):
    return lax.rsqrt(jnp.mean(widened * widened, axis=-1, keepdims=True) + epsilon)


def nt_dot(left, right):
    return lax.dot_general(
        left, right, (((1,), (1,)), ((), ())), preferred_element_type=jnp.float32
    )


def pack_kernel(expand, contract, packed, stage, done):
    grown = pltpu.make_async_copy(expand, stage, done.at[0])
    shrunk = pltpu.make_async_copy(contract, packed.at[2], done.at[1])
    grown.start()
    shrunk.start()
    grown.wait()
    for which in range(2):
        packed[which] = stage[which].T
    shrunk.wait()


def pack_weights(expand_weight, contract_weight):
    in_place = pl.BlockSpec(memory_space=pltpu.HBM)
    return pl.pallas_call(
        pack_kernel,
        out_shape=jax.ShapeDtypeStruct((3,) + contract_weight.shape, jnp.bfloat16),
        in_specs=[in_place, in_place],
        out_specs=pl.BlockSpec(memory_space=pltpu.VMEM),
        scratch_shapes=[
            pltpu.VMEM(expand_weight.shape, jnp.bfloat16),
            pltpu.SemaphoreType.DMA((2,)),
        ],
        compiler_params=pltpu.CompilerParams(vmem_limit_bytes=60 * MIB),
        name="pack_weights",
    )(expand_weight, contract_weight)


def segments(items, lengths, rows):
    down = lax.broadcasted_iota(jnp.int32, (rows, 1), 0)
    across = lax.broadcasted_iota(jnp.int32, (1, rows), 1)
    seg_down = jnp.zeros((rows, 1), jnp.int32)
    seg_across = jnp.zeros((1, rows), jnp.int32)
    end = 0
    for item in range(items):
        end = end + lengths[item]
        seg_down += (down >= end).astype(jnp.int32)
        seg_across += (across >= end).astype(jnp.int32)
    return seg_down, seg_across


def live_rows(items, lengths):
    total = lengths[0]
    for item in range(1, items):
        total = total + lengths[item]
    return total


def row_tile(rows):
    return 256 if rows % 256 == 0 else rows


def project_kernel(
    items,
    core,
    lengths,
    their_lengths,
    tokens,
    their_tokens,
    gains,
    query_key_value,
    own,
    theirs,
    weights,
    stage,
    done,
):
    rows = their_tokens.shape[0]
    tile = row_tile(rows)
    wide = weights.shape[1] // 3
    copies = [pltpu.make_async_copy(tokens, stage, done.at[3])]
    for which in range(3):
        column = pl.multiple_of(2 * which * wide + core[0] * wide, wide)
        copies.append(
            pltpu.make_async_copy(
                query_key_value.at[:, pl.ds(column, wide)],
                weights.at[:, which * wide : (which + 1) * wide],
                done.at[which],
            )
        )
    for copy in copies:
        copy.start()
    for copy in copies:
        copy.wait()
    for counts, source, target in ((lengths, stage, own), (their_lengths, their_tokens, theirs)):
        live = live_rows(items, counts)
        for start in range(0, rows, tile):
            here = slice(start, start + tile)

            @pl.when(start < live)
            def _():
                widened = source[here, :].astype(jnp.float32)
                x = (widened * inverse_rms(widened) * gains[0:1, :]).astype(jnp.bfloat16)
                part = jnp.dot(x, weights[...], preferred_element_type=jnp.float32)
                part = part.astype(jnp.bfloat16)
                target[here, :wide] = part[:, :wide] * jnp.bfloat16(HEAD ** (-0.5))
                target[here, wide:] = part[:, wide:]


def project(core, lengths, their_lengths, tokens, their_tokens, norm_gains, query_key_value):
    rows = tokens.shape[0]
    result = jax.ShapeDtypeStruct((rows, 3 * (D // 2)), jnp.bfloat16)
    whole = pl.BlockSpec(memory_space=pltpu.VMEM)
    in_place = pl.BlockSpec(memory_space=pltpu.HBM)
    scalars = pl.BlockSpec(memory_space=pltpu.SMEM)
    return pl.pallas_call(
        functools.partial(project_kernel, lengths.shape[0]),
        in_specs=[scalars, scalars, scalars, in_place, whole, whole, in_place],
        out_specs=(whole, whole),
        out_shape=(result, result),
        scratch_shapes=[
            pltpu.VMEM((D, 3 * (D // 2)), jnp.bfloat16),
            pltpu.VMEM(tokens.shape, jnp.bfloat16),
            pltpu.SemaphoreType.DMA((4,)),
        ],
        compiler_params=pltpu.CompilerParams(vmem_limit_bytes=24 * MIB),
        cost_estimate=SHORT,
        name="project",
    )(core, lengths, their_lengths, tokens, their_tokens, norm_gains, query_key_value)


def heads_kernel(items, lengths, their_lengths, own, theirs, mixed_heads):
    rows = own.shape[0]
    tile = row_tile(rows)
    group = own.shape[1] // 3
    wide = 2 * HEAD
    lane = lax.broadcasted_iota(jnp.int32, (1, wide), 1) // HEAD

    def attend(source, target, seg_down, seg_across, start, keys):
        here = slice(start, start + tile)
        bias = jnp.where(seg_down[here] == seg_across[:, :keys], 0.0, -1e30)
        for begin in range(0, group, wide):
            q = source[here, begin : begin + wide]
            k = source[:keys, group + begin : group + begin + wide]
            v = source[:keys, 2 * group + begin : 2 * group + begin + wide]
            mixed = jnp.zeros((tile, wide), jnp.float32)
            for head in range(2):
                mine = lane == head
                qh = jnp.where(mine, q, jnp.bfloat16(0))
                vh = jnp.where(mine, v, jnp.bfloat16(1))
                logits = nt_dot(qh, k) + bias
                highest = jnp.max(logits, axis=1, keepdims=True)
                weights = jnp.exp(logits - highest).astype(jnp.bfloat16)
                out = jnp.dot(weights, vh, preferred_element_type=jnp.float32)
                other = (1 - head) * HEAD
                inverse = 1.0 / out[:, other : other + 1]
                mixed = jnp.where(mine, out * inverse, mixed)
            target[here, begin : begin + wide] = mixed.astype(jnp.bfloat16)

    for block, (counts, source) in enumerate(((lengths, own), (their_lengths, theirs))):
        live = live_rows(items, counts)
        seg_down, seg_across = segments(items, counts, rows)
        target = mixed_heads.at[block]
        for keys in range(tile, rows + 1, tile):

            @pl.when((live <= keys) & (live > keys - tile))
            def _():
                for start in range(0, keys, tile):
                    attend(source, target, seg_down, seg_across, start, keys)


def heads(lengths, their_lengths, own, theirs):
    whole = pl.BlockSpec(memory_space=pltpu.VMEM)
    scalars = pl.BlockSpec(memory_space=pltpu.SMEM)
    return pl.pallas_call(
        functools.partial(heads_kernel, lengths.shape[0]),
        out_shape=jax.ShapeDtypeStruct((2, own.shape[0], own.shape[1] // 3), jnp.bfloat16),
        in_specs=[scalars, scalars, whole, whole],
        out_specs=whole,
        compiler_params=pltpu.CompilerParams(vmem_limit_bytes=24 * MIB),
        cost_estimate=SHORT,
        name="heads",
    )(lengths, their_lengths, own, theirs)


def join_kernel(
    items,
    core,
    lengths,
    their_lengths,
    tokens,
    their_tokens,
    gains,
    wo,
    here_heads,
    there_heads,
    residual,
    normed,
    their_normed,
):
    rows = tokens.shape[0]
    tile = row_tile(rows)
    low = core[0] == 0
    blocks = (
        (lengths, tokens, residual, normed, 0),
        (their_lengths, their_tokens, None, their_normed, 1),
    )
    for counts, source, kept, target, block in blocks:
        live = live_rows(items, counts)
        for start in range(0, rows, tile):
            here = slice(start, start + tile)

            @pl.when(start < live)
            def _():
                mine, other = here_heads[block, here, :], there_heads[1 - block, here, :]
                mixed = jnp.concatenate(
                    [jnp.where(low, mine, other), jnp.where(low, other, mine)], axis=1
                )
                total = source[here, :].astype(jnp.float32)
                total += jnp.dot(mixed, wo[...], preferred_element_type=jnp.float32)
                row = start + lax.broadcasted_iota(jnp.int32, (tile, 1), 0)
                rounded = jnp.where(row < live, total, 0.0).astype(jnp.bfloat16)
                if kept is not None:
                    kept[here, :] = rounded
                widened = rounded.astype(jnp.float32)
                scaled = widened * inverse_rms(widened) * gains[1:2, :]
                target[here, :] = scaled.astype(jnp.bfloat16)

            @pl.when(start >= live)
            def _():
                if kept is not None:
                    kept[here, :] = jnp.zeros((tile, D), jnp.bfloat16)
                target[here, :] = jnp.zeros((tile, D), jnp.bfloat16)


def join_heads(core, lengths, their_lengths, *arrays):
    rows = jax.ShapeDtypeStruct(arrays[0].shape, jnp.bfloat16)
    whole = pl.BlockSpec(memory_space=pltpu.VMEM)
    scalars = pl.BlockSpec(memory_space=pltpu.SMEM)
    return pl.pallas_call(
        functools.partial(join_kernel, lengths.shape[0]),
        out_shape=(rows, rows, rows),
        in_specs=[scalars] * 3 + [whole] * len(arrays),
        out_specs=(whole, whole, whole),
        compiler_params=pltpu.CompilerParams(vmem_limit_bytes=24 * MIB),
        cost_estimate=SHORT,
        name="join_heads",
    )(core, lengths, their_lengths, *arrays)


def hidden_kernel(count, resumed, x, *refs):
    blocks = refs[:count]
    before = refs[count] if resumed else None
    total = refs[-1]
    rows = x.shape[0]
    tile = row_tile(rows)

    def weight(which, part):
        return jnp.concatenate([block[which] for block in part], axis=0)

    each = max(1, CHUNK // blocks[0].shape[1])
    groups = [blocks[i : i + each] for i in range(0, count, each)]
    for start in range(0, rows, tile):
        span = slice(start, start + tile)
        live = jnp.max(jnp.abs(x[span, :].astype(jnp.float32))) > 0.0

        @pl.when(live)
        def _():
            here = x[span, :]
            grown = None
            for part in groups:
                gate = nt_dot(here, weight(0, part))
                up = nt_dot(here, weight(1, part))
                active = (jax.nn.gelu(gate, approximate=True) * up).astype(jnp.bfloat16)
                term = jnp.dot(active, weight(2, part), preferred_element_type=jnp.float32)
                grown = term if grown is None else grown + term
            if before is not None:
                grown = grown + before[span, :]
            total[span, :] = grown.astype(total.dtype)

        @pl.when(jnp.logical_not(live))
        def _():
            total[span, :] = jnp.zeros((tile, D), total.dtype)


def hidden(normed, blocks, before, kind):
    units = sum(block.shape[1] for block in blocks)
    extra = () if before is None else (before,)
    return pl.pallas_call(
        functools.partial(hidden_kernel, len(blocks), before is not None),
        out_shape=jax.ShapeDtypeStruct(normed.shape, kind),
        compiler_params=pltpu.CompilerParams(vmem_limit_bytes=28 * MIB),
        cost_estimate=SHORT,
        name="hidden",
    )(normed, *blocks, *extra)


def pool_kernel(items, count, lengths, gains, residual, pool, *refs):
    sums, (vectors, candidates) = refs[:count], refs[count:]
    rows = residual.shape[0]
    total = residual[...].astype(jnp.float32)
    for part in sums:
        total += part[...].astype(jnp.float32)
    finished = total.astype(jnp.bfloat16).astype(jnp.float32)
    final_rows = (finished * inverse_rms(finished) * gains[2:3, :]).astype(jnp.bfloat16)
    slots = 16
    across = lax.broadcasted_iota(jnp.int32, (slots, rows), 1)
    slot = lax.broadcasted_iota(jnp.int32, (slots, rows), 0)
    slot_column = lax.broadcasted_iota(jnp.int32, (slots, 1), 0)
    member = jnp.zeros((slots, rows), jnp.float32)
    counts = jnp.ones((slots, 1), jnp.float32)
    begin = 0
    for item in range(items):
        end = begin + lengths[item]
        inside = (slot == item) & (across >= begin) & (across < end)
        member = jnp.where(inside, 1.0, member)
        counts = jnp.where(slot_column == item, lengths[item].astype(jnp.float32), counts)
        begin = end
    summed = jnp.dot(member.astype(jnp.bfloat16), final_rows, preferred_element_type=jnp.float32)
    pooled = (summed / counts).astype(jnp.bfloat16)
    e = jnp.dot(pooled, pool[...], preferred_element_type=jnp.float32)
    e = e * inverse_rms(e)
    vectors[...] = e[:items, :]
    mine = e[:items, :].astype(jnp.bfloat16)
    for device in range(candidates.shape[0]):
        candidates[device] = mine


def pool_items(devices, lengths, norm_gains, residual, pool_weight, sums):
    items = lengths.shape[0]
    whole = pl.BlockSpec(memory_space=pltpu.VMEM)
    return pl.pallas_call(
        functools.partial(pool_kernel, items, len(sums)),
        out_shape=(
            jax.ShapeDtypeStruct((items, D), jnp.float32),
            jax.ShapeDtypeStruct((devices, items, D), jnp.bfloat16),
        ),
        in_specs=[pl.BlockSpec(memory_space=pltpu.SMEM)] + [whole] * (3 + len(sums)),
        out_specs=(whole, whole),
        compiler_params=pltpu.CompilerParams(vmem_limit_bytes=24 * MIB),
        cost_estimate=SHORT,
        name="pool_items",
    )(lengths, norm_gains, residual, pool_weight, *sums)


def loss_kernel(queries, list_ids, labels, candidates, loss):
    widened = queries[...].astype(jnp.float32)
    query_unit = (widened * inverse_rms(widened)).astype(jnp.bfloat16)
    each = labels.shape[0]
    chosen = None
    for which in range(LISTS):
        scores = nt_dot(candidates[which * each : (which + 1) * each, :], query_unit)
        if chosen is None:
            chosen = scores
        else:
            chosen = jnp.where(list_ids[...] == which, scores, chosen)
    chosen = chosen * (score_scale / D)
    target = jnp.exp(labels[...].astype(jnp.float32))
    target = target / jnp.sum(target, axis=0, keepdims=True)
    log_total = jnp.log(jnp.sum(jnp.exp(chosen), axis=0, keepdims=True))
    loss[...] = log_total - jnp.sum(target * chosen, axis=0, keepdims=True)


def list_loss(queries, list_ids, labels, candidates):
    count = queries.shape[0]
    return pl.pallas_call(
        loss_kernel,
        out_shape=jax.ShapeDtypeStruct((1, count), jnp.float32),
        compiler_params=pltpu.CompilerParams(vmem_limit_bytes=16 * MIB),
        name="list_loss",
    )(queries, list_ids.reshape(1, count), labels.T, candidates).reshape(count)


def swapped(value, count, bit):
    return lax.ppermute(value, "dp", [(i, i ^ bit) for i in range(count)])


def after(value, *earlier):
    return lax.optimization_barrier((value, earlier))[0]


def local(
    count,
    planes,
    tokens,
    lengths,
    norm_gains,
    query_key_value,
    attention_out,
    expand_weight,
    contract_weight,
    pool_weight,
    queries,
    list_ids,
    labels,
):
    inner = count // OUTER
    core = (lax.axis_index("dp") % 2).astype(jnp.int32).reshape(1)
    their_tokens = swapped(tokens, count, 1)
    their_lengths = swapped(lengths, count, 1)
    counts = (lengths, their_lengths)

    def attend(turn):
        own, theirs = project(core, *counts, tokens, their_tokens, norm_gains, query_key_value)
        mine = heads(*counts, turn(0, own), theirs)
        turn(1, mine)
        other = swapped(mine, count, 1)
        return join_heads(
            core, *counts, tokens, their_tokens, norm_gains, attention_out, mine, other
        )

    if planes == 2 and inner == 4:

        def hop(value, same, across, crossed):
            pairs = []
            for here in range(planes * count):
                y, place = divmod(here, count)
                z, x, c = place // inner, place % inner // 2, place % 2
                role = 0 if c == y else 1
                link = across if role else same
                if link == "y":
                    y = 1 - y
                elif link == "x":
                    x = 1 - x
                else:
                    z = (z + (1 if link == "up" else OUTER - 1)) % OUTER
                role = 1 - role if crossed else role
                pairs.append((here, y * count + z * inner + x * 2 + (1 - y if role else y)))
            return lax.ppermute(value, ("groups", "dp"), pairs)

        v = [pack_weights(expand_weight, contract_weight)]
        v.append(hop(v[0], "up", "x", False))

        def turn(number, value):
            if number == 0:
                v[1], value = after((v[1], value))
                v.append(hop(v[1], "x", "down", True))
                v.append(hop(v[1], "up", "y", False))
            elif number == 1:
                v[2], v[3], _ = after((v[2], v[3], value))
                v.append(hop(v[2], "x", "y", False))
                v.append(hop(v[3], "y", "down", False))
            elif number == 2:
                v[4], value = after((v[4], value))
                v.append(hop(v[4], "y", "x", False))
            else:
                v[5], value = after((v[5], value))
                v.append(hop(v[5], "x", "down", True))
            return value

        residual, normed, theirs = attend(turn)
        normed = turn(2, normed)
        first = tuple(v[:4])
        own_sum = turn(3, hidden(normed, first, None, jnp.float32))
        second = tuple(v[4:6])
        third = tuple(v[6:8])
    else:
        packed = jnp.concatenate([expand_weight.transpose(0, 2, 1), contract_weight[None]], axis=0)
        same_core = [list(range(first, count, 2)) for first in range(2)]
        gathered = lax.all_gather(
            packed, "dp", axis=1, tiled=True, axis_index_groups=same_core
        )
        residual, normed, theirs = attend(lambda number, value: value)
        units = gathered.shape[1]
        first = (gathered[:, : units // 2],)
        second = (gathered[:, units // 2 : units // 4 * 3],)
        third = (gathered[:, units // 4 * 3 :],)
        own_sum = hidden(normed, first, None, jnp.float32)

    their_sum = hidden(theirs, first, None, jnp.float32)
    own_sum = hidden(normed, second, own_sum, jnp.float32)
    their_sum = hidden(theirs, second, their_sum, jnp.float32)
    their_sum = hidden(theirs, third, their_sum, jnp.bfloat16)
    back = swapped(their_sum, count, 1)
    own_sum = hidden(after(normed, their_sum), third, own_sum, jnp.float32)
    item_vectors, candidates = pool_items(
        count, lengths, norm_gains, residual, pool_weight, (own_sum, back)
    )
    every = lax.all_to_all(candidates, "dp", 0, 0, tiled=True)
    every = every.reshape(count * lengths.shape[0], D)
    return item_vectors, list_loss(queries, list_ids, labels, every)


def solution(mesh):
    return jax.shard_map(
        functools.partial(local, mesh.shape["dp"], mesh.shape["groups"]),
        mesh=mesh,
        in_specs=(
            P(("groups", "dp"), None),
            P(("groups", "dp")),
            P(),
            P(),
            P(),
            P(None, None, "dp"),
            P("dp", None),
            P(),
            P(("groups", "dp"), None),
            P(("groups", "dp")),
            P(("groups", "dp"), None),
        ),
        out_specs=(P(("groups", "dp"), None), P(("groups", "dp"))),
        check_vma=False,
    )
```

```python
import functools

import jax
import jax.numpy as jnp
from jax import lax
from jax.experimental import pallas as pl
from jax.experimental.pallas import tpu as pltpu
from jax.sharding import PartitionSpec as P

D = 768
HEAD = 64
LISTS = 2
OUTER = 4
CHUNK = 256

epsilon = 1e-06
score_scale = 32.0
MIB = 1024 * 1024
SHORT = pl.CostEstimate(flops=1000, bytes_accessed=1000, transcendentals=0)


def inverse_rms(widened):
    return lax.rsqrt(jnp.mean(widened * widened, axis=-1, keepdims=True) + epsilon)


def nt_dot(left, right):
    return lax.dot_general(
        left, right, (((1,), (1,)), ((), ())), preferred_element_type=jnp.float32
    )


def pack_kernel(expand, contract, packed, stage, done):
    grown = pltpu.make_async_copy(expand, stage, done.at[0])
    shrunk = pltpu.make_async_copy(contract, packed.at[2], done.at[1])
    grown.start()
    shrunk.start()
    grown.wait()
    for which in range(2):
        packed[which] = stage[which].T
    shrunk.wait()


def pack_weights(expand_weight, contract_weight):
    in_place = pl.BlockSpec(memory_space=pltpu.HBM)
    return pl.pallas_call(
        pack_kernel,
        out_shape=jax.ShapeDtypeStruct((3,) + contract_weight.shape, jnp.bfloat16),
        in_specs=[in_place, in_place],
        out_specs=pl.BlockSpec(memory_space=pltpu.VMEM),
        scratch_shapes=[
            pltpu.VMEM(expand_weight.shape, jnp.bfloat16),
            pltpu.SemaphoreType.DMA((2,)),
        ],
        compiler_params=pltpu.CompilerParams(vmem_limit_bytes=60 * MIB),
        name="pack_weights",
    )(expand_weight, contract_weight)


def row_tile(rows):
    return 256 if rows % 256 == 0 else rows


def live_tiles(items, lengths, tile):
    total = lengths[0]
    for item in range(1, items):
        total = total + lengths[item]
    return (total + tile - 1) // tile


def tile_rows(index, tile):
    return pl.ds(pl.multiple_of(index * tile, tile), tile)


def project_kernel(items, lengths, their_lengths, tokens, their_tokens, gains, weights, out):
    tile = row_tile(tokens.shape[0])
    wide = weights.shape[1] // 3
    for block, (counts, source) in enumerate(((lengths, tokens), (their_lengths, their_tokens))):

        def body(index, carry):
            here = tile_rows(index, tile)
            widened = source[here, :].astype(jnp.float32)
            x = (widened * inverse_rms(widened) * gains[0:1, :]).astype(jnp.bfloat16)
            part = jnp.dot(x, weights[...], preferred_element_type=jnp.float32)
            part = part.astype(jnp.bfloat16)
            out[block, here, :wide] = part[:, :wide] * jnp.bfloat16(HEAD ** (-0.5))
            out[block, here, wide:] = part[:, wide:]
            return carry

        lax.fori_loop(0, live_tiles(items, counts, tile), body, 0)


def call(kernel, name, scalars, arrays, out_shape, limit=24):
    whole = pl.BlockSpec(memory_space=pltpu.VMEM)
    return pl.pallas_call(
        functools.partial(kernel, scalars[0].shape[0]),
        in_specs=[pl.BlockSpec(memory_space=pltpu.SMEM)] * len(scalars) + [whole] * len(arrays),
        out_specs=jax.tree.map(lambda _: whole, out_shape),
        out_shape=out_shape,
        compiler_params=pltpu.CompilerParams(vmem_limit_bytes=limit * MIB),
        cost_estimate=SHORT,
        name=name,
    )(*scalars, *arrays)


def project(lengths, their_lengths, tokens, their_tokens, norm_gains, weights):
    out = jax.ShapeDtypeStruct((2, tokens.shape[0], weights.shape[1]), jnp.bfloat16)
    arrays = (tokens, their_tokens, norm_gains, weights)
    return call(project_kernel, "project", (lengths, their_lengths), arrays, out)


def heads_kernel(items, lengths, their_lengths, projected, mixed_heads):
    rows = projected.shape[1]
    tile = row_tile(rows)
    group = projected.shape[2] // 3
    wide = 2 * HEAD
    pairs = group // wide
    lane = lax.broadcasted_iota(jnp.int32, (1, wide), 1) // HEAD

    def one_block(block, carry):
        ends = []
        end = 0
        for item in range(items):
            end = end + jnp.where(block == 0, lengths[item], their_lengths[item])
            ends.append(end)
        tiles = (end + tile - 1) // tile

        def segment(position):
            return sum((position >= end).astype(jnp.int32) for end in ends)

        for keys in range(tile, rows + 1, tile):
            across = segment(lax.broadcasted_iota(jnp.int32, (1, keys), 1))

            def body(index, carry):
                row = index // pairs
                begin = pl.multiple_of((index % pairs) * wide, wide)
                here = tile_rows(row, tile)
                down = segment(row * tile + lax.broadcasted_iota(jnp.int32, (tile, 1), 0))
                same = down == across
                q = projected[block, here, pl.ds(begin, wide)]
                k = projected[block, :keys, pl.ds(group + begin, wide)]
                v = projected[block, :keys, pl.ds(2 * group + begin, wide)]
                mixed = jnp.zeros((tile, wide), jnp.float32)
                for head in range(2):
                    mine = lane == head
                    qh = jnp.where(mine, q, jnp.bfloat16(0))
                    vh = jnp.where(mine, v, jnp.bfloat16(1))
                    logits = jnp.where(same, nt_dot(qh, k), -1e30)
                    highest = jnp.max(logits, axis=1, keepdims=True)
                    weights = jnp.exp(logits - highest).astype(jnp.bfloat16)
                    out = jnp.dot(weights, vh, preferred_element_type=jnp.float32)
                    other = (1 - head) * HEAD
                    inverse = 1.0 / out[:, other : other + 1]
                    mixed = jnp.where(mine, out * inverse, mixed)
                mixed_heads[block, here, pl.ds(begin, wide)] = mixed.astype(jnp.bfloat16)
                return carry

            count = keys // tile
            lax.fori_loop(0, jnp.where(tiles == count, count * pairs, 0), body, 0)
        return carry

    lax.fori_loop(0, 2, one_block, 0)


def heads(lengths, their_lengths, projected):
    out = jax.ShapeDtypeStruct(projected.shape[:2] + (projected.shape[2] // 3,), jnp.bfloat16)
    return call(heads_kernel, "heads", (lengths, their_lengths), (projected,), out)


def join_kernel(
    items,
    lengths,
    their_lengths,
    core,
    tokens,
    their_tokens,
    gains,
    wo,
    here_heads,
    there_heads,
    residual,
    normed,
    their_normed,
):
    tile = row_tile(tokens.shape[0])
    low = core[0] == 0
    blocks = (
        (lengths, tokens, residual, normed),
        (their_lengths, their_tokens, None, their_normed),
    )
    for block, (counts, source, kept, target) in enumerate(blocks):

        def body(index, carry):
            here = tile_rows(index, tile)
            mine, other = here_heads[block, here, :], there_heads[1 - block, here, :]
            mixed = jnp.concatenate(
                [jnp.where(low, mine, other), jnp.where(low, other, mine)], axis=1
            )
            total = source[here, :].astype(jnp.float32)
            total += jnp.dot(mixed, wo[...], preferred_element_type=jnp.float32)
            rounded = total.astype(jnp.bfloat16)
            if kept is not None:
                kept[here, :] = rounded
            widened = rounded.astype(jnp.float32)
            target[here, :] = (widened * inverse_rms(widened) * gains[1:2, :]).astype(jnp.bfloat16)
            return carry

        lax.fori_loop(0, live_tiles(items, counts, tile), body, 0)


def join_heads(core, lengths, their_lengths, *arrays):
    rows = jax.ShapeDtypeStruct(arrays[0].shape, jnp.bfloat16)
    scalars = (lengths, their_lengths, core)
    return call(join_kernel, "join_heads", scalars, arrays, (rows, rows, rows))


def hidden_kernel(resumed, items, lengths, x, *refs):
    blocks = refs[: len(refs) - 1 - resumed]
    before = refs[-2] if resumed else None
    total = refs[-1]
    tile = row_tile(x.shape[0])
    each = max(1, CHUNK // blocks[0].shape[1])
    groups = [blocks[i : i + each] for i in range(0, len(blocks), each)]

    def weight(which, part):
        return jnp.concatenate([block[which] for block in part], axis=0)

    def body(index, carry):
        span = tile_rows(index, tile)
        here = x[span, :]
        grown = None if before is None else before[span, :]
        for part in groups:
            gate = nt_dot(here, weight(0, part))
            up = nt_dot(here, weight(1, part))
            active = (jax.nn.gelu(gate, approximate=True) * up).astype(jnp.bfloat16)
            term = jnp.dot(active, weight(2, part), preferred_element_type=jnp.float32)
            grown = term if grown is None else grown + term
        total[span, :] = grown.astype(total.dtype)
        return carry

    lax.fori_loop(0, live_tiles(items, lengths, tile), body, 0)


def hidden(lengths, normed, blocks, before, kind):
    resumed = before is not None
    arrays = (normed, *blocks) + ((before,) if resumed else ())
    out = jax.ShapeDtypeStruct(normed.shape, kind)
    kernel = functools.partial(hidden_kernel, resumed)
    return call(kernel, "hidden", (lengths,), arrays, out)


def pool_kernel(items, lengths, gains, residual, pool, *refs):
    sums, (vectors, candidates) = refs[:-2], refs[-2:]
    tile = row_tile(residual.shape[0])
    slots = 16
    slot = lax.broadcasted_iota(jnp.int32, (slots, 1), 0)
    first = jnp.zeros((slots, 1), jnp.int32)
    last = jnp.zeros((slots, 1), jnp.int32)
    begin = 0
    for item in range(items):
        end = begin + lengths[item]
        first = jnp.where(slot == item, begin, first)
        last = jnp.where(slot == item, end, last)
        begin = end

    def body(index, summed):
        here = tile_rows(index, tile)
        total = residual[here, :].astype(jnp.float32)
        for part in sums:
            total += part[here, :].astype(jnp.float32)
        finished = total.astype(jnp.bfloat16).astype(jnp.float32)
        final_rows = (finished * inverse_rms(finished) * gains[2:3, :]).astype(jnp.bfloat16)
        across = index * tile + lax.broadcasted_iota(jnp.int32, (slots, tile), 1)
        member = jnp.where((across >= first) & (across < last), 1.0, 0.0)
        return summed + jnp.dot(
            member.astype(jnp.bfloat16), final_rows, preferred_element_type=jnp.float32
        )

    summed = lax.fori_loop(
        0, live_tiles(items, lengths, tile), body, jnp.zeros((slots, D), jnp.float32)
    )
    counts = jnp.maximum(last - first, 1).astype(jnp.float32)
    pooled = (summed / counts).astype(jnp.bfloat16)
    e = jnp.dot(pooled, pool[...], preferred_element_type=jnp.float32)
    e = e * inverse_rms(e)
    vectors[...] = e[:items, :]
    mine = e[:items, :].astype(jnp.bfloat16)
    for device in range(candidates.shape[0]):
        candidates[device] = mine


def pool_items(devices, lengths, norm_gains, residual, pool_weight, sums):
    items = lengths.shape[0]
    out = (
        jax.ShapeDtypeStruct((items, D), jnp.float32),
        jax.ShapeDtypeStruct((devices, items, D), jnp.bfloat16),
    )
    arrays = (norm_gains, residual, pool_weight, *sums)
    return call(pool_kernel, "pool_items", (lengths,), arrays, out)


def loss_kernel(queries, list_ids, labels, candidates, loss):
    widened = queries[...].astype(jnp.float32)
    query_unit = (widened * inverse_rms(widened)).astype(jnp.bfloat16)
    each = labels.shape[0]
    chosen = None
    for which in range(LISTS):
        scores = nt_dot(candidates[which * each : (which + 1) * each, :], query_unit)
        if chosen is None:
            chosen = scores
        else:
            chosen = jnp.where(list_ids[...] == which, scores, chosen)
    chosen = chosen * (score_scale / D)
    target = jnp.exp(labels[...].astype(jnp.float32))
    target = target / jnp.sum(target, axis=0, keepdims=True)
    log_total = jnp.log(jnp.sum(jnp.exp(chosen), axis=0, keepdims=True))
    loss[...] = log_total - jnp.sum(target * chosen, axis=0, keepdims=True)


def list_loss(queries, list_ids, labels, candidates):
    count = queries.shape[0]
    return pl.pallas_call(
        loss_kernel,
        out_shape=jax.ShapeDtypeStruct((1, count), jnp.float32),
        compiler_params=pltpu.CompilerParams(vmem_limit_bytes=16 * MIB),
        name="list_loss",
    )(queries, list_ids.reshape(1, count), labels.T, candidates).reshape(count)


def swapped(value, count, bit):
    return lax.ppermute(value, "dp", [(i, i ^ bit) for i in range(count)])


def after(value, *earlier):
    return lax.optimization_barrier((value, earlier))[0]


def local(
    count,
    planes,
    tokens,
    lengths,
    norm_gains,
    query_key_value,
    attention_out,
    expand_weight,
    contract_weight,
    pool_weight,
    queries,
    list_ids,
    labels,
):
    inner = count // OUTER
    core = (lax.axis_index("dp") % 2).astype(jnp.int32).reshape(1)
    their_tokens = swapped(tokens, count, 1)
    their_lengths = swapped(lengths, count, 1)
    counts = (lengths, their_lengths)

    wide = D // 2
    weights = jnp.concatenate(
        [
            lax.dynamic_slice_in_dim(query_key_value, (2 * which + core[0]) * wide, wide, axis=1)
            for which in range(3)
        ],
        axis=1,
    )

    def attend(turn):
        projected = project(*counts, tokens, their_tokens, norm_gains, weights)
        mine = turn(1, heads(*counts, turn(0, projected)))
        other = swapped(mine, count, 1)
        return join_heads(
            core, *counts, tokens, their_tokens, norm_gains, attention_out, mine, other
        )

    if planes == 2 and inner == 4:

        def hop(value, same, across, crossed):
            pairs = []
            for here in range(planes * count):
                y, place = divmod(here, count)
                z, x, c = place // inner, place % inner // 2, place % 2
                role = 0 if c == y else 1
                link = across if role else same
                if link == "y":
                    y = 1 - y
                elif link == "x":
                    x = 1 - x
                else:
                    z = (z + (1 if link == "up" else OUTER - 1)) % OUTER
                role = 1 - role if crossed else role
                pairs.append((here, y * count + z * inner + x * 2 + (1 - y if role else y)))
            return lax.ppermute(value, ("groups", "dp"), pairs)

        v = [pack_weights(expand_weight, contract_weight)]
        v.append(hop(v[0], "up", "x", False))

        def turn(number, value):
            if number == 0:
                v[1], value = after((v[1], value))
                v.append(hop(v[1], "x", "down", True))
                v.append(hop(v[1], "up", "y", False))
            else:
                v[2], v[3], value = after((v[2], v[3], value))
                v.append(hop(v[2], "x", "y", False))
                v.append(hop(v[3], "y", "down", False))
            return value

        residual, normed, theirs = attend(turn)
        first = tuple(v[:4])
        own_sum = hidden(lengths, normed, first, None, jnp.float32)
        v[4], v[5], theirs = after((v[4], v[5], theirs), own_sum)
        v.append(hop(v[4], "y", "x", False))
        v.append(hop(v[5], "x", "down", True))
        second = tuple(v[4:6])
        third = tuple(v[6:8])
    else:
        packed = jnp.concatenate([expand_weight.transpose(0, 2, 1), contract_weight[None]], axis=0)
        same_core = [list(range(first, count, 2)) for first in range(2)]
        gathered = lax.all_gather(
            packed, "dp", axis=1, tiled=True, axis_index_groups=same_core
        )
        residual, normed, theirs = attend(lambda number, value: value)
        units = gathered.shape[1]
        first = (gathered[:, : units // 2],)
        second = (gathered[:, units // 2 : units // 4 * 3],)
        third = (gathered[:, units // 4 * 3 :],)
        own_sum = hidden(lengths, normed, first, None, jnp.float32)

    their_sum = hidden(their_lengths, theirs, first, None, jnp.float32)
    own_sum = hidden(lengths, normed, second, own_sum, jnp.float32)
    their_sum = hidden(their_lengths, theirs, second, their_sum, jnp.float32)
    their_sum = hidden(their_lengths, theirs, third, their_sum, jnp.bfloat16)
    back = swapped(their_sum, count, 1)
    own_sum = hidden(lengths, after(normed, their_sum), third, own_sum, jnp.float32)
    item_vectors, candidates = pool_items(
        count, lengths, norm_gains, residual, pool_weight, (own_sum, back)
    )
    every = lax.all_to_all(candidates, "dp", 0, 0, tiled=True)
    every = every.reshape(count * lengths.shape[0], D)
    return item_vectors, list_loss(queries, list_ids, labels, every)


def solution(mesh):
    return jax.shard_map(
        functools.partial(local, mesh.shape["dp"], mesh.shape["groups"]),
        mesh=mesh,
        in_specs=(
            P(("groups", "dp"), None),
            P(("groups", "dp")),
            P(),
            P(),
            P(),
            P(None, None, "dp"),
            P("dp", None),
            P(),
            P(("groups", "dp"), None),
            P(("groups", "dp")),
            P(("groups", "dp"), None),
        ),
        out_specs=(P(("groups", "dp"), None), P(("groups", "dp"))),
        check_vma=False,
    )
```

```python
import functools

import jax
import jax.numpy as jnp
from jax import lax
from jax.experimental import pallas as pl
from jax.experimental.pallas import tpu as pltpu
from jax.sharding import PartitionSpec as P

D = 768
HEAD = 64
LISTS = 2
OUTER = 4
CHUNK = 256

epsilon = 1e-06
score_scale = 32.0
MIB = 1024 * 1024
SHORT = pl.CostEstimate(flops=1000, bytes_accessed=1000, transcendentals=0)


def inverse_rms(widened):
    return lax.rsqrt(jnp.mean(widened * widened, axis=-1, keepdims=True) + epsilon)


def nt_dot(left, right):
    return lax.dot_general(
        left, right, (((1,), (1,)), ((), ())), preferred_element_type=jnp.float32
    )


def pack_kernel(expand, contract, here, there, stage, done):
    half = here.shape[1]
    copies = [pltpu.make_async_copy(expand, stage, done.at[0])]
    for index, target in enumerate((here, there)):
        source = contract.at[index * half : (index + 1) * half, :]
        copies.append(pltpu.make_async_copy(source, target.at[2], done.at[1 + index]))
    for copy in copies:
        copy.start()
    copies[0].wait()
    for which in range(2):
        turned = stage[which].T
        here[which] = turned[:half, :]
        there[which] = turned[half:, :]
    copies[1].wait()
    copies[2].wait()


def pack_weights(expand_weight, contract_weight):
    in_place = pl.BlockSpec(memory_space=pltpu.HBM)
    whole = pl.BlockSpec(memory_space=pltpu.VMEM)
    half = jax.ShapeDtypeStruct((3, contract_weight.shape[0] // 2, D), jnp.bfloat16)
    return pl.pallas_call(
        pack_kernel,
        out_shape=(half, half),
        in_specs=[in_place, in_place],
        out_specs=(whole, whole),
        scratch_shapes=[
            pltpu.VMEM(expand_weight.shape, jnp.bfloat16),
            pltpu.SemaphoreType.DMA((3,)),
        ],
        compiler_params=pltpu.CompilerParams(vmem_limit_bytes=60 * MIB),
        name="pack_weights",
    )(expand_weight, contract_weight)


def row_tile(rows):
    return 256 if rows % 256 == 0 else rows


def live_tiles(items, lengths, tile):
    total = lengths[0]
    for item in range(1, items):
        total = total + lengths[item]
    return (total + tile - 1) // tile


def tile_rows(index, tile):
    return pl.ds(pl.multiple_of(index * tile, tile), tile)


def project_kernel(items, lengths, their_lengths, tokens, their_tokens, gains, weights, out):
    tile = row_tile(tokens.shape[0])
    wide = weights.shape[1] // 3
    for block, (counts, source) in enumerate(((lengths, tokens), (their_lengths, their_tokens))):

        def body(index, carry):
            here = tile_rows(index, tile)
            widened = source[here, :].astype(jnp.float32)
            x = (widened * inverse_rms(widened) * gains[0:1, :]).astype(jnp.bfloat16)
            part = jnp.dot(x, weights[...], preferred_element_type=jnp.float32)
            part = part.astype(jnp.bfloat16)
            out[block, here, :wide] = part[:, :wide] * jnp.bfloat16(HEAD ** (-0.5))
            out[block, here, wide:] = part[:, wide:]
            return carry

        lax.fori_loop(0, live_tiles(items, counts, tile), body, 0)


def call(kernel, name, scalars, arrays, out_shape, limit=24):
    whole = pl.BlockSpec(memory_space=pltpu.VMEM)
    return pl.pallas_call(
        functools.partial(kernel, scalars[0].shape[0]),
        in_specs=[pl.BlockSpec(memory_space=pltpu.SMEM)] * len(scalars) + [whole] * len(arrays),
        out_specs=jax.tree.map(lambda _: whole, out_shape),
        out_shape=out_shape,
        compiler_params=pltpu.CompilerParams(vmem_limit_bytes=limit * MIB),
        cost_estimate=SHORT,
        name=name,
    )(*scalars, *arrays)


def project(lengths, their_lengths, tokens, their_tokens, norm_gains, weights):
    out = jax.ShapeDtypeStruct((2, tokens.shape[0], weights.shape[1]), jnp.bfloat16)
    arrays = (tokens, their_tokens, norm_gains, weights)
    return call(project_kernel, "project", (lengths, their_lengths), arrays, out)


def heads_kernel(items, lengths, their_lengths, projected, mixed_heads):
    rows = projected.shape[1]
    tile = row_tile(rows)
    group = projected.shape[2] // 3
    wide = 2 * HEAD
    lane = lax.broadcasted_iota(jnp.int32, (1, wide), 1) // HEAD

    def one_block(block, carry):
        ends = []
        end = 0
        for item in range(items):
            end = end + jnp.where(block == 0, lengths[item], their_lengths[item])
            ends.append(end)
        tiles = (end + tile - 1) // tile

        def segment(position):
            return sum((position >= end).astype(jnp.int32) for end in ends)

        for keys in range(tile, rows + 1, tile):
            across = segment(lax.broadcasted_iota(jnp.int32, (1, keys), 1))

            def body(row, carry):
                here = tile_rows(row, tile)
                down = segment(row * tile + lax.broadcasted_iota(jnp.int32, (tile, 1), 0))
                same = down == across
                for begin in range(0, group, wide):
                    q = projected[block, here, begin : begin + wide]
                    k = projected[block, :keys, group + begin : group + begin + wide]
                    v = projected[block, :keys, 2 * group + begin : 2 * group + begin + wide]
                    mixed = jnp.zeros((tile, wide), jnp.float32)
                    for head in range(2):
                        mine = lane == head
                        qh = jnp.where(mine, q, jnp.bfloat16(0))
                        vh = jnp.where(mine, v, jnp.bfloat16(1))
                        logits = jnp.where(same, nt_dot(qh, k), -1e30)
                        highest = jnp.max(logits, axis=1, keepdims=True)
                        weights = jnp.exp(logits - highest).astype(jnp.bfloat16)
                        out = jnp.dot(weights, vh, preferred_element_type=jnp.float32)
                        other = (1 - head) * HEAD
                        inverse = 1.0 / out[:, other : other + 1]
                        mixed = jnp.where(mine, out * inverse, mixed)
                    mixed_heads[block, here, begin : begin + wide] = mixed.astype(jnp.bfloat16)
                return carry

            count = keys // tile
            lax.fori_loop(0, jnp.where(tiles == count, count, 0), body, 0)
        return carry

    lax.fori_loop(0, 2, one_block, 0)


def heads(lengths, their_lengths, projected):
    out = jax.ShapeDtypeStruct(projected.shape[:2] + (projected.shape[2] // 3,), jnp.bfloat16)
    return call(heads_kernel, "heads", (lengths, their_lengths), (projected,), out)


def join_kernel(
    items,
    lengths,
    their_lengths,
    core,
    tokens,
    their_tokens,
    gains,
    wo,
    here_heads,
    there_heads,
    residual,
    normed,
    their_normed,
):
    tile = row_tile(tokens.shape[0])
    low = core[0] == 0
    blocks = (
        (lengths, tokens, residual, normed),
        (their_lengths, their_tokens, None, their_normed),
    )
    for block, (counts, source, kept, target) in enumerate(blocks):

        def body(index, carry):
            here = tile_rows(index, tile)
            mine, other = here_heads[block, here, :], there_heads[1 - block, here, :]
            mixed = jnp.concatenate(
                [jnp.where(low, mine, other), jnp.where(low, other, mine)], axis=1
            )
            total = source[here, :].astype(jnp.float32)
            total += jnp.dot(mixed, wo[...], preferred_element_type=jnp.float32)
            rounded = total.astype(jnp.bfloat16)
            if kept is not None:
                kept[here, :] = rounded
            widened = rounded.astype(jnp.float32)
            target[here, :] = (widened * inverse_rms(widened) * gains[1:2, :]).astype(jnp.bfloat16)
            return carry

        lax.fori_loop(0, live_tiles(items, counts, tile), body, 0)


def join_heads(core, lengths, their_lengths, *arrays):
    rows = jax.ShapeDtypeStruct(arrays[0].shape, jnp.bfloat16)
    scalars = (lengths, their_lengths, core)
    return call(join_kernel, "join_heads", scalars, arrays, (rows, rows, rows))


def hidden_kernel(resumed, items, lengths, x, *refs):
    blocks = refs[: len(refs) - 1 - resumed]
    before = refs[-2] if resumed else None
    total = refs[-1]
    tile = row_tile(x.shape[0])
    pieces = []
    for block in blocks:
        pieces += [block] if len(block.shape) == 3 else [block.at[i] for i in range(block.shape[0])]
    each = max(1, CHUNK // pieces[0].shape[1])
    groups = [pieces[i : i + each] for i in range(0, len(pieces), each)]

    def weight(which, part):
        return jnp.concatenate([piece[which] for piece in part], axis=0)

    def body(index, carry):
        span = tile_rows(index, tile)
        here = x[span, :]
        grown = None if before is None else before[span, :]
        for part in groups:
            gate = nt_dot(here, weight(0, part))
            up = nt_dot(here, weight(1, part))
            active = (jax.nn.gelu(gate, approximate=True) * up).astype(jnp.bfloat16)
            term = jnp.dot(active, weight(2, part), preferred_element_type=jnp.float32)
            grown = term if grown is None else grown + term
        total[span, :] = grown.astype(total.dtype)
        return carry

    lax.fori_loop(0, live_tiles(items, lengths, tile), body, 0)


def hidden(lengths, normed, blocks, before, kind):
    resumed = before is not None
    arrays = (normed, *blocks) + ((before,) if resumed else ())
    out = jax.ShapeDtypeStruct(normed.shape, kind)
    kernel = functools.partial(hidden_kernel, resumed)
    return call(kernel, "hidden", (lengths,), arrays, out)


def pool_kernel(items, lengths, gains, residual, pool, *refs):
    sums, (vectors, candidates) = refs[:-2], refs[-2:]
    tile = row_tile(residual.shape[0])
    slots = 16
    slot = lax.broadcasted_iota(jnp.int32, (slots, 1), 0)
    first = jnp.zeros((slots, 1), jnp.int32)
    last = jnp.zeros((slots, 1), jnp.int32)
    begin = 0
    for item in range(items):
        end = begin + lengths[item]
        first = jnp.where(slot == item, begin, first)
        last = jnp.where(slot == item, end, last)
        begin = end

    def body(index, summed):
        here = tile_rows(index, tile)
        total = residual[here, :].astype(jnp.float32)
        for part in sums:
            total += part[here, :].astype(jnp.float32)
        finished = total.astype(jnp.bfloat16).astype(jnp.float32)
        final_rows = (finished * inverse_rms(finished) * gains[2:3, :]).astype(jnp.bfloat16)
        across = index * tile + lax.broadcasted_iota(jnp.int32, (slots, tile), 1)
        member = jnp.where((across >= first) & (across < last), 1.0, 0.0)
        return summed + jnp.dot(
            member.astype(jnp.bfloat16), final_rows, preferred_element_type=jnp.float32
        )

    summed = lax.fori_loop(
        0, live_tiles(items, lengths, tile), body, jnp.zeros((slots, D), jnp.float32)
    )
    counts = jnp.maximum(last - first, 1).astype(jnp.float32)
    pooled = (summed / counts).astype(jnp.bfloat16)
    e = jnp.dot(pooled, pool[...], preferred_element_type=jnp.float32)
    e = e * inverse_rms(e)
    vectors[...] = e[:items, :]
    mine = e[:items, :].astype(jnp.bfloat16)
    for device in range(candidates.shape[0]):
        candidates[device] = mine


def pool_items(devices, lengths, norm_gains, residual, pool_weight, sums):
    items = lengths.shape[0]
    out = (
        jax.ShapeDtypeStruct((items, D), jnp.float32),
        jax.ShapeDtypeStruct((devices, items, D), jnp.bfloat16),
    )
    arrays = (norm_gains, residual, pool_weight, *sums)
    return call(pool_kernel, "pool_items", (lengths,), arrays, out)


def loss_kernel(queries, list_ids, labels, candidates, loss):
    widened = queries[...].astype(jnp.float32)
    query_unit = (widened * inverse_rms(widened)).astype(jnp.bfloat16)
    each = labels.shape[0]
    chosen = None
    for which in range(LISTS):
        scores = nt_dot(candidates[which * each : (which + 1) * each, :], query_unit)
        if chosen is None:
            chosen = scores
        else:
            chosen = jnp.where(list_ids[...] == which, scores, chosen)
    chosen = chosen * (score_scale / D)
    target = jnp.exp(labels[...].astype(jnp.float32))
    target = target / jnp.sum(target, axis=0, keepdims=True)
    log_total = jnp.log(jnp.sum(jnp.exp(chosen), axis=0, keepdims=True))
    loss[...] = log_total - jnp.sum(target * chosen, axis=0, keepdims=True)


def list_loss(queries, list_ids, labels, candidates):
    count = queries.shape[0]
    return pl.pallas_call(
        loss_kernel,
        out_shape=jax.ShapeDtypeStruct((1, count), jnp.float32),
        compiler_params=pltpu.CompilerParams(vmem_limit_bytes=16 * MIB),
        name="list_loss",
    )(queries, list_ids.reshape(1, count), labels.T, candidates).reshape(count)


def swapped(value, count, bit):
    return lax.ppermute(value, "dp", [(i, i ^ bit) for i in range(count)])


def after(value, *earlier):
    return lax.optimization_barrier((value, earlier))[0]


def local(
    count,
    planes,
    tokens,
    lengths,
    norm_gains,
    query_key_value,
    attention_out,
    expand_weight,
    contract_weight,
    pool_weight,
    queries,
    list_ids,
    labels,
):
    inner = count // OUTER
    core = (lax.axis_index("dp") % 2).astype(jnp.int32).reshape(1)
    their_tokens = swapped(tokens, count, 1)
    their_lengths = swapped(lengths, count, 1)
    counts = (lengths, their_lengths)

    wide = D // 2
    weights = jnp.concatenate(
        [
            lax.dynamic_slice_in_dim(query_key_value, (2 * which + core[0]) * wide, wide, axis=1)
            for which in range(3)
        ],
        axis=1,
    )

    def attend(turn):
        projected = project(*counts, tokens, their_tokens, norm_gains, weights)
        mine = turn(1, heads(*counts, turn(0, projected)))
        other = swapped(mine, count, 1)
        return join_heads(
            core, *counts, tokens, their_tokens, norm_gains, attention_out, mine, other
        )

    same_core = [list(range(first, count, 2)) for first in range(2)]
    if planes == 2 and inner == 4:

        def hop(value, same, across, crossed):
            pairs = []
            for here in range(planes * count):
                y, place = divmod(here, count)
                z, x, c = place // inner, place % inner // 2, place % 2
                role = 0 if c == y else 1
                link = across if role else same
                if link == "y":
                    y = 1 - y
                elif link == "x":
                    x = 1 - x
                else:
                    z = (z + (1 if link == "up" else OUTER - 1)) % OUTER
                role = 1 - role if crossed else role
                pairs.append((here, y * count + z * inner + x * 2 + (1 - y if role else y)))
            return lax.ppermute(value, ("groups", "dp"), pairs)

        mine, rest = pack_weights(expand_weight, contract_weight)
        gathered = lax.all_gather(
            rest, "dp", axis=0, tiled=False, axis_index_groups=same_core
        )
        v = [mine]
        v.append(hop(v[0], "up", "x", False))

        def turn(number, value):
            if number == 0:
                v[1], value = after((v[1], value))
                v.append(hop(v[1], "x", "down", True))
                v.append(hop(v[1], "up", "y", False))
            else:
                v[2], v[3], value = after((v[2], v[3], value))
                v.append(hop(v[2], "x", "y", False))
                v.append(hop(v[3], "y", "down", False))
            return value

        residual, normed, theirs = attend(turn)
        first = tuple(v[:4])
        own_sum = hidden(lengths, normed, first, None, jnp.float32)
        v[4], v[5], theirs = after((v[4], v[5], theirs), own_sum)
        v.append(hop(v[4], "y", "x", False))
        v.append(hop(v[5], "x", "down", True))
        second = (gathered,)
        third = tuple(v[4:8])
    else:
        packed = jnp.concatenate([expand_weight.transpose(0, 2, 1), contract_weight[None]], axis=0)
        gathered = lax.all_gather(
            packed, "dp", axis=1, tiled=True, axis_index_groups=same_core
        )
        residual, normed, theirs = attend(lambda number, value: value)
        units = gathered.shape[1]
        first = (gathered[:, : units // 2],)
        second = (gathered[:, units // 2 : units // 4 * 3],)
        third = (gathered[:, units // 4 * 3 :],)
        own_sum = hidden(lengths, normed, first, None, jnp.float32)

    their_sum = hidden(their_lengths, theirs, first, None, jnp.float32)
    own_sum = hidden(lengths, normed, second, own_sum, jnp.float32)
    their_sum = hidden(their_lengths, theirs, second, their_sum, jnp.float32)
    their_sum = hidden(their_lengths, theirs, third, their_sum, jnp.bfloat16)
    back = swapped(their_sum, count, 1)
    own_sum = hidden(lengths, after(normed, their_sum), third, own_sum, jnp.float32)
    item_vectors, candidates = pool_items(
        count, lengths, norm_gains, residual, pool_weight, (own_sum, back)
    )
    every = lax.all_to_all(candidates, "dp", 0, 0, tiled=True)
    every = every.reshape(count * lengths.shape[0], D)
    return item_vectors, list_loss(queries, list_ids, labels, every)


def solution(mesh):
    return jax.shard_map(
        functools.partial(local, mesh.shape["dp"], mesh.shape["groups"]),
        mesh=mesh,
        in_specs=(
            P(("groups", "dp"), None),
            P(("groups", "dp")),
            P(),
            P(),
            P(),
            P(None, None, "dp"),
            P("dp", None),
            P(),
            P(("groups", "dp"), None),
            P(("groups", "dp")),
            P(("groups", "dp"), None),
        ),
        out_specs=(P(("groups", "dp"), None), P(("groups", "dp"))),
        check_vma=False,
    )
```

```python
import functools

import jax
import jax.numpy as jnp
from jax import lax
from jax.experimental import pallas as pl
from jax.experimental.pallas import tpu as pltpu
from jax.sharding import PartitionSpec as P

D = 768
HEAD = 64
LISTS = 2
OUTER = 4
CHUNK = 256

epsilon = 1e-06
score_scale = 32.0
MIB = 1024 * 1024
SHORT = pl.CostEstimate(flops=1000, bytes_accessed=1000, transcendentals=0)


def inverse_rms(widened):
    return lax.rsqrt(jnp.mean(widened * widened, axis=-1, keepdims=True) + epsilon)


def nt_dot(left, right):
    return lax.dot_general(
        left, right, (((1,), (1,)), ((), ())), preferred_element_type=jnp.float32
    )


def pack_kernel(expand, contract, packed, stage, done):
    grown = pltpu.make_async_copy(expand, stage, done.at[0])
    shrunk = pltpu.make_async_copy(contract, packed.at[2], done.at[1])
    grown.start()
    shrunk.start()
    grown.wait()
    for which in range(2):
        packed[which] = stage[which].T
    shrunk.wait()


def pack_weights(expand_weight, contract_weight):
    in_place = pl.BlockSpec(memory_space=pltpu.HBM)
    return pl.pallas_call(
        pack_kernel,
        out_shape=jax.ShapeDtypeStruct((3,) + contract_weight.shape, jnp.bfloat16),
        in_specs=[in_place, in_place],
        out_specs=pl.BlockSpec(memory_space=pltpu.VMEM),
        scratch_shapes=[
            pltpu.VMEM(expand_weight.shape, jnp.bfloat16),
            pltpu.SemaphoreType.DMA((2,)),
        ],
        compiler_params=pltpu.CompilerParams(vmem_limit_bytes=60 * MIB),
        name="pack_weights",
    )(expand_weight, contract_weight)


def row_tile(rows):
    return 256 if rows % 256 == 0 else rows


def live_tiles(items, lengths, tile):
    total = lengths[0]
    for item in range(1, items):
        total = total + lengths[item]
    return (total + tile - 1) // tile


def tile_rows(index, tile):
    return pl.ds(pl.multiple_of(index * tile, tile), tile)


def project_kernel(items, lengths, their_lengths, tokens, their_tokens, gains, weights, out):
    tile = row_tile(tokens.shape[0])
    wide = weights.shape[1] // 3
    for block, (counts, source) in enumerate(((lengths, tokens), (their_lengths, their_tokens))):

        def body(index, carry):
            here = tile_rows(index, tile)
            widened = source[here, :].astype(jnp.float32)
            x = (widened * inverse_rms(widened) * gains[0:1, :]).astype(jnp.bfloat16)
            part = jnp.dot(x, weights[...], preferred_element_type=jnp.float32)
            part = part.astype(jnp.bfloat16)
            out[block, here, :wide] = part[:, :wide] * jnp.bfloat16(HEAD ** (-0.5))
            out[block, here, wide:] = part[:, wide:]
            return carry

        lax.fori_loop(0, live_tiles(items, counts, tile), body, 0)


def call(kernel, name, scalars, arrays, out_shape, limit=24):
    whole = pl.BlockSpec(memory_space=pltpu.VMEM)
    return pl.pallas_call(
        functools.partial(kernel, scalars[0].shape[0]),
        in_specs=[pl.BlockSpec(memory_space=pltpu.SMEM)] * len(scalars) + [whole] * len(arrays),
        out_specs=jax.tree.map(lambda _: whole, out_shape),
        out_shape=out_shape,
        compiler_params=pltpu.CompilerParams(vmem_limit_bytes=limit * MIB),
        cost_estimate=SHORT,
        name=name,
    )(*scalars, *arrays)


def project(lengths, their_lengths, tokens, their_tokens, norm_gains, weights):
    out = jax.ShapeDtypeStruct((2, tokens.shape[0], weights.shape[1]), jnp.bfloat16)
    arrays = (tokens, their_tokens, norm_gains, weights)
    return call(project_kernel, "project", (lengths, their_lengths), arrays, out)


def heads_kernel(first, last, items, lengths, their_lengths, projected, *refs):
    mixed_heads = refs[-1]
    rows = projected.shape[1]
    tile = row_tile(rows)
    group = projected.shape[2] // 3
    wide = 2 * HEAD
    lane = lax.broadcasted_iota(jnp.int32, (1, wide), 1) // HEAD

    def one_block(block, carry):
        ends = []
        end = 0
        for item in range(items):
            end = end + jnp.where(block == 0, lengths[item], their_lengths[item])
            ends.append(end)
        tiles = (end + tile - 1) // tile

        def segment(position):
            return sum((position >= end).astype(jnp.int32) for end in ends)

        for keys in range(tile, rows + 1, tile):
            across = segment(lax.broadcasted_iota(jnp.int32, (1, keys), 1))

            def body(row, carry):
                here = tile_rows(row, tile)
                down = segment(row * tile + lax.broadcasted_iota(jnp.int32, (tile, 1), 0))
                same = down == across
                for begin in range(first * HEAD, last * HEAD, wide):
                    q = projected[block, here, begin : begin + wide]
                    k = projected[block, :keys, group + begin : group + begin + wide]
                    v = projected[block, :keys, 2 * group + begin : 2 * group + begin + wide]
                    mixed = jnp.zeros((tile, wide), jnp.float32)
                    for head in range(2):
                        mine = lane == head
                        qh = jnp.where(mine, q, jnp.bfloat16(0))
                        vh = jnp.where(mine, v, jnp.bfloat16(1))
                        logits = jnp.where(same, nt_dot(qh, k), -1e30)
                        highest = jnp.max(logits, axis=1, keepdims=True)
                        weights = jnp.exp(logits - highest).astype(jnp.bfloat16)
                        out = jnp.dot(weights, vh, preferred_element_type=jnp.float32)
                        other = (1 - head) * HEAD
                        inverse = 1.0 / out[:, other : other + 1]
                        mixed = jnp.where(mine, out * inverse, mixed)
                    mixed_heads[block, here, begin : begin + wide] = mixed.astype(jnp.bfloat16)
                if len(refs) > 1:
                    mixed_heads[block, here, : first * HEAD] = refs[0][block, here, :]
                return carry

            count = keys // tile
            lax.fori_loop(0, jnp.where(tiles == count, count, 0), body, 0)
        return carry

    lax.fori_loop(0, 2, one_block, 0)


def heads(first, last, lengths, their_lengths, projected, *earlier):
    out = jax.ShapeDtypeStruct(projected.shape[:2] + (last * HEAD,), jnp.bfloat16)
    kernel = functools.partial(heads_kernel, first, last)
    return call(kernel, "heads", (lengths, their_lengths), (projected, *earlier), out)


def join_kernel(
    items,
    lengths,
    their_lengths,
    core,
    tokens,
    their_tokens,
    gains,
    wo,
    here_heads,
    there_heads,
    residual,
    normed,
    their_normed,
):
    tile = row_tile(tokens.shape[0])
    low = core[0] == 0
    blocks = (
        (lengths, tokens, residual, normed),
        (their_lengths, their_tokens, None, their_normed),
    )
    for block, (counts, source, kept, target) in enumerate(blocks):

        def body(index, carry):
            here = tile_rows(index, tile)
            mine, other = here_heads[block, here, :], there_heads[1 - block, here, :]
            mixed = jnp.concatenate(
                [jnp.where(low, mine, other), jnp.where(low, other, mine)], axis=1
            )
            total = source[here, :].astype(jnp.float32)
            total += jnp.dot(mixed, wo[...], preferred_element_type=jnp.float32)
            rounded = total.astype(jnp.bfloat16)
            if kept is not None:
                kept[here, :] = rounded
            widened = rounded.astype(jnp.float32)
            target[here, :] = (widened * inverse_rms(widened) * gains[1:2, :]).astype(jnp.bfloat16)
            return carry

        lax.fori_loop(0, live_tiles(items, counts, tile), body, 0)


def join_heads(core, lengths, their_lengths, *arrays):
    rows = jax.ShapeDtypeStruct(arrays[0].shape, jnp.bfloat16)
    scalars = (lengths, their_lengths, core)
    return call(join_kernel, "join_heads", scalars, arrays, (rows, rows, rows))


def hidden_kernel(resumed, items, lengths, x, *refs):
    blocks = refs[: len(refs) - 1 - resumed]
    before = refs[-2] if resumed else None
    total = refs[-1]
    tile = row_tile(x.shape[0])
    pieces = []
    for block in blocks:
        pieces += [block] if len(block.shape) == 3 else [block.at[i] for i in range(block.shape[0])]
    each = max(1, CHUNK // pieces[0].shape[1])
    groups = [pieces[i : i + each] for i in range(0, len(pieces), each)]

    def weight(which, part):
        return jnp.concatenate([piece[which] for piece in part], axis=0)

    def body(index, carry):
        span = tile_rows(index, tile)
        here = x[span, :]
        grown = None if before is None else before[span, :]
        for part in groups:
            gate = nt_dot(here, weight(0, part))
            up = nt_dot(here, weight(1, part))
            active = (jax.nn.gelu(gate, approximate=True) * up).astype(jnp.bfloat16)
            term = jnp.dot(active, weight(2, part), preferred_element_type=jnp.float32)
            grown = term if grown is None else grown + term
        total[span, :] = grown.astype(total.dtype)
        return carry

    lax.fori_loop(0, live_tiles(items, lengths, tile), body, 0)


def hidden(lengths, normed, blocks, before, kind):
    resumed = before is not None
    arrays = (normed, *blocks) + ((before,) if resumed else ())
    out = jax.ShapeDtypeStruct(normed.shape, kind)
    kernel = functools.partial(hidden_kernel, resumed)
    return call(kernel, "hidden", (lengths,), arrays, out)


def pool_kernel(items, lengths, gains, residual, pool, *refs):
    sums, (vectors, candidates) = refs[:-2], refs[-2:]
    tile = row_tile(residual.shape[0])
    slots = 16
    slot = lax.broadcasted_iota(jnp.int32, (slots, 1), 0)
    first = jnp.zeros((slots, 1), jnp.int32)
    last = jnp.zeros((slots, 1), jnp.int32)
    begin = 0
    for item in range(items):
        end = begin + lengths[item]
        first = jnp.where(slot == item, begin, first)
        last = jnp.where(slot == item, end, last)
        begin = end

    def body(index, summed):
        here = tile_rows(index, tile)
        total = residual[here, :].astype(jnp.float32)
        for part in sums:
            total += part[here, :].astype(jnp.float32)
        finished = total.astype(jnp.bfloat16).astype(jnp.float32)
        final_rows = (finished * inverse_rms(finished) * gains[2:3, :]).astype(jnp.bfloat16)
        across = index * tile + lax.broadcasted_iota(jnp.int32, (slots, tile), 1)
        member = jnp.where((across >= first) & (across < last), 1.0, 0.0)
        return summed + jnp.dot(
            member.astype(jnp.bfloat16), final_rows, preferred_element_type=jnp.float32
        )

    summed = lax.fori_loop(
        0, live_tiles(items, lengths, tile), body, jnp.zeros((slots, D), jnp.float32)
    )
    counts = jnp.maximum(last - first, 1).astype(jnp.float32)
    pooled = (summed / counts).astype(jnp.bfloat16)
    e = jnp.dot(pooled, pool[...], preferred_element_type=jnp.float32)
    e = e * inverse_rms(e)
    vectors[...] = e[:items, :]
    mine = e[:items, :].astype(jnp.bfloat16)
    for device in range(candidates.shape[0]):
        candidates[device] = mine


def pool_items(devices, lengths, norm_gains, residual, pool_weight, sums):
    items = lengths.shape[0]
    out = (
        jax.ShapeDtypeStruct((items, D), jnp.float32),
        jax.ShapeDtypeStruct((devices, items, D), jnp.bfloat16),
    )
    arrays = (norm_gains, residual, pool_weight, *sums)
    return call(pool_kernel, "pool_items", (lengths,), arrays, out)


def loss_kernel(queries, list_ids, labels, candidates, loss):
    widened = queries[...].astype(jnp.float32)
    query_unit = (widened * inverse_rms(widened)).astype(jnp.bfloat16)
    each = labels.shape[0]
    chosen = None
    for which in range(LISTS):
        scores = nt_dot(candidates[which * each : (which + 1) * each, :], query_unit)
        if chosen is None:
            chosen = scores
        else:
            chosen = jnp.where(list_ids[...] == which, scores, chosen)
    chosen = chosen * (score_scale / D)
    target = jnp.exp(labels[...].astype(jnp.float32))
    target = target / jnp.sum(target, axis=0, keepdims=True)
    log_total = jnp.log(jnp.sum(jnp.exp(chosen), axis=0, keepdims=True))
    loss[...] = log_total - jnp.sum(target * chosen, axis=0, keepdims=True)


def list_loss(queries, list_ids, labels, candidates):
    count = queries.shape[0]
    return pl.pallas_call(
        loss_kernel,
        out_shape=jax.ShapeDtypeStruct((1, count), jnp.float32),
        compiler_params=pltpu.CompilerParams(vmem_limit_bytes=16 * MIB),
        name="list_loss",
    )(queries, list_ids.reshape(1, count), labels.T, candidates).reshape(count)


def swapped(value, count, bit):
    return lax.ppermute(value, "dp", [(i, i ^ bit) for i in range(count)])


def after(value, *earlier):
    return lax.optimization_barrier((value, earlier))[0]


def local(
    count,
    planes,
    tokens,
    lengths,
    norm_gains,
    query_key_value,
    attention_out,
    expand_weight,
    contract_weight,
    pool_weight,
    queries,
    list_ids,
    labels,
):
    inner = count // OUTER
    core = (lax.axis_index("dp") % 2).astype(jnp.int32).reshape(1)
    their_tokens = swapped(tokens, count, 1)
    their_lengths = swapped(lengths, count, 1)
    counts = (lengths, their_lengths)

    wide = D // 2
    weights = jnp.concatenate(
        [
            lax.dynamic_slice_in_dim(query_key_value, (2 * which + core[0]) * wide, wide, axis=1)
            for which in range(3)
        ],
        axis=1,
    )

    def attend(turn):
        projected = turn(0, project(*counts, tokens, their_tokens, norm_gains, weights))
        some = turn(1, heads(0, 4, *counts, projected))
        mine = turn(2, heads(4, D // HEAD // 2, *counts, projected, some))
        other = swapped(mine, count, 1)
        return join_heads(
            core, *counts, tokens, their_tokens, norm_gains, attention_out, mine, other
        )

    same_core = [list(range(first, count, 2)) for first in range(2)]
    if planes == 2 and inner == 4:

        def hop(value, same, across, crossed):
            pairs = []
            for here in range(planes * count):
                y, place = divmod(here, count)
                z, x, c = place // inner, place % inner // 2, place % 2
                role = 0 if c == y else 1
                link = across if role else same
                if link == "y":
                    y = 1 - y
                elif link == "x":
                    x = 1 - x
                else:
                    z = (z + (1 if link == "up" else OUTER - 1)) % OUTER
                role = 1 - role if crossed else role
                pairs.append((here, y * count + z * inner + x * 2 + (1 - y if role else y)))
            return lax.ppermute(value, ("groups", "dp"), pairs)

        v = [pack_weights(expand_weight, contract_weight)]
        v.append(hop(v[0], "up", "x", False))

        def turn(number, value):
            if number == 0:
                v[1], value = after((v[1], value))
                v.append(hop(v[1], "x", "down", True))
                v.append(hop(v[1], "up", "y", False))
            elif number == 1:
                v[2], value = after((v[2], value))
                v.append(hop(v[2], "x", "y", False))
            else:
                v.append(hop(v[3], "y", "down", False))
                v[3], v[4], value = after((v[3], v[4], value))
                v.append(hop(v[4], "y", "x", False))
            return value

        residual, normed, theirs = attend(turn)
        v[5], normed, theirs = after((v[5], normed, theirs))
        v.append(hop(v[5], "x", "down", True))
        first = tuple(v[:4])
        second = tuple(v[4:6])
        third = tuple(v[6:8])
        own_sum = hidden(lengths, normed, first, None, jnp.float32)
    else:
        packed = jnp.concatenate([expand_weight.transpose(0, 2, 1), contract_weight[None]], axis=0)
        gathered = lax.all_gather(
            packed, "dp", axis=1, tiled=True, axis_index_groups=same_core
        )
        residual, normed, theirs = attend(lambda number, value: value)
        units = gathered.shape[1]
        first = (gathered[:, : units // 2],)
        second = (gathered[:, units // 2 : units // 4 * 3],)
        third = (gathered[:, units // 4 * 3 :],)
        own_sum = hidden(lengths, normed, first, None, jnp.float32)

    their_sum = hidden(their_lengths, theirs, first, None, jnp.float32)
    own_sum = hidden(lengths, normed, second, own_sum, jnp.float32)
    their_sum = hidden(their_lengths, theirs, second, their_sum, jnp.float32)
    third, their_sum = after((third, their_sum), own_sum)
    their_sum = hidden(their_lengths, theirs, third, their_sum, jnp.bfloat16)
    back = swapped(their_sum, count, 1)
    own_sum = hidden(lengths, after(normed, their_sum), third, own_sum, jnp.float32)
    item_vectors, candidates = pool_items(
        count, lengths, norm_gains, residual, pool_weight, (own_sum, back)
    )
    every = lax.all_to_all(candidates, "dp", 0, 0, tiled=True)
    every = every.reshape(count * lengths.shape[0], D)
    return item_vectors, list_loss(queries, list_ids, labels, every)


def solution(mesh):
    return jax.shard_map(
        functools.partial(local, mesh.shape["dp"], mesh.shape["groups"]),
        mesh=mesh,
        in_specs=(
            P(("groups", "dp"), None),
            P(("groups", "dp")),
            P(),
            P(),
            P(),
            P(None, None, "dp"),
            P("dp", None),
            P(),
            P(("groups", "dp"), None),
            P(("groups", "dp")),
            P(("groups", "dp"), None),
        ),
        out_specs=(P(("groups", "dp"), None), P(("groups", "dp"))),
        check_vma=False,
    )
```

```python
import functools

import jax
import jax.numpy as jnp
from jax import lax
from jax.experimental import pallas as pl
from jax.experimental.pallas import tpu as pltpu
from jax.sharding import PartitionSpec as P

D = 768
HEAD = 64
LISTS = 2
OUTER = 4
CHUNK = 256

SCORE_SCALE = HEAD ** (-0.5) * 1.4426950408889634
epsilon = 1e-06
score_scale = 32.0
MIB = 1024 * 1024
SHORT = pl.CostEstimate(flops=1000, bytes_accessed=1000, transcendentals=0)


def inverse_rms(widened):
    return lax.rsqrt(jnp.mean(widened * widened, axis=-1, keepdims=True) + epsilon)


def nt_dot(left, right):
    return lax.dot_general(
        left, right, (((1,), (1,)), ((), ())), preferred_element_type=jnp.float32
    )


def pack_kernel(expand, contract, packed, stage, done):
    grown = pltpu.make_async_copy(expand, stage, done.at[0])
    shrunk = pltpu.make_async_copy(contract, packed.at[2], done.at[1])
    grown.start()
    shrunk.start()
    grown.wait()
    for which in range(2):
        packed[which] = stage[which].T
    shrunk.wait()


def pack_weights(expand_weight, contract_weight):
    in_place = pl.BlockSpec(memory_space=pltpu.HBM)
    return pl.pallas_call(
        pack_kernel,
        out_shape=jax.ShapeDtypeStruct((3,) + contract_weight.shape, jnp.bfloat16),
        in_specs=[in_place, in_place],
        out_specs=pl.BlockSpec(memory_space=pltpu.VMEM),
        scratch_shapes=[
            pltpu.VMEM(expand_weight.shape, jnp.bfloat16),
            pltpu.SemaphoreType.DMA((2,)),
        ],
        compiler_params=pltpu.CompilerParams(vmem_limit_bytes=60 * MIB),
        name="pack_weights",
    )(expand_weight, contract_weight)


def row_tile(rows):
    return 256 if rows % 256 == 0 else rows


def live_tiles(items, lengths, tile):
    total = lengths[0]
    for item in range(1, items):
        total = total + lengths[item]
    return (total + tile - 1) // tile


def tile_rows(index, tile):
    return pl.ds(pl.multiple_of(index * tile, tile), tile)


def project_kernel(items, lengths, tokens, gains, weights, out):
    tile = row_tile(tokens.shape[0])

    def body(index, carry):
        here = tile_rows(index, tile)
        widened = tokens[here, :].astype(jnp.float32)
        x = (widened * inverse_rms(widened) * gains[0:1, :]).astype(jnp.bfloat16)
        for which in range(3):
            span = slice(which * D, (which + 1) * D)
            part = jnp.dot(x, weights[:, span], preferred_element_type=jnp.float32)
            if which == 0:
                part = part * SCORE_SCALE
            out[here, span] = part.astype(jnp.bfloat16)
        return carry

    lax.fori_loop(0, live_tiles(items, lengths, tile), body, 0)


def call(kernel, name, scalars, arrays, out_shape, limit=24):
    whole = pl.BlockSpec(memory_space=pltpu.VMEM)
    return pl.pallas_call(
        functools.partial(kernel, scalars[0].shape[0]),
        in_specs=[pl.BlockSpec(memory_space=pltpu.SMEM)] * len(scalars) + [whole] * len(arrays),
        out_specs=jax.tree.map(lambda _: whole, out_shape),
        out_shape=out_shape,
        compiler_params=pltpu.CompilerParams(vmem_limit_bytes=limit * MIB),
        cost_estimate=SHORT,
        name=name,
    )(*scalars, *arrays)


def project(lengths, tokens, norm_gains, query_key_value):
    out = jax.ShapeDtypeStruct((tokens.shape[0], 3 * D), jnp.bfloat16)
    return call(project_kernel, "project", (lengths,), (tokens, norm_gains, query_key_value), out)


def heads_kernel(items, lengths, projected, mixed_heads):
    rows = projected.shape[0]
    tile = row_tile(rows)
    wide = 2 * HEAD
    group = D // 2
    lane = lax.broadcasted_iota(jnp.int32, (1, wide), 1) // HEAD
    ends = []
    end = 0
    for item in range(items):
        end = end + lengths[item]
        ends.append(end)
    tiles = (end + tile - 1) // tile

    def segment(position):
        return sum((position >= end).astype(jnp.int32) for end in ends)

    for keys in range(tile, rows + 1, tile):
        across = segment(lax.broadcasted_iota(jnp.int32, (1, keys), 1))

        def body(index, carry):
            row = index // 2
            here = tile_rows(row, tile)
            offset = pl.multiple_of(index % 2 * group, group)
            down = segment(row * tile + lax.broadcasted_iota(jnp.int32, (tile, 1), 0))
            same = down == across

            def columns(kind, head):
                return pl.ds(kind * D + offset + head // 2 * wide, wide)

            def scores(head):
                q = projected[here, columns(0, head)]
                q = jnp.where(lane == head % 2, q, jnp.bfloat16(0))
                return nt_dot(q, projected[:keys, columns(1, head)])

            count = group // HEAD
            ahead = scores(0)
            for head in range(count):
                logits = jnp.where(same, ahead, -1e30)
                if head + 1 < count:
                    ahead = scores(head + 1)
                highest = jnp.max(logits, axis=1, keepdims=True)
                weights = jnp.exp2((logits - highest).astype(jnp.bfloat16))
                mine = lane == head % 2
                v = jnp.where(mine, projected[:keys, columns(2, head)], jnp.bfloat16(1))
                out = jnp.dot(weights, v, preferred_element_type=jnp.float32)
                other = (1 - head % 2) * HEAD
                out = out * (1.0 / out[:, other : other + 1])
                mixed = out if head % 2 == 0 else jnp.where(mine, out, mixed)
                if head % 2 == 1:
                    mixed_heads[here, columns(0, head)] = mixed.astype(jnp.bfloat16)
            return carry

        count = keys // tile
        lax.fori_loop(0, jnp.where(tiles == count, 2 * count, 0), body, 0)


def heads(lengths, projected):
    out = jax.ShapeDtypeStruct((projected.shape[0], D), jnp.bfloat16)
    return call(heads_kernel, "heads", (lengths,), (projected,), out)


def join_kernel(items, lengths, tokens, gains, wo, mixed_heads, residual, normed):
    tile = row_tile(tokens.shape[0])

    def body(index, carry):
        here = tile_rows(index, tile)
        total = tokens[here, :].astype(jnp.float32)
        total += jnp.dot(mixed_heads[here, :], wo[...], preferred_element_type=jnp.float32)
        rounded = total.astype(jnp.bfloat16)
        residual[here, :] = rounded
        widened = rounded.astype(jnp.float32)
        normed[here, :] = (widened * inverse_rms(widened) * gains[1:2, :]).astype(jnp.bfloat16)
        return carry

    lax.fori_loop(0, live_tiles(items, lengths, tile), body, 0)


def join_heads(lengths, *arrays):
    rows = jax.ShapeDtypeStruct(arrays[0].shape, jnp.bfloat16)
    return call(join_kernel, "join_heads", (lengths,), arrays, (rows, rows))


def hidden_kernel(resumed, items, lengths, x, *refs):
    blocks = refs[: len(refs) - 1 - resumed]
    before = refs[-2] if resumed else None
    total = refs[-1]
    tile = row_tile(x.shape[0])
    pieces = []
    for block in blocks:
        pieces += [block] if len(block.shape) == 3 else [block.at[i] for i in range(block.shape[0])]
    each = max(1, CHUNK // pieces[0].shape[1])
    groups = [pieces[i : i + each] for i in range(0, len(pieces), each)]

    def weight(which, part):
        return jnp.concatenate([piece[which] for piece in part], axis=0)

    def body(index, carry):
        span = tile_rows(index, tile)
        here = x[span, :]
        grown = None if before is None else before[span, :]
        for part in groups:
            gate = nt_dot(here, weight(0, part))
            up = nt_dot(here, weight(1, part))
            active = (jax.nn.gelu(gate, approximate=True) * up).astype(jnp.bfloat16)
            term = jnp.dot(active, weight(2, part), preferred_element_type=jnp.float32)
            grown = term if grown is None else grown + term
        total[span, :] = grown.astype(total.dtype)
        return carry

    lax.fori_loop(0, live_tiles(items, lengths, tile), body, 0)


def hidden(lengths, normed, blocks, before, kind):
    resumed = before is not None
    arrays = (normed, *blocks) + ((before,) if resumed else ())
    out = jax.ShapeDtypeStruct(normed.shape, kind)
    kernel = functools.partial(hidden_kernel, resumed)
    return call(kernel, "hidden", (lengths,), arrays, out)


def pool_kernel(items, lengths, gains, residual, pool, *refs):
    sums, (vectors, candidates) = refs[:-2], refs[-2:]
    tile = row_tile(residual.shape[0])
    slots = 16
    slot = lax.broadcasted_iota(jnp.int32, (slots, 1), 0)
    first = jnp.zeros((slots, 1), jnp.int32)
    last = jnp.zeros((slots, 1), jnp.int32)
    begin = 0
    for item in range(items):
        end = begin + lengths[item]
        first = jnp.where(slot == item, begin, first)
        last = jnp.where(slot == item, end, last)
        begin = end

    def body(index, summed):
        here = tile_rows(index, tile)
        total = residual[here, :].astype(jnp.float32)
        for part in sums:
            total += part[here, :].astype(jnp.float32)
        finished = total.astype(jnp.bfloat16).astype(jnp.float32)
        final_rows = (finished * inverse_rms(finished) * gains[2:3, :]).astype(jnp.bfloat16)
        across = index * tile + lax.broadcasted_iota(jnp.int32, (slots, tile), 1)
        member = jnp.where((across >= first) & (across < last), 1.0, 0.0)
        return summed + jnp.dot(
            member.astype(jnp.bfloat16), final_rows, preferred_element_type=jnp.float32
        )

    summed = lax.fori_loop(
        0, live_tiles(items, lengths, tile), body, jnp.zeros((slots, D), jnp.float32)
    )
    counts = jnp.maximum(last - first, 1).astype(jnp.float32)
    pooled = (summed / counts).astype(jnp.bfloat16)
    e = jnp.dot(pooled, pool[...], preferred_element_type=jnp.float32)
    e = e * inverse_rms(e)
    vectors[...] = e[:items, :]
    mine = e[:items, :].astype(jnp.bfloat16)
    for device in range(candidates.shape[0]):
        candidates[device] = mine


def pool_items(devices, lengths, norm_gains, residual, pool_weight, sums):
    items = lengths.shape[0]
    out = (
        jax.ShapeDtypeStruct((items, D), jnp.float32),
        jax.ShapeDtypeStruct((devices, items, D), jnp.bfloat16),
    )
    arrays = (norm_gains, residual, pool_weight, *sums)
    return call(pool_kernel, "pool_items", (lengths,), arrays, out)


def loss_kernel(queries, list_ids, labels, candidates, loss):
    widened = queries[...].astype(jnp.float32)
    query_unit = (widened * inverse_rms(widened)).astype(jnp.bfloat16)
    each = labels.shape[0]
    chosen = None
    for which in range(LISTS):
        scores = nt_dot(candidates[which * each : (which + 1) * each, :], query_unit)
        if chosen is None:
            chosen = scores
        else:
            chosen = jnp.where(list_ids[...] == which, scores, chosen)
    chosen = chosen * (score_scale / D)
    target = jnp.exp(labels[...].astype(jnp.float32))
    target = target / jnp.sum(target, axis=0, keepdims=True)
    log_total = jnp.log(jnp.sum(jnp.exp(chosen), axis=0, keepdims=True))
    loss[...] = log_total - jnp.sum(target * chosen, axis=0, keepdims=True)


def list_loss(queries, list_ids, labels, candidates):
    count = queries.shape[0]
    return pl.pallas_call(
        loss_kernel,
        out_shape=jax.ShapeDtypeStruct((1, count), jnp.float32),
        compiler_params=pltpu.CompilerParams(vmem_limit_bytes=16 * MIB),
        name="list_loss",
    )(queries, list_ids.reshape(1, count), labels.T, candidates).reshape(count)


def swapped(value, count, bit):
    return lax.ppermute(value, "dp", [(i, i ^ bit) for i in range(count)])


def after(value, *earlier):
    return lax.optimization_barrier((value, earlier))[0]


def local(
    count,
    planes,
    tokens,
    lengths,
    norm_gains,
    query_key_value,
    attention_out,
    expand_weight,
    contract_weight,
    pool_weight,
    queries,
    list_ids,
    labels,
):
    inner = count // OUTER
    their_lengths = swapped(lengths, count, 1)

    def attend(turn):
        projected = turn(0, project(lengths, tokens, norm_gains, query_key_value))
        mixed_heads = heads(lengths, projected)
        joined = join_heads(lengths, tokens, norm_gains, attention_out, mixed_heads)
        residual, normed = turn(1, joined)
        return residual, normed, swapped(normed, count, 1)

    same_core = [list(range(first, count, 2)) for first in range(2)]
    if planes == 2 and inner == 4:

        def hop(value, same, across, crossed):
            pairs = []
            for here in range(planes * count):
                y, place = divmod(here, count)
                z, x, c = place // inner, place % inner // 2, place % 2
                role = 0 if c == y else 1
                link = across if role else same
                if link == "y":
                    y = 1 - y
                elif link == "x":
                    x = 1 - x
                else:
                    z = (z + (1 if link == "up" else OUTER - 1)) % OUTER
                role = 1 - role if crossed else role
                pairs.append((here, y * count + z * inner + x * 2 + (1 - y if role else y)))
            return lax.ppermute(value, ("groups", "dp"), pairs)

        v = [pack_weights(expand_weight, contract_weight)]
        v.append(hop(v[0], "x", "up", True))

        def turn(number, value):
            if number == 0:
                v[1], value = after((v[1], value))
                v.append(hop(v[1], "up", "down", False))
                v.append(hop(v[1], "x", "y", False))
                v.append(hop(v[1], "y", "up", False))
            else:
                v[2:5], value = after((v[2:5], value))
                v.append(hop(v[2], "up", "y", False))
                v.append(hop(v[2], "x", "x", False))
                v.append(hop(v[2], "y", "down", False))
            return value

        residual, normed, theirs = attend(turn)
        first = tuple(v[:5])
        third = tuple(v[5:8])
        own_sum = hidden(lengths, normed, first, None, jnp.float32)
    else:
        packed = jnp.concatenate([expand_weight.transpose(0, 2, 1), contract_weight[None]], axis=0)
        gathered = lax.all_gather(
            packed, "dp", axis=1, tiled=True, axis_index_groups=same_core
        )
        residual, normed, theirs = attend(lambda number, value: value)
        units = gathered.shape[1]
        first = (gathered[:, : units // 2],)
        third = (gathered[:, units // 2 :],)
        own_sum = hidden(lengths, normed, first, None, jnp.float32)

    their_sum = hidden(their_lengths, theirs, first, None, jnp.float32)
    third, their_sum = after((third, their_sum), own_sum)
    their_sum = hidden(their_lengths, theirs, third, their_sum, jnp.bfloat16)
    back = swapped(their_sum, count, 1)
    own_sum = hidden(lengths, after(normed, their_sum), third, own_sum, jnp.float32)
    item_vectors, candidates = pool_items(
        count, lengths, norm_gains, residual, pool_weight, (own_sum, back)
    )
    every = lax.all_to_all(candidates, "dp", 0, 0, tiled=True)
    every = every.reshape(count * lengths.shape[0], D)
    return item_vectors, list_loss(queries, list_ids, labels, every)


def solution(mesh):
    return jax.shard_map(
        functools.partial(local, mesh.shape["dp"], mesh.shape["groups"]),
        mesh=mesh,
        in_specs=(
            P(("groups", "dp"), None),
            P(("groups", "dp")),
            P(),
            P(),
            P(),
            P(None, None, "dp"),
            P("dp", None),
            P(),
            P(("groups", "dp"), None),
            P(("groups", "dp")),
            P(("groups", "dp"), None),
        ),
        out_specs=(P(("groups", "dp"), None), P(("groups", "dp"))),
        check_vma=False,
    )
```

```python
import functools

import jax
import jax.numpy as jnp
from jax import lax
from jax.experimental import pallas as pl
from jax.experimental.pallas import tpu as pltpu
from jax.sharding import PartitionSpec as P

D = 768
HEAD = 64
LISTS = 2
OUTER = 4
CHUNK = 256

SCORE_SCALE = HEAD ** (-0.5) * 1.4426950408889634
epsilon = 1e-06
score_scale = 32.0
MIB = 1024 * 1024
SHORT = pl.CostEstimate(flops=1000, bytes_accessed=1000, transcendentals=0)


def inverse_rms(widened):
    return lax.rsqrt(jnp.mean(widened * widened, axis=-1, keepdims=True) + epsilon)


def nt_dot(left, right):
    return lax.dot_general(
        left, right, (((1,), (1,)), ((), ())), preferred_element_type=jnp.float32
    )


LANES = 128


def pack_kernel(expand, contract, packed, done):
    copies = [
        pltpu.make_async_copy(expand.at[which], packed.at[which], done.at[which])
        for which in range(2)
    ]
    for piece in range(D // LANES):
        columns = slice(piece * LANES, (piece + 1) * LANES)
        source, target = contract.at[:, columns], packed.at[2, columns, :]
        copies.append(pltpu.make_async_copy(source, target, done.at[2 + piece]))
    for copy in copies:
        copy.start()
    for copy in copies:
        copy.wait()


def pack_weights(expand_weight, contract_weight):
    in_place = pl.BlockSpec(memory_space=pltpu.HBM)
    return pl.pallas_call(
        pack_kernel,
        out_shape=jax.ShapeDtypeStruct((3, D, LANES), jnp.bfloat16),
        in_specs=[in_place, in_place],
        out_specs=in_place,
        scratch_shapes=[pltpu.SemaphoreType.DMA((2 + D // LANES,))],
        compiler_params=pltpu.CompilerParams(vmem_limit_bytes=60 * MIB),
        name="pack_weights",
    )(expand_weight, contract_weight)


def row_tile(rows):
    return 256 if rows % 256 == 0 else rows


def live_tiles(items, lengths, tile):
    total = lengths[0]
    for item in range(1, items):
        total = total + lengths[item]
    return (total + tile - 1) // tile


def tile_rows(index, tile):
    return pl.ds(pl.multiple_of(index * tile, tile), tile)


def project_kernel(items, lengths, tokens, gains, weights, out):
    tile = row_tile(tokens.shape[0])

    def body(index, carry):
        here = tile_rows(index, tile)
        widened = tokens[here, :].astype(jnp.float32)
        x = (widened * inverse_rms(widened) * gains[0:1, :]).astype(jnp.bfloat16)
        for which in range(3):
            span = slice(which * D, (which + 1) * D)
            part = jnp.dot(x, weights[:, span], preferred_element_type=jnp.float32)
            if which == 0:
                part = part * SCORE_SCALE
            out[here, span] = part.astype(jnp.bfloat16)
        return carry

    lax.fori_loop(0, live_tiles(items, lengths, tile), body, 0)


def call(kernel, name, scalars, arrays, out_shape, limit=24):
    whole = pl.BlockSpec(memory_space=pltpu.VMEM)
    return pl.pallas_call(
        functools.partial(kernel, scalars[0].shape[0]),
        in_specs=[pl.BlockSpec(memory_space=pltpu.SMEM)] * len(scalars) + [whole] * len(arrays),
        out_specs=jax.tree.map(lambda _: whole, out_shape),
        out_shape=out_shape,
        compiler_params=pltpu.CompilerParams(vmem_limit_bytes=limit * MIB),
        cost_estimate=SHORT,
        name=name,
    )(*scalars, *arrays)


def project(lengths, tokens, norm_gains, query_key_value):
    out = jax.ShapeDtypeStruct((tokens.shape[0], 3 * D), jnp.bfloat16)
    return call(project_kernel, "project", (lengths,), (tokens, norm_gains, query_key_value), out)


def heads_kernel(items, lengths, projected, mixed_heads):
    rows = projected.shape[0]
    tile = row_tile(rows)
    wide = 2 * HEAD
    group = D // 2
    lane = lax.broadcasted_iota(jnp.int32, (1, wide), 1) // HEAD
    ends = []
    end = 0
    for item in range(items):
        end = end + lengths[item]
        ends.append(end)
    tiles = (end + tile - 1) // tile

    def segment(position):
        return sum((position >= end).astype(jnp.int32) for end in ends)

    for keys in range(tile, rows + 1, tile):
        across = segment(lax.broadcasted_iota(jnp.int32, (1, keys), 1))

        def body(index, carry):
            row = index // 2
            here = tile_rows(row, tile)
            offset = pl.multiple_of(index % 2 * group, group)
            down = segment(row * tile + lax.broadcasted_iota(jnp.int32, (tile, 1), 0))
            same = down == across

            def columns(kind, head):
                return pl.ds(kind * D + offset + head // 2 * wide, wide)

            def scores(head):
                q = projected[here, columns(0, head)]
                q = jnp.where(lane == head % 2, q, jnp.bfloat16(0))
                return nt_dot(q, projected[:keys, columns(1, head)])

            count = group // HEAD
            ahead = scores(0)
            for head in range(count):
                logits = jnp.where(same, ahead, -1e30)
                if head + 1 < count:
                    ahead = scores(head + 1)
                highest = jnp.max(logits, axis=1, keepdims=True)
                weights = jnp.exp2((logits - highest).astype(jnp.bfloat16))
                mine = lane == head % 2
                v = jnp.where(mine, projected[:keys, columns(2, head)], jnp.bfloat16(1))
                out = jnp.dot(weights, v, preferred_element_type=jnp.float32)
                other = (1 - head % 2) * HEAD
                out = out * (1.0 / out[:, other : other + 1])
                mixed = out if head % 2 == 0 else jnp.where(mine, out, mixed)
                if head % 2 == 1:
                    mixed_heads[here, columns(0, head)] = mixed.astype(jnp.bfloat16)
            return carry

        count = keys // tile
        lax.fori_loop(0, jnp.where(tiles == count, 2 * count, 0), body, 0)


def heads(lengths, projected):
    out = jax.ShapeDtypeStruct((projected.shape[0], D), jnp.bfloat16)
    return call(heads_kernel, "heads", (lengths,), (projected,), out)


def join_kernel(items, lengths, tokens, gains, wo, mixed_heads, residual, normed):
    tile = row_tile(tokens.shape[0])

    def body(index, carry):
        here = tile_rows(index, tile)
        total = tokens[here, :].astype(jnp.float32)
        total += jnp.dot(mixed_heads[here, :], wo[...], preferred_element_type=jnp.float32)
        rounded = total.astype(jnp.bfloat16)
        residual[here, :] = rounded
        widened = rounded.astype(jnp.float32)
        normed[here, :] = (widened * inverse_rms(widened) * gains[1:2, :]).astype(jnp.bfloat16)
        return carry

    lax.fori_loop(0, live_tiles(items, lengths, tile), body, 0)


def join_heads(lengths, *arrays):
    rows = jax.ShapeDtypeStruct(arrays[0].shape, jnp.bfloat16)
    return call(join_kernel, "join_heads", (lengths,), arrays, (rows, rows))


def hidden_kernel(resumed, items, lengths, x, *refs):
    blocks = refs[: len(refs) - 1 - resumed]
    before = refs[-2] if resumed else None
    total = refs[-1]
    tile = row_tile(x.shape[0])
    each = CHUNK // LANES
    groups = [blocks[i : i + each] for i in range(0, len(blocks), each)]

    def grow(which, part):
        return jnp.concatenate([block[which] for block in part], axis=1)

    def shrink(part):
        rows = []
        for block in part:
            pieces = [block[2, i : i + LANES, :] for i in range(0, D, LANES)]
            rows.append(jnp.concatenate(pieces, axis=1))
        return jnp.concatenate(rows, axis=0)

    def body(index, carry):
        span = tile_rows(index, tile)
        here = x[span, :]
        grown = None if before is None else before[span, :]
        for part in groups:
            gate = jnp.dot(here, grow(0, part), preferred_element_type=jnp.float32)
            up = jnp.dot(here, grow(1, part), preferred_element_type=jnp.float32)
            active = (jax.nn.gelu(gate, approximate=True) * up).astype(jnp.bfloat16)
            term = jnp.dot(active, shrink(part), preferred_element_type=jnp.float32)
            grown = term if grown is None else grown + term
        total[span, :] = grown.astype(total.dtype)
        return carry

    lax.fori_loop(0, live_tiles(items, lengths, tile), body, 0)


def hidden(lengths, normed, blocks, before, kind):
    resumed = before is not None
    arrays = (normed, *blocks) + ((before,) if resumed else ())
    out = jax.ShapeDtypeStruct(normed.shape, kind)
    kernel = functools.partial(hidden_kernel, resumed)
    return call(kernel, "hidden", (lengths,), arrays, out)


def pool_kernel(items, lengths, gains, residual, pool, *refs):
    sums, (vectors, candidates) = refs[:-2], refs[-2:]
    tile = row_tile(residual.shape[0])
    slots = 16
    slot = lax.broadcasted_iota(jnp.int32, (slots, 1), 0)
    first = jnp.zeros((slots, 1), jnp.int32)
    last = jnp.zeros((slots, 1), jnp.int32)
    begin = 0
    for item in range(items):
        end = begin + lengths[item]
        first = jnp.where(slot == item, begin, first)
        last = jnp.where(slot == item, end, last)
        begin = end

    def body(index, summed):
        here = tile_rows(index, tile)
        total = residual[here, :].astype(jnp.float32)
        for part in sums:
            total += part[here, :].astype(jnp.float32)
        finished = total.astype(jnp.bfloat16).astype(jnp.float32)
        final_rows = (finished * inverse_rms(finished) * gains[2:3, :]).astype(jnp.bfloat16)
        across = index * tile + lax.broadcasted_iota(jnp.int32, (slots, tile), 1)
        member = jnp.where((across >= first) & (across < last), 1.0, 0.0)
        return summed + jnp.dot(
            member.astype(jnp.bfloat16), final_rows, preferred_element_type=jnp.float32
        )

    summed = lax.fori_loop(
        0, live_tiles(items, lengths, tile), body, jnp.zeros((slots, D), jnp.float32)
    )
    counts = jnp.maximum(last - first, 1).astype(jnp.float32)
    pooled = (summed / counts).astype(jnp.bfloat16)
    e = jnp.dot(pooled, pool[...], preferred_element_type=jnp.float32)
    e = e * inverse_rms(e)
    vectors[...] = e[:items, :]
    mine = e[:items, :].astype(jnp.bfloat16)
    for device in range(candidates.shape[0]):
        candidates[device] = mine


def pool_items(devices, lengths, norm_gains, residual, pool_weight, sums):
    items = lengths.shape[0]
    out = (
        jax.ShapeDtypeStruct((items, D), jnp.float32),
        jax.ShapeDtypeStruct((devices, items, D), jnp.bfloat16),
    )
    arrays = (norm_gains, residual, pool_weight, *sums)
    return call(pool_kernel, "pool_items", (lengths,), arrays, out)


def loss_kernel(queries, list_ids, labels, candidates, loss):
    widened = queries[...].astype(jnp.float32)
    query_unit = (widened * inverse_rms(widened)).astype(jnp.bfloat16)
    each = labels.shape[0]
    chosen = None
    for which in range(LISTS):
        scores = nt_dot(candidates[which * each : (which + 1) * each, :], query_unit)
        if chosen is None:
            chosen = scores
        else:
            chosen = jnp.where(list_ids[...] == which, scores, chosen)
    chosen = chosen * (score_scale / D)
    target = jnp.exp(labels[...].astype(jnp.float32))
    target = target / jnp.sum(target, axis=0, keepdims=True)
    log_total = jnp.log(jnp.sum(jnp.exp(chosen), axis=0, keepdims=True))
    loss[...] = log_total - jnp.sum(target * chosen, axis=0, keepdims=True)


def list_loss(queries, list_ids, labels, candidates):
    count = queries.shape[0]
    return pl.pallas_call(
        loss_kernel,
        out_shape=jax.ShapeDtypeStruct((1, count), jnp.float32),
        compiler_params=pltpu.CompilerParams(vmem_limit_bytes=16 * MIB),
        name="list_loss",
    )(queries, list_ids.reshape(1, count), labels.T, candidates).reshape(count)


def swapped(value, count, bit):
    return lax.ppermute(value, "dp", [(i, i ^ bit) for i in range(count)])


def after(value, *earlier):
    return lax.optimization_barrier((value, earlier))[0]


def local(
    count,
    planes,
    tokens,
    lengths,
    norm_gains,
    query_key_value,
    attention_out,
    expand_weight,
    contract_weight,
    pool_weight,
    queries,
    list_ids,
    labels,
):
    inner = count // OUTER
    their_lengths = swapped(lengths, count, 1)

    def attend(turn):
        projected = turn(0, project(lengths, tokens, norm_gains, query_key_value))
        mixed_heads = heads(lengths, projected)
        residual, normed = join_heads(lengths, tokens, norm_gains, attention_out, mixed_heads)
        return residual, turn(1, normed), swapped(normed, count, 1)

    same_core = [list(range(first, count, 2)) for first in range(2)]
    if planes == 2 and inner == 4 and contract_weight.shape[0] == LANES:

        def hop(value, same, across, crossed):
            pairs = []
            for here in range(planes * count):
                y, place = divmod(here, count)
                z, x, c = place // inner, place % inner // 2, place % 2
                role = 0 if c == y else 1
                link = across if role else same
                if link == "y":
                    y = 1 - y
                elif link == "x":
                    x = 1 - x
                else:
                    z = (z + (1 if link == "up" else OUTER - 1)) % OUTER
                role = 1 - role if crossed else role
                pairs.append((here, y * count + z * inner + x * 2 + (1 - y if role else y)))
            return lax.ppermute(value, ("groups", "dp"), pairs)

        v = [pack_weights(expand_weight, contract_weight)]
        v.append(hop(v[0], "x", "up", True))

        def turn(number, value):
            if number == 0:
                v[1], value = after((v[1], value))
                v.append(hop(v[1], "up", "down", False))
                v.append(hop(v[1], "y", "up", False))
                v.append(hop(v[1], "x", "y", False))
            else:
                v[2:5], value = after((v[2:5], value))
                v.append(hop(v[2], "up", "y", False))
                v.append(hop(v[2], "x", "x", False))
                v.append(hop(v[2], "y", "down", False))
            return value

        residual, normed, theirs = attend(turn)
        first = tuple(v[:5])
        third = tuple(v[5:8])
        own_sum = hidden(lengths, normed, first, None, jnp.float32)
    else:
        grown = lax.all_gather(
            expand_weight, "dp", axis=2, tiled=True, axis_index_groups=same_core
        )
        shrunk = lax.all_gather(
            contract_weight, "dp", axis=0, tiled=True, axis_index_groups=same_core
        )
        grown = grown.reshape(2, D, -1, LANES).transpose(2, 0, 1, 3)
        shrunk = shrunk.reshape(-1, LANES, D // LANES, LANES).transpose(0, 2, 1, 3)
        v = jnp.concatenate([grown, shrunk.reshape(-1, 1, D, LANES)], axis=1)
        residual, normed, theirs = attend(lambda number, value: value)
        first = tuple(v[:5])
        third = tuple(v[5:])
        own_sum = hidden(lengths, normed, first, None, jnp.float32)

    their_sum = hidden(their_lengths, theirs, first, None, jnp.float32)
    third, their_sum = after((third, their_sum), own_sum)
    their_sum = hidden(their_lengths, theirs, third, their_sum, jnp.bfloat16)
    back = swapped(their_sum, count, 1)
    own_sum = hidden(lengths, after(normed, their_sum), third, own_sum, jnp.float32)
    item_vectors, candidates = pool_items(
        count, lengths, norm_gains, residual, pool_weight, (own_sum, back)
    )
    every = lax.all_to_all(candidates, "dp", 0, 0, tiled=True)
    every = every.reshape(count * lengths.shape[0], D)
    return item_vectors, list_loss(queries, list_ids, labels, every)


def solution(mesh):
    return jax.shard_map(
        functools.partial(local, mesh.shape["dp"], mesh.shape["groups"]),
        mesh=mesh,
        in_specs=(
            P(("groups", "dp"), None),
            P(("groups", "dp")),
            P(),
            P(),
            P(),
            P(None, None, "dp"),
            P("dp", None),
            P(),
            P(("groups", "dp"), None),
            P(("groups", "dp")),
            P(("groups", "dp"), None),
        ),
        out_specs=(P(("groups", "dp"), None), P(("groups", "dp"))),
        check_vma=False,
    )
```

```python
import functools

import jax
import jax.numpy as jnp
from jax import lax
from jax.experimental import pallas as pl
from jax.experimental.pallas import tpu as pltpu
from jax.sharding import PartitionSpec as P

D = 768
HEAD = 64
LISTS = 2
OUTER = 4
CHUNK = 256

SCORE_SCALE = HEAD ** (-0.5) * 1.4426950408889634
epsilon = 1e-06
score_scale = 32.0
MIB = 1024 * 1024
SHORT = pl.CostEstimate(flops=1000, bytes_accessed=1000, transcendentals=0)


def inverse_rms(widened):
    return lax.rsqrt(jnp.mean(widened * widened, axis=-1, keepdims=True) + epsilon)


def nt_dot(left, right):
    return lax.dot_general(
        left, right, (((1,), (1,)), ((), ())), preferred_element_type=jnp.float32
    )


LANES = 128


def pack_kernel(expand, contract, packed, done):
    copies = [
        pltpu.make_async_copy(expand.at[which], packed.at[which], done.at[which])
        for which in range(2)
    ]
    for piece in range(D // LANES):
        columns = slice(piece * LANES, (piece + 1) * LANES)
        source, target = contract.at[:, columns], packed.at[2, columns, :]
        copies.append(pltpu.make_async_copy(source, target, done.at[2 + piece]))
    for copy in copies:
        copy.start()
    for copy in copies:
        copy.wait()


def pack_weights(expand_weight, contract_weight):
    in_place = pl.BlockSpec(memory_space=pltpu.HBM)
    return pl.pallas_call(
        pack_kernel,
        out_shape=jax.ShapeDtypeStruct((3, D, LANES), jnp.bfloat16),
        in_specs=[in_place, in_place],
        out_specs=pl.BlockSpec(memory_space=pltpu.VMEM),
        scratch_shapes=[pltpu.SemaphoreType.DMA((2 + D // LANES,))],
        compiler_params=pltpu.CompilerParams(vmem_limit_bytes=60 * MIB),
        name="pack_weights",
    )(expand_weight, contract_weight)


def row_tile(rows):
    return 256 if rows % 256 == 0 else rows


def live_tiles(items, lengths, tile):
    total = lengths[0]
    for item in range(1, items):
        total = total + lengths[item]
    return (total + tile - 1) // tile


def tile_rows(index, tile):
    return pl.ds(pl.multiple_of(index * tile, tile), tile)


def project_kernel(items, lengths, tokens, gains, weights, out):
    tile = row_tile(tokens.shape[0])

    def body(index, carry):
        here = tile_rows(index, tile)
        widened = tokens[here, :].astype(jnp.float32)
        x = (widened * inverse_rms(widened) * gains[0:1, :]).astype(jnp.bfloat16)
        for which in range(3):
            span = slice(which * D, (which + 1) * D)
            part = jnp.dot(x, weights[:, span], preferred_element_type=jnp.float32)
            if which == 0:
                part = part * SCORE_SCALE
            out[here, span] = part.astype(jnp.bfloat16)
        return carry

    lax.fori_loop(0, live_tiles(items, lengths, tile), body, 0)


def call(kernel, name, scalars, arrays, out_shape, limit=24):
    whole = pl.BlockSpec(memory_space=pltpu.VMEM)
    return pl.pallas_call(
        functools.partial(kernel, scalars[0].shape[0]),
        in_specs=[pl.BlockSpec(memory_space=pltpu.SMEM)] * len(scalars) + [whole] * len(arrays),
        out_specs=jax.tree.map(lambda _: whole, out_shape),
        out_shape=out_shape,
        compiler_params=pltpu.CompilerParams(vmem_limit_bytes=limit * MIB),
        cost_estimate=SHORT,
        name=name,
    )(*scalars, *arrays)


def project(lengths, tokens, norm_gains, query_key_value):
    out = jax.ShapeDtypeStruct((tokens.shape[0], 3 * D), jnp.bfloat16)
    return call(project_kernel, "project", (lengths,), (tokens, norm_gains, query_key_value), out)


def heads_kernel(items, lengths, projected, mixed_heads):
    rows = projected.shape[0]
    tile = row_tile(rows)
    wide = 2 * HEAD
    group = D // 2
    lane = lax.broadcasted_iota(jnp.int32, (1, wide), 1) // HEAD
    ends = []
    end = 0
    for item in range(items):
        end = end + lengths[item]
        ends.append(end)
    tiles = (end + tile - 1) // tile

    def segment(position):
        return sum((position >= end).astype(jnp.int32) for end in ends)

    for keys in range(tile, rows + 1, tile):
        across = segment(lax.broadcasted_iota(jnp.int32, (1, keys), 1))

        def body(index, carry):
            row = index // 2
            here = tile_rows(row, tile)
            offset = pl.multiple_of(index % 2 * group, group)
            down = segment(row * tile + lax.broadcasted_iota(jnp.int32, (tile, 1), 0))
            same = down == across

            def columns(kind, head):
                return pl.ds(kind * D + offset + head // 2 * wide, wide)

            def scores(head):
                q = projected[here, columns(0, head)]
                q = jnp.where(lane == head % 2, q, jnp.bfloat16(0))
                return nt_dot(q, projected[:keys, columns(1, head)])

            count = group // HEAD
            ahead = scores(0)
            for head in range(count):
                logits = jnp.where(same, ahead, -1e30)
                if head + 1 < count:
                    ahead = scores(head + 1)
                highest = jnp.max(logits, axis=1, keepdims=True)
                weights = jnp.exp2((logits - highest).astype(jnp.bfloat16))
                mine = lane == head % 2
                v = jnp.where(mine, projected[:keys, columns(2, head)], jnp.bfloat16(1))
                out = jnp.dot(weights, v, preferred_element_type=jnp.float32)
                other = (1 - head % 2) * HEAD
                out = out * (1.0 / out[:, other : other + 1])
                mixed = out if head % 2 == 0 else jnp.where(mine, out, mixed)
                if head % 2 == 1:
                    mixed_heads[here, columns(0, head)] = mixed.astype(jnp.bfloat16)
            return carry

        count = keys // tile
        lax.fori_loop(0, jnp.where(tiles == count, 2 * count, 0), body, 0)


def heads(lengths, projected):
    out = jax.ShapeDtypeStruct((projected.shape[0], D), jnp.bfloat16)
    return call(heads_kernel, "heads", (lengths,), (projected,), out)


def join_kernel(items, lengths, tokens, gains, wo, mixed_heads, residual, normed):
    tile = row_tile(tokens.shape[0])

    def body(index, carry):
        here = tile_rows(index, tile)
        total = tokens[here, :].astype(jnp.float32)
        total += jnp.dot(mixed_heads[here, :], wo[...], preferred_element_type=jnp.float32)
        rounded = total.astype(jnp.bfloat16)
        residual[here, :] = rounded
        widened = rounded.astype(jnp.float32)
        normed[here, :] = (widened * inverse_rms(widened) * gains[1:2, :]).astype(jnp.bfloat16)
        return carry

    lax.fori_loop(0, live_tiles(items, lengths, tile), body, 0)


def join_heads(lengths, *arrays):
    rows = jax.ShapeDtypeStruct(arrays[0].shape, jnp.bfloat16)
    return call(join_kernel, "join_heads", (lengths,), arrays, (rows, rows))


def hidden_kernel(resumed, items, lengths, x, *refs):
    blocks = refs[: len(refs) - 1 - resumed]
    before = refs[-2] if resumed else None
    total = refs[-1]
    tile = row_tile(x.shape[0])
    each = CHUNK // LANES
    groups = [blocks[i : i + each] for i in range(0, len(blocks), each)]

    def grow(which, part):
        return jnp.concatenate([block[which] for block in part], axis=1)

    def shrink(part):
        rows = []
        for block in part:
            pieces = [block[2, i : i + LANES, :] for i in range(0, D, LANES)]
            rows.append(jnp.concatenate(pieces, axis=1))
        return jnp.concatenate(rows, axis=0)

    def one_tile(span):
        here = x[span, :]
        grown = None if before is None else before[span, :]
        for part in groups:
            gate = jnp.dot(here, grow(0, part), preferred_element_type=jnp.float32)
            up = jnp.dot(here, grow(1, part), preferred_element_type=jnp.float32)
            active = (jax.nn.gelu(gate, approximate=True) * up).astype(jnp.bfloat16)
            term = jnp.dot(active, shrink(part), preferred_element_type=jnp.float32)
            grown = term if grown is None else grown + term
        total[span, :] = grown.astype(total.dtype)

    def body(index, carry):
        one_tile(tile_rows(index, tile))
        return carry

    tiles = live_tiles(items, lengths, tile)
    every = x.shape[0] // tile
    lax.fori_loop(0, jnp.where(tiles == every, 0, tiles), body, 0)

    @pl.when(tiles == every)
    def _():
        for index in range(every):
            one_tile(slice(index * tile, (index + 1) * tile))


def hidden(lengths, normed, blocks, before, kind):
    resumed = before is not None
    arrays = (normed, *blocks) + ((before,) if resumed else ())
    out = jax.ShapeDtypeStruct(normed.shape, kind)
    kernel = functools.partial(hidden_kernel, resumed)
    return call(kernel, "hidden", (lengths,), arrays, out)


def pool_kernel(items, lengths, gains, residual, pool, *refs):
    sums, (vectors, candidates) = refs[:-2], refs[-2:]
    tile = row_tile(residual.shape[0])
    slots = 16
    slot = lax.broadcasted_iota(jnp.int32, (slots, 1), 0)
    first = jnp.zeros((slots, 1), jnp.int32)
    last = jnp.zeros((slots, 1), jnp.int32)
    begin = 0
    for item in range(items):
        end = begin + lengths[item]
        first = jnp.where(slot == item, begin, first)
        last = jnp.where(slot == item, end, last)
        begin = end

    def body(index, summed):
        here = tile_rows(index, tile)
        total = residual[here, :].astype(jnp.float32)
        for part in sums:
            total += part[here, :].astype(jnp.float32)
        finished = total.astype(jnp.bfloat16).astype(jnp.float32)
        final_rows = (finished * inverse_rms(finished) * gains[2:3, :]).astype(jnp.bfloat16)
        across = index * tile + lax.broadcasted_iota(jnp.int32, (slots, tile), 1)
        member = jnp.where((across >= first) & (across < last), 1.0, 0.0)
        return summed + jnp.dot(
            member.astype(jnp.bfloat16), final_rows, preferred_element_type=jnp.float32
        )

    summed = lax.fori_loop(
        0, live_tiles(items, lengths, tile), body, jnp.zeros((slots, D), jnp.float32)
    )
    counts = jnp.maximum(last - first, 1).astype(jnp.float32)
    pooled = (summed / counts).astype(jnp.bfloat16)
    e = jnp.dot(pooled, pool[...], preferred_element_type=jnp.float32)
    e = e * inverse_rms(e)
    vectors[...] = e[:items, :]
    mine = e[:items, :].astype(jnp.bfloat16)
    for device in range(candidates.shape[0]):
        candidates[device] = mine


def pool_items(devices, lengths, norm_gains, residual, pool_weight, sums):
    items = lengths.shape[0]
    out = (
        jax.ShapeDtypeStruct((items, D), jnp.float32),
        jax.ShapeDtypeStruct((devices, items, D), jnp.bfloat16),
    )
    arrays = (norm_gains, residual, pool_weight, *sums)
    return call(pool_kernel, "pool_items", (lengths,), arrays, out)


def loss_kernel(queries, list_ids, labels, candidates, loss):
    widened = queries[...].astype(jnp.float32)
    query_unit = (widened * inverse_rms(widened)).astype(jnp.bfloat16)
    each = labels.shape[0]
    chosen = None
    for which in range(LISTS):
        scores = nt_dot(candidates[which * each : (which + 1) * each, :], query_unit)
        if chosen is None:
            chosen = scores
        else:
            chosen = jnp.where(list_ids[...] == which, scores, chosen)
    chosen = chosen * (score_scale / D)
    target = jnp.exp(labels[...].astype(jnp.float32))
    target = target / jnp.sum(target, axis=0, keepdims=True)
    log_total = jnp.log(jnp.sum(jnp.exp(chosen), axis=0, keepdims=True))
    loss[...] = log_total - jnp.sum(target * chosen, axis=0, keepdims=True)


def list_loss(queries, list_ids, labels, candidates):
    count = queries.shape[0]
    return pl.pallas_call(
        loss_kernel,
        out_shape=jax.ShapeDtypeStruct((1, count), jnp.float32),
        compiler_params=pltpu.CompilerParams(vmem_limit_bytes=16 * MIB),
        name="list_loss",
    )(queries, list_ids.reshape(1, count), labels.T, candidates).reshape(count)


def swapped(value, count, bit):
    return lax.ppermute(value, "dp", [(i, i ^ bit) for i in range(count)])


def after(value, *earlier):
    return lax.optimization_barrier((value, earlier))[0]


def local(
    count,
    planes,
    tokens,
    lengths,
    norm_gains,
    query_key_value,
    attention_out,
    expand_weight,
    contract_weight,
    pool_weight,
    queries,
    list_ids,
    labels,
):
    inner = count // OUTER
    their_lengths = swapped(lengths, count, 1)

    def attend(turn):
        projected = turn(0, project(lengths, tokens, norm_gains, query_key_value))
        mixed_heads = heads(lengths, projected)
        residual, normed = join_heads(lengths, tokens, norm_gains, attention_out, mixed_heads)
        return residual, turn(1, normed), swapped(normed, count, 1)

    same_core = [list(range(first, count, 2)) for first in range(2)]
    if planes == 2 and inner == 4 and contract_weight.shape[0] == LANES:

        def hop(value, same, across, crossed):
            pairs = []
            for here in range(planes * count):
                y, place = divmod(here, count)
                z, x, c = place // inner, place % inner // 2, place % 2
                role = 0 if c == y else 1
                link = across if role else same
                if link == "y":
                    y = 1 - y
                elif link == "x":
                    x = 1 - x
                else:
                    z = (z + (1 if link == "up" else OUTER - 1)) % OUTER
                role = 1 - role if crossed else role
                pairs.append((here, y * count + z * inner + x * 2 + (1 - y if role else y)))
            return lax.ppermute(value, ("groups", "dp"), pairs)

        v = [pack_weights(expand_weight, contract_weight)]
        v.append(hop(v[0], "x", "up", True))

        def turn(number, value):
            if number == 0:
                v[1], value = after((v[1], value))
                v.append(hop(v[1], "up", "down", False))
                v.append(hop(v[1], "y", "up", False))
                v.append(hop(v[1], "x", "y", False))
            else:
                v[2:5], value = after((v[2:5], value))
                v.append(hop(v[2], "up", "y", False))
                v.append(hop(v[2], "x", "x", False))
                v.append(hop(v[2], "y", "down", False))
            return value

        residual, normed, theirs = attend(turn)
        first = tuple(v[:5])
        third = tuple(v[5:8])
        own_sum = hidden(lengths, normed, first, None, jnp.float32)
    else:
        grown = lax.all_gather(
            expand_weight, "dp", axis=2, tiled=True, axis_index_groups=same_core
        )
        shrunk = lax.all_gather(
            contract_weight, "dp", axis=0, tiled=True, axis_index_groups=same_core
        )
        grown = grown.reshape(2, D, -1, LANES).transpose(2, 0, 1, 3)
        shrunk = shrunk.reshape(-1, LANES, D // LANES, LANES).transpose(0, 2, 1, 3)
        v = jnp.concatenate([grown, shrunk.reshape(-1, 1, D, LANES)], axis=1)
        residual, normed, theirs = attend(lambda number, value: value)
        first = tuple(v[:5])
        third = tuple(v[5:])
        own_sum = hidden(lengths, normed, first, None, jnp.float32)

    their_sum = hidden(their_lengths, theirs, first, None, jnp.float32)
    third, their_sum = after((third, their_sum), own_sum)
    their_sum = hidden(their_lengths, theirs, third, their_sum, jnp.bfloat16)
    back = swapped(their_sum, count, 1)
    own_sum = hidden(lengths, after(normed, their_sum), third, own_sum, jnp.float32)
    item_vectors, candidates = pool_items(
        count, lengths, norm_gains, residual, pool_weight, (own_sum, back)
    )
    every = lax.all_to_all(candidates, "dp", 0, 0, tiled=True)
    every = every.reshape(count * lengths.shape[0], D)
    return item_vectors, list_loss(queries, list_ids, labels, every)


def solution(mesh):
    return jax.shard_map(
        functools.partial(local, mesh.shape["dp"], mesh.shape["groups"]),
        mesh=mesh,
        in_specs=(
            P(("groups", "dp"), None),
            P(("groups", "dp")),
            P(),
            P(),
            P(),
            P(None, None, "dp"),
            P("dp", None),
            P(),
            P(("groups", "dp"), None),
            P(("groups", "dp")),
            P(("groups", "dp"), None),
        ),
        out_specs=(P(("groups", "dp"), None), P(("groups", "dp"))),
        check_vma=False,
    )
```

```python
import functools

import jax
import jax.numpy as jnp
from jax import lax
from jax.experimental import pallas as pl
from jax.experimental.pallas import tpu as pltpu
from jax.sharding import PartitionSpec as P

D = 768
HEAD = 64
LISTS = 2
OUTER = 4
CHUNK = 256

SCORE_SCALE = HEAD ** (-0.5) * 1.4426950408889634
epsilon = 1e-06
score_scale = 32.0
MIB = 1024 * 1024
SHORT = pl.CostEstimate(flops=1000, bytes_accessed=1000, transcendentals=0)


def inverse_rms(widened):
    return lax.rsqrt(jnp.mean(widened * widened, axis=-1, keepdims=True) + epsilon)


def nt_dot(left, right):
    return lax.dot_general(
        left, right, (((1,), (1,)), ((), ())), preferred_element_type=jnp.float32
    )


LANES = 128


def pack_kernel(expand, contract, packed, done):
    copies = [
        pltpu.make_async_copy(expand.at[which], packed.at[which], done.at[which])
        for which in range(2)
    ]
    for piece in range(D // LANES):
        columns = slice(piece * LANES, (piece + 1) * LANES)
        source, target = contract.at[:, columns], packed.at[2, columns, :]
        copies.append(pltpu.make_async_copy(source, target, done.at[2 + piece]))
    for copy in copies:
        copy.start()
    for copy in copies:
        copy.wait()


def pack_weights(expand_weight, contract_weight):
    in_place = pl.BlockSpec(memory_space=pltpu.HBM)
    return pl.pallas_call(
        pack_kernel,
        out_shape=jax.ShapeDtypeStruct((3, D, LANES), jnp.bfloat16),
        in_specs=[in_place, in_place],
        out_specs=pl.BlockSpec(memory_space=pltpu.VMEM),
        scratch_shapes=[pltpu.SemaphoreType.DMA((2 + D // LANES,))],
        compiler_params=pltpu.CompilerParams(vmem_limit_bytes=60 * MIB),
        name="pack_weights",
    )(expand_weight, contract_weight)


def row_tile(rows):
    return 256 if rows % 256 == 0 else rows


def live_tiles(items, lengths, tile):
    total = lengths[0]
    for item in range(1, items):
        total = total + lengths[item]
    return (total + tile - 1) // tile


def tile_rows(index, tile):
    return pl.ds(pl.multiple_of(index * tile, tile), tile)


def project_kernel(items, lengths, tokens, gains, weights, out):
    tile = row_tile(tokens.shape[0])

    def body(index, carry):
        here = tile_rows(index, tile)
        widened = tokens[here, :].astype(jnp.float32)
        x = (widened * inverse_rms(widened) * gains[0:1, :]).astype(jnp.bfloat16)
        for which in range(3):
            span = slice(which * D, (which + 1) * D)
            part = jnp.dot(x, weights[:, span], preferred_element_type=jnp.float32)
            if which == 0:
                part = part * SCORE_SCALE
            out[here, span] = part.astype(jnp.bfloat16)
        return carry

    lax.fori_loop(0, live_tiles(items, lengths, tile), body, 0)


def call(kernel, name, scalars, arrays, out_shape, scratch=()):
    whole = pl.BlockSpec(memory_space=pltpu.VMEM)
    return pl.pallas_call(
        functools.partial(kernel, scalars[0].shape[0]),
        in_specs=[pl.BlockSpec(memory_space=pltpu.SMEM)] * len(scalars) + [whole] * len(arrays),
        out_specs=jax.tree.map(lambda _: whole, out_shape),
        out_shape=out_shape,
        compiler_params=pltpu.CompilerParams(vmem_limit_bytes=24 * MIB),
        scratch_shapes=scratch,
        cost_estimate=SHORT,
        name=name,
    )(*scalars, *arrays)


def project(lengths, tokens, norm_gains, query_key_value):
    out = jax.ShapeDtypeStruct((tokens.shape[0], 3 * D), jnp.bfloat16)
    return call(project_kernel, "project", (lengths,), (tokens, norm_gains, query_key_value), out)


def heads_kernel(items, lengths, projected, mixed_heads):
    rows = projected.shape[0]
    tile = row_tile(rows)
    wide = 2 * HEAD
    group = D // 2
    lane = lax.broadcasted_iota(jnp.int32, (1, wide), 1) // HEAD
    ends = []
    end = 0
    for item in range(items):
        end = end + lengths[item]
        ends.append(end)
    tiles = (end + tile - 1) // tile

    def segment(position):
        return sum((position >= end).astype(jnp.int32) for end in ends)

    for keys in range(tile, rows + 1, tile):
        across = segment(lax.broadcasted_iota(jnp.int32, (1, keys), 1))

        def body(index, carry):
            row = index // 2
            here = tile_rows(row, tile)
            offset = pl.multiple_of(index % 2 * group, group)
            down = segment(row * tile + lax.broadcasted_iota(jnp.int32, (tile, 1), 0))
            same = down == across

            def columns(kind, head):
                return pl.ds(kind * D + offset + head // 2 * wide, wide)

            def scores(head):
                q = projected[here, columns(0, head)]
                q = jnp.where(lane == head % 2, q, jnp.bfloat16(0))
                return nt_dot(q, projected[:keys, columns(1, head)])

            count = group // HEAD
            ahead = scores(0)
            for head in range(count):
                logits = jnp.where(same, ahead, -1e30)
                if head + 1 < count:
                    ahead = scores(head + 1)
                highest = jnp.max(logits, axis=1, keepdims=True)
                weights = jnp.exp2((logits - highest).astype(jnp.bfloat16))
                mine = lane == head % 2
                v = jnp.where(mine, projected[:keys, columns(2, head)], jnp.bfloat16(1))
                out = jnp.dot(weights, v, preferred_element_type=jnp.float32)
                other = (1 - head % 2) * HEAD
                out = out * (1.0 / out[:, other : other + 1])
                mixed = out if head % 2 == 0 else jnp.where(mine, out, mixed)
                if head % 2 == 1:
                    mixed_heads[here, columns(0, head)] = mixed.astype(jnp.bfloat16)
            return carry

        count = keys // tile
        lax.fori_loop(0, jnp.where(tiles == count, 2 * count, 0), body, 0)


def heads(lengths, projected):
    out = jax.ShapeDtypeStruct((projected.shape[0], D), jnp.bfloat16)
    return call(heads_kernel, "heads", (lengths,), (projected,), out)


def join_kernel(items, lengths, tokens, gains, wo, mixed_heads, residual, normed):
    tile = row_tile(tokens.shape[0])

    def body(index, carry):
        here = tile_rows(index, tile)
        total = tokens[here, :].astype(jnp.float32)
        total += jnp.dot(mixed_heads[here, :], wo[...], preferred_element_type=jnp.float32)
        rounded = total.astype(jnp.bfloat16)
        residual[here, :] = rounded
        widened = rounded.astype(jnp.float32)
        normed[here, :] = (widened * inverse_rms(widened) * gains[1:2, :]).astype(jnp.bfloat16)
        return carry

    lax.fori_loop(0, live_tiles(items, lengths, tile), body, 0)


def join_heads(lengths, *arrays):
    rows = jax.ShapeDtypeStruct(arrays[0].shape, jnp.bfloat16)
    return call(join_kernel, "join_heads", (lengths,), arrays, (rows, rows))


def grow(block_group, which):
    return jnp.concatenate([block[which] for block in block_group], axis=1)


def shrink(block_group):
    rows = []
    for block in block_group:
        pieces = [block[2, i : i + LANES, :] for i in range(0, D, LANES)]
        rows.append(jnp.concatenate(pieces, axis=1))
    return jnp.concatenate(rows, axis=0)


def hidden_units(here, blocks):
    each = CHUNK // LANES
    grown = None
    for start in range(0, len(blocks), each):
        group = blocks[start : start + each]
        gate = jnp.dot(here, grow(group, 0), preferred_element_type=jnp.float32)
        up = jnp.dot(here, grow(group, 1), preferred_element_type=jnp.float32)
        active = (jax.nn.gelu(gate, approximate=True) * up).astype(jnp.bfloat16)
        term = jnp.dot(active, shrink(group), preferred_element_type=jnp.float32)
        grown = term if grown is None else grown + term
    return grown


def all_tiles(tiles, every, tile, one_tile):
    def body(index, carry):
        one_tile(tile_rows(index, tile))
        return carry

    lax.fori_loop(0, jnp.where(tiles == every, 0, tiles), body, 0)

    @pl.when(tiles == every)
    def _():
        for index in range(every):
            one_tile(slice(index * tile, (index + 1) * tile))


def first_kernel(items, lengths, x, *refs):
    blocks, total = refs[:-1], refs[-1]
    tile = row_tile(x.shape[0])

    def one_tile(span):
        total[span, :] = hidden_units(x[span, :], blocks)

    all_tiles(live_tiles(items, lengths, tile), x.shape[0] // tile, tile, one_tile)


def first_units(lengths, normed, blocks):
    out = jax.ShapeDtypeStruct(normed.shape, jnp.float32)
    return call(first_kernel, "first_units", (lengths,), (normed, *blocks), out)


def last_kernel(items, lengths, their_lengths, normed, their_normed, own, theirs, *refs):
    blocks, (own_total, their_total) = refs[:-2], refs[-2:]
    tile = row_tile(normed.shape[0])
    every = normed.shape[0] // tile
    tiles = live_tiles(items, lengths, tile)
    their_tiles = live_tiles(items, their_lengths, tile)

    def one_tile(span):
        grown = theirs[span, :] + hidden_units(their_normed[span, :], blocks)
        their_total[span, :] = grown.astype(jnp.bfloat16)

    all_tiles(their_tiles, every, tile, one_tile)

    def own_tile(span):
        own_total[span, :] = own[span, :] + hidden_units(normed[span, :], blocks)

    all_tiles(jnp.where(tiles > their_tiles, tiles, 0), every, tile, own_tile)


def last_units(lengths, their_lengths, normed, their_normed, own, theirs, blocks):
    out = (
        jax.ShapeDtypeStruct(normed.shape, jnp.float32),
        jax.ShapeDtypeStruct(normed.shape, jnp.bfloat16),
    )
    arrays = (normed, their_normed, own, theirs, *blocks)
    return call(last_kernel, "last_units", (lengths, their_lengths), arrays, out)


def pool_kernel(
    items, lengths, their_lengths, gains, residual, pool, normed, own, own_total, back, *refs
):
    blocks, (vectors, candidates), total = refs[:-3], refs[-3:-1], refs[-1]
    tile = row_tile(residual.shape[0])
    tiles = live_tiles(items, lengths, tile)
    done = tiles > live_tiles(items, their_lengths, tile)
    slots = 16
    slot = lax.broadcasted_iota(jnp.int32, (slots, 1), 0)
    first = jnp.zeros((slots, 1), jnp.int32)
    last = jnp.zeros((slots, 1), jnp.int32)
    begin = 0
    for item in range(items):
        end = begin + lengths[item]
        first = jnp.where(slot == item, begin, first)
        last = jnp.where(slot == item, end, last)
        begin = end

    def body(index, summed):
        here = tile_rows(index, tile)

        @pl.when(done)
        def _():
            total[...] = own_total[here, :]

        @pl.when(jnp.logical_not(done))
        def _():
            total[...] = own[here, :] + hidden_units(normed[here, :], blocks)

        finished = residual[here, :].astype(jnp.float32) + total[...]
        finished += back[here, :].astype(jnp.float32)
        finished = finished.astype(jnp.bfloat16).astype(jnp.float32)
        final_rows = (finished * inverse_rms(finished) * gains[2:3, :]).astype(jnp.bfloat16)
        across = index * tile + lax.broadcasted_iota(jnp.int32, (slots, tile), 1)
        member = jnp.where((across >= first) & (across < last), 1.0, 0.0)
        return summed + jnp.dot(
            member.astype(jnp.bfloat16), final_rows, preferred_element_type=jnp.float32
        )

    summed = lax.fori_loop(0, tiles, body, jnp.zeros((slots, D), jnp.float32))
    counts = jnp.maximum(last - first, 1).astype(jnp.float32)
    pooled = (summed / counts).astype(jnp.bfloat16)
    e = jnp.dot(pooled, pool[...], preferred_element_type=jnp.float32)
    e = e * inverse_rms(e)
    vectors[...] = e[:items, :]
    mine = e[:items, :].astype(jnp.bfloat16)
    for device in range(candidates.shape[0]):
        candidates[device] = mine


def pool_items(devices, lengths, their_lengths, *arrays):
    items = lengths.shape[0]
    out = (
        jax.ShapeDtypeStruct((items, D), jnp.float32),
        jax.ShapeDtypeStruct((devices, items, D), jnp.bfloat16),
    )
    tile = row_tile(arrays[1].shape[0])
    scratch = [pltpu.VMEM((tile, D), jnp.float32)]
    return call(pool_kernel, "pool_items", (lengths, their_lengths), arrays, out, scratch)


def loss_kernel(queries, list_ids, labels, candidates, loss):
    widened = queries[...].astype(jnp.float32)
    query_unit = (widened * inverse_rms(widened)).astype(jnp.bfloat16)
    each = labels.shape[0]
    chosen = None
    for which in range(LISTS):
        scores = nt_dot(candidates[which * each : (which + 1) * each, :], query_unit)
        if chosen is None:
            chosen = scores
        else:
            chosen = jnp.where(list_ids[...] == which, scores, chosen)
    chosen = chosen * (score_scale / D)
    target = jnp.exp(labels[...].astype(jnp.float32))
    target = target / jnp.sum(target, axis=0, keepdims=True)
    log_total = jnp.log(jnp.sum(jnp.exp(chosen), axis=0, keepdims=True))
    loss[...] = log_total - jnp.sum(target * chosen, axis=0, keepdims=True)


def list_loss(queries, list_ids, labels, candidates):
    count = queries.shape[0]
    return pl.pallas_call(
        loss_kernel,
        out_shape=jax.ShapeDtypeStruct((1, count), jnp.float32),
        compiler_params=pltpu.CompilerParams(vmem_limit_bytes=16 * MIB),
        name="list_loss",
    )(queries, list_ids.reshape(1, count), labels.T, candidates).reshape(count)


def swapped(value, count, bit):
    return lax.ppermute(value, "dp", [(i, i ^ bit) for i in range(count)])


def after(value, *earlier):
    return lax.optimization_barrier((value, earlier))[0]


def local(
    count,
    planes,
    tokens,
    lengths,
    norm_gains,
    query_key_value,
    attention_out,
    expand_weight,
    contract_weight,
    pool_weight,
    queries,
    list_ids,
    labels,
):
    inner = count // OUTER
    their_lengths = swapped(lengths, count, 1)

    def attend(turn):
        projected = turn(0, project(lengths, tokens, norm_gains, query_key_value))
        mixed_heads = heads(lengths, projected)
        residual, normed = join_heads(lengths, tokens, norm_gains, attention_out, mixed_heads)
        return residual, turn(1, normed), swapped(normed, count, 1)

    same_core = [list(range(first, count, 2)) for first in range(2)]
    if planes == 2 and inner == 4 and contract_weight.shape[0] == LANES:

        def hop(value, same, across, crossed):
            pairs = []
            for here in range(planes * count):
                y, place = divmod(here, count)
                z, x, c = place // inner, place % inner // 2, place % 2
                role = 0 if c == y else 1
                link = across if role else same
                if link == "y":
                    y = 1 - y
                elif link == "x":
                    x = 1 - x
                else:
                    z = (z + (1 if link == "up" else OUTER - 1)) % OUTER
                role = 1 - role if crossed else role
                pairs.append((here, y * count + z * inner + x * 2 + (1 - y if role else y)))
            return lax.ppermute(value, ("groups", "dp"), pairs)

        v = [pack_weights(expand_weight, contract_weight)]
        v.append(hop(v[0], "x", "up", True))

        def turn(number, value):
            if number == 0:
                v[1], value = after((v[1], value))
                v.append(hop(v[1], "up", "down", False))
                v.append(hop(v[1], "y", "up", False))
                v.append(hop(v[1], "x", "y", False))
            else:
                v[2:5], value = after((v[2:5], value))
                v.append(hop(v[2], "up", "y", False))
                v.append(hop(v[2], "x", "x", False))
                v.append(hop(v[2], "y", "down", False))
            return value

        residual, normed, theirs = attend(turn)
        first = tuple(v[:5])
        third = tuple(v[5:8])
        own_sum = first_units(lengths, normed, first)
    else:
        grown = lax.all_gather(
            expand_weight, "dp", axis=2, tiled=True, axis_index_groups=same_core
        )
        shrunk = lax.all_gather(
            contract_weight, "dp", axis=0, tiled=True, axis_index_groups=same_core
        )
        grown = grown.reshape(2, D, -1, LANES).transpose(2, 0, 1, 3)
        shrunk = shrunk.reshape(-1, LANES, D // LANES, LANES).transpose(0, 2, 1, 3)
        v = jnp.concatenate([grown, shrunk.reshape(-1, 1, D, LANES)], axis=1)
        residual, normed, theirs = attend(lambda number, value: value)
        first = tuple(v[:5])
        third = tuple(v[5:])
        own_sum = first_units(lengths, normed, first)

    their_sum = first_units(their_lengths, theirs, first)
    counts = (lengths, their_lengths)
    own_total, their_total = last_units(*counts, normed, theirs, own_sum, their_sum, third)
    back = swapped(their_total, count, 1)
    item_vectors, candidates = pool_items(
        count,
        *counts,
        norm_gains,
        residual,
        pool_weight,
        normed,
        own_sum,
        own_total,
        back,
        *third,
    )
    every = lax.all_to_all(candidates, "dp", 0, 0, tiled=True)
    every = every.reshape(count * lengths.shape[0], D)
    return item_vectors, list_loss(queries, list_ids, labels, every)


def solution(mesh):
    return jax.shard_map(
        functools.partial(local, mesh.shape["dp"], mesh.shape["groups"]),
        mesh=mesh,
        in_specs=(
            P(("groups", "dp"), None),
            P(("groups", "dp")),
            P(),
            P(),
            P(),
            P(None, None, "dp"),
            P("dp", None),
            P(),
            P(("groups", "dp"), None),
            P(("groups", "dp")),
            P(("groups", "dp"), None),
        ),
        out_specs=(P(("groups", "dp"), None), P(("groups", "dp"))),
        check_vma=False,
    )
```

```python
import functools

import jax
import jax.numpy as jnp
from jax import lax
from jax.experimental import pallas as pl
from jax.experimental.pallas import tpu as pltpu
from jax.sharding import PartitionSpec as P

D = 768
HEAD = 64
LISTS = 2
OUTER = 4
CHUNK = 256

SCORE_SCALE = HEAD ** (-0.5) * 1.4426950408889634
epsilon = 1e-06
score_scale = 32.0
MIB = 1024 * 1024
SHORT = pl.CostEstimate(flops=1000, bytes_accessed=1000, transcendentals=0)
LONG = pl.CostEstimate(flops=40_000_000_000, bytes_accessed=1000, transcendentals=0)


def inverse_rms(widened):
    return lax.rsqrt(jnp.mean(widened * widened, axis=-1, keepdims=True) + epsilon)


def nt_dot(left, right):
    return lax.dot_general(
        left, right, (((1,), (1,)), ((), ())), preferred_element_type=jnp.float32
    )


LANES = 128


def pack_kernel(expand, contract, packed, done):
    copies = [
        pltpu.make_async_copy(expand.at[which], packed.at[which], done.at[which])
        for which in range(2)
    ]
    for piece in range(D // LANES):
        columns = slice(piece * LANES, (piece + 1) * LANES)
        source, target = contract.at[:, columns], packed.at[2, columns, :]
        copies.append(pltpu.make_async_copy(source, target, done.at[2 + piece]))
    for copy in copies:
        copy.start()
    for copy in copies:
        copy.wait()


def pack_weights(expand_weight, contract_weight):
    in_place = pl.BlockSpec(memory_space=pltpu.HBM)
    return pl.pallas_call(
        pack_kernel,
        out_shape=jax.ShapeDtypeStruct((3, D, LANES), jnp.bfloat16),
        in_specs=[in_place, in_place],
        out_specs=pl.BlockSpec(memory_space=pltpu.VMEM),
        scratch_shapes=[pltpu.SemaphoreType.DMA((2 + D // LANES,))],
        compiler_params=pltpu.CompilerParams(vmem_limit_bytes=60 * MIB),
        name="pack_weights",
    )(expand_weight, contract_weight)


def row_tile(rows):
    return 256 if rows % 256 == 0 else rows


def live_tiles(items, lengths, tile):
    total = lengths[0]
    for item in range(1, items):
        total = total + lengths[item]
    return (total + tile - 1) // tile


def tile_rows(index, tile):
    return pl.ds(pl.multiple_of(index * tile, tile), tile)


def project_kernel(items, lengths, tokens, gains, weights, out):
    tile = row_tile(tokens.shape[0])

    def body(index, carry):
        here = tile_rows(index, tile)
        widened = tokens[here, :].astype(jnp.float32)
        x = (widened * inverse_rms(widened) * gains[0:1, :]).astype(jnp.bfloat16)
        for which in range(3):
            span = slice(which * D, (which + 1) * D)
            part = jnp.dot(x, weights[:, span], preferred_element_type=jnp.float32)
            if which == 0:
                part = part * SCORE_SCALE
            out[here, span] = part.astype(jnp.bfloat16)
        return carry

    lax.fori_loop(0, live_tiles(items, lengths, tile), body, 0)


def call(kernel, name, scalars, arrays, out_shape, scratch=(), cost=SHORT):
    whole = pl.BlockSpec(memory_space=pltpu.VMEM)
    return pl.pallas_call(
        functools.partial(kernel, scalars[0].shape[0]),
        in_specs=[pl.BlockSpec(memory_space=pltpu.SMEM)] * len(scalars) + [whole] * len(arrays),
        out_specs=jax.tree.map(lambda _: whole, out_shape),
        out_shape=out_shape,
        compiler_params=pltpu.CompilerParams(vmem_limit_bytes=24 * MIB),
        scratch_shapes=scratch,
        cost_estimate=cost,
        name=name,
    )(*scalars, *arrays)


def project(lengths, tokens, norm_gains, query_key_value):
    out = jax.ShapeDtypeStruct((tokens.shape[0], 3 * D), jnp.bfloat16)
    return call(project_kernel, "project", (lengths,), (tokens, norm_gains, query_key_value), out)


def heads_kernel(items, lengths, projected, mixed_heads):
    rows = projected.shape[0]
    tile = row_tile(rows)
    wide = 2 * HEAD
    group = D // 2
    lane = lax.broadcasted_iota(jnp.int32, (1, wide), 1) // HEAD
    ends = []
    end = 0
    for item in range(items):
        end = end + lengths[item]
        ends.append(end)
    tiles = (end + tile - 1) // tile

    def segment(position):
        return sum((position >= end).astype(jnp.int32) for end in ends)

    for keys in range(tile, rows + 1, tile):
        across = segment(lax.broadcasted_iota(jnp.int32, (1, keys), 1))

        def body(index, carry):
            row = index // 2
            here = tile_rows(row, tile)
            offset = pl.multiple_of(index % 2 * group, group)
            down = segment(row * tile + lax.broadcasted_iota(jnp.int32, (tile, 1), 0))
            same = down == across

            def columns(kind, head):
                return pl.ds(kind * D + offset + head // 2 * wide, wide)

            def scores(head):
                q = projected[here, columns(0, head)]
                q = jnp.where(lane == head % 2, q, jnp.bfloat16(0))
                return nt_dot(q, projected[:keys, columns(1, head)])

            count = group // HEAD
            ahead = scores(0)
            for head in range(count):
                logits = jnp.where(same, ahead, -1e30)
                if head + 1 < count:
                    ahead = scores(head + 1)
                highest = jnp.max(logits, axis=1, keepdims=True)
                weights = jnp.exp2((logits - highest).astype(jnp.bfloat16))
                mine = lane == head % 2
                v = jnp.where(mine, projected[:keys, columns(2, head)], jnp.bfloat16(1))
                out = jnp.dot(weights, v, preferred_element_type=jnp.float32)
                other = (1 - head % 2) * HEAD
                out = out * (1.0 / out[:, other : other + 1])
                mixed = out if head % 2 == 0 else jnp.where(mine, out, mixed)
                if head % 2 == 1:
                    mixed_heads[here, columns(0, head)] = mixed.astype(jnp.bfloat16)
            return carry

        count = keys // tile
        lax.fori_loop(0, jnp.where(tiles == count, 2 * count, 0), body, 0)


def heads(lengths, projected):
    out = jax.ShapeDtypeStruct((projected.shape[0], D), jnp.bfloat16)
    return call(heads_kernel, "heads", (lengths,), (projected,), out)


def join_kernel(items, lengths, tokens, gains, wo, mixed_heads, residual, normed):
    tile = row_tile(tokens.shape[0])

    def body(index, carry):
        here = tile_rows(index, tile)
        total = tokens[here, :].astype(jnp.float32)
        total += jnp.dot(mixed_heads[here, :], wo[...], preferred_element_type=jnp.float32)
        rounded = total.astype(jnp.bfloat16)
        residual[here, :] = rounded
        widened = rounded.astype(jnp.float32)
        normed[here, :] = (widened * inverse_rms(widened) * gains[1:2, :]).astype(jnp.bfloat16)
        return carry

    lax.fori_loop(0, live_tiles(items, lengths, tile), body, 0)


def join_heads(lengths, *arrays):
    rows = jax.ShapeDtypeStruct(arrays[0].shape, jnp.bfloat16)
    return call(join_kernel, "join_heads", (lengths,), arrays, (rows, rows))


def grow(block_group, which):
    return jnp.concatenate([block[which] for block in block_group], axis=1)


def shrink(block_group):
    rows = []
    for block in block_group:
        pieces = [block[2, i : i + LANES, :] for i in range(0, D, LANES)]
        rows.append(jnp.concatenate(pieces, axis=1))
    return jnp.concatenate(rows, axis=0)


def hidden_units(here, blocks):
    each = CHUNK // LANES
    grown = None
    for start in range(0, len(blocks), each):
        group = blocks[start : start + each]
        gate = jnp.dot(here, grow(group, 0), preferred_element_type=jnp.float32)
        up = jnp.dot(here, grow(group, 1), preferred_element_type=jnp.float32)
        active = (jax.nn.gelu(gate, approximate=True) * up).astype(jnp.bfloat16)
        term = jnp.dot(active, shrink(group), preferred_element_type=jnp.float32)
        grown = term if grown is None else grown + term
    return grown


def all_tiles(tiles, every, tile, one_tile):
    def body(index, carry):
        one_tile(tile_rows(index, tile))
        return carry

    lax.fori_loop(0, jnp.where(tiles == every, 0, tiles), body, 0)

    @pl.when(tiles == every)
    def _():
        for index in range(every):
            one_tile(slice(index * tile, (index + 1) * tile))


def first_kernel(items, lengths, x, *refs):
    blocks, total = refs[:-1], refs[-1]
    tile = row_tile(x.shape[0])

    def one_tile(span):
        total[span, :] = hidden_units(x[span, :], blocks)

    all_tiles(live_tiles(items, lengths, tile), x.shape[0] // tile, tile, one_tile)


def first_units(lengths, normed, blocks):
    out = jax.ShapeDtypeStruct(normed.shape, jnp.float32)
    return call(first_kernel, "first_units", (lengths,), (normed, *blocks), out, cost=LONG)


def last_kernel(items, lengths, their_lengths, normed, their_normed, own, theirs, *refs):
    blocks, (own_total, their_total) = refs[:-2], refs[-2:]
    tile = row_tile(normed.shape[0])
    every = normed.shape[0] // tile
    tiles = live_tiles(items, lengths, tile)
    their_tiles = live_tiles(items, their_lengths, tile)

    def one_tile(span):
        grown = theirs[span, :] + hidden_units(their_normed[span, :], blocks)
        their_total[span, :] = grown.astype(jnp.bfloat16)

    all_tiles(their_tiles, every, tile, one_tile)

    def own_tile(span):
        own_total[span, :] = own[span, :] + hidden_units(normed[span, :], blocks)

    all_tiles(jnp.where(tiles > their_tiles, tiles, 0), every, tile, own_tile)


def last_units(lengths, their_lengths, normed, their_normed, own, theirs, blocks):
    out = (
        jax.ShapeDtypeStruct(normed.shape, jnp.float32),
        jax.ShapeDtypeStruct(normed.shape, jnp.bfloat16),
    )
    arrays = (normed, their_normed, own, theirs, *blocks)
    return call(last_kernel, "last_units", (lengths, their_lengths), arrays, out)


def pool_kernel(
    items, lengths, their_lengths, gains, residual, pool, normed, own, own_total, back, *refs
):
    blocks, (vectors, candidates), total = refs[:-3], refs[-3:-1], refs[-1]
    tile = row_tile(residual.shape[0])
    tiles = live_tiles(items, lengths, tile)
    done = tiles > live_tiles(items, their_lengths, tile)
    slots = 16
    slot = lax.broadcasted_iota(jnp.int32, (slots, 1), 0)
    first = jnp.zeros((slots, 1), jnp.int32)
    last = jnp.zeros((slots, 1), jnp.int32)
    begin = 0
    for item in range(items):
        end = begin + lengths[item]
        first = jnp.where(slot == item, begin, first)
        last = jnp.where(slot == item, end, last)
        begin = end

    def body(index, summed):
        here = tile_rows(index, tile)

        @pl.when(done)
        def _():
            total[...] = own_total[here, :]

        @pl.when(jnp.logical_not(done))
        def _():
            total[...] = own[here, :] + hidden_units(normed[here, :], blocks)

        finished = residual[here, :].astype(jnp.float32) + total[...]
        finished += back[here, :].astype(jnp.float32)
        finished = finished.astype(jnp.bfloat16).astype(jnp.float32)
        final_rows = (finished * inverse_rms(finished) * gains[2:3, :]).astype(jnp.bfloat16)
        across = index * tile + lax.broadcasted_iota(jnp.int32, (slots, tile), 1)
        member = jnp.where((across >= first) & (across < last), 1.0, 0.0)
        return summed + jnp.dot(
            member.astype(jnp.bfloat16), final_rows, preferred_element_type=jnp.float32
        )

    summed = lax.fori_loop(0, tiles, body, jnp.zeros((slots, D), jnp.float32))
    counts = jnp.maximum(last - first, 1).astype(jnp.float32)
    pooled = (summed / counts).astype(jnp.bfloat16)
    e = jnp.dot(pooled, pool[...], preferred_element_type=jnp.float32)
    e = e * inverse_rms(e)
    vectors[...] = e[:items, :]
    candidates[...] = e[:items, :].astype(jnp.bfloat16)


def pool_items(lengths, their_lengths, *arrays):
    items = lengths.shape[0]
    out = (
        jax.ShapeDtypeStruct((items, D), jnp.float32),
        jax.ShapeDtypeStruct((items, D), jnp.bfloat16),
    )
    tile = row_tile(arrays[1].shape[0])
    scratch = [pltpu.VMEM((tile, D), jnp.float32)]
    return call(pool_kernel, "pool_items", (lengths, their_lengths), arrays, out, scratch)


def loss_kernel(queries, list_ids, labels, candidates, loss):
    widened = queries[...].astype(jnp.float32)
    query_unit = (widened * inverse_rms(widened)).astype(jnp.bfloat16)
    each = labels.shape[0]
    chosen = None
    for which in range(LISTS):
        scores = nt_dot(candidates[which * each : (which + 1) * each, :], query_unit)
        if chosen is None:
            chosen = scores
        else:
            chosen = jnp.where(list_ids[...] == which, scores, chosen)
    chosen = chosen * (score_scale / D)
    target = jnp.exp(labels[...].astype(jnp.float32))
    target = target / jnp.sum(target, axis=0, keepdims=True)
    log_total = jnp.log(jnp.sum(jnp.exp(chosen), axis=0, keepdims=True))
    loss[...] = log_total - jnp.sum(target * chosen, axis=0, keepdims=True)


def list_loss(queries, list_ids, labels, candidates):
    count = queries.shape[0]
    return pl.pallas_call(
        loss_kernel,
        out_shape=jax.ShapeDtypeStruct((1, count), jnp.float32),
        compiler_params=pltpu.CompilerParams(vmem_limit_bytes=16 * MIB),
        name="list_loss",
    )(queries, list_ids.reshape(1, count), labels.T, candidates).reshape(count)


def swapped(value, count, bit):
    return lax.ppermute(value, "dp", [(i, i ^ bit) for i in range(count)])


def after(value, *earlier):
    return lax.optimization_barrier((value, earlier))[0]


def local(
    count,
    planes,
    tokens,
    lengths,
    norm_gains,
    query_key_value,
    attention_out,
    expand_weight,
    contract_weight,
    pool_weight,
    queries,
    list_ids,
    labels,
):
    inner = count // OUTER
    their_lengths = swapped(lengths, count, 1)

    def attend(turn):
        projected = turn(0, project(lengths, tokens, norm_gains, query_key_value))
        mixed_heads = heads(lengths, projected)
        residual, normed = join_heads(lengths, tokens, norm_gains, attention_out, mixed_heads)
        return residual, turn(1, normed), swapped(normed, count, 1)

    same_core = [list(range(first, count, 2)) for first in range(2)]
    if planes == 2 and inner == 4 and contract_weight.shape[0] == LANES:

        def hop(value, same, across, crossed):
            pairs = []
            for here in range(planes * count):
                y, place = divmod(here, count)
                z, x, c = place // inner, place % inner // 2, place % 2
                role = 0 if c == y else 1
                link = across if role else same
                if link == "y":
                    y = 1 - y
                elif link == "x":
                    x = 1 - x
                else:
                    z = (z + (1 if link == "up" else OUTER - 1)) % OUTER
                role = 1 - role if crossed else role
                pairs.append((here, y * count + z * inner + x * 2 + (1 - y if role else y)))
            return lax.ppermute(value, ("groups", "dp"), pairs)

        v = [pack_weights(expand_weight, contract_weight)]
        v.append(hop(v[0], "x", "up", True))

        def turn(number, value):
            if number == 0:
                v[1], value = after((v[1], value))
                v.append(hop(v[1], "up", "down", False))
                v.append(hop(v[1], "y", "up", False))
                v.append(hop(v[1], "x", "y", False))
            else:
                v[2], value = after((v[2], value))
                v.append(hop(v[2], "up", "y", False))
                v.append(hop(v[2], "x", "x", False))
                v.append(hop(v[2], "y", "down", False))
            return value

        residual, normed, theirs = attend(turn)
        first = tuple(v[:5])
        third = tuple(v[5:8])
        own_sum = first_units(lengths, normed, first)
    else:
        grown = lax.all_gather(
            expand_weight, "dp", axis=2, tiled=True, axis_index_groups=same_core
        )
        shrunk = lax.all_gather(
            contract_weight, "dp", axis=0, tiled=True, axis_index_groups=same_core
        )
        grown = grown.reshape(2, D, -1, LANES).transpose(2, 0, 1, 3)
        shrunk = shrunk.reshape(-1, LANES, D // LANES, LANES).transpose(0, 2, 1, 3)
        v = jnp.concatenate([grown, shrunk.reshape(-1, 1, D, LANES)], axis=1)
        residual, normed, theirs = attend(lambda number, value: value)
        first = tuple(v[:5])
        third = tuple(v[5:])
        own_sum = first_units(lengths, normed, first)

    their_sum = first_units(their_lengths, theirs, first)
    counts = (lengths, their_lengths)
    own_total, their_total = last_units(*counts, normed, theirs, own_sum, their_sum, third)
    back = swapped(their_total, count, 1)
    item_vectors, candidates = pool_items(
        *counts,
        norm_gains,
        residual,
        pool_weight,
        normed,
        own_sum,
        own_total,
        back,
        *third,
    )
    upper = lax.axis_index("dp") % 2 == 1
    other = swapped(candidates, count, 1)
    chip = jnp.concatenate(
        [jnp.where(upper, other, candidates), jnp.where(upper, candidates, other)], axis=0
    )
    every = lax.all_to_all(
        jnp.broadcast_to(chip, (count // 2, *chip.shape)),
        "dp",
        0,
        0,
        axis_index_groups=same_core,
        tiled=True,
    )
    every = every.reshape(count * lengths.shape[0], D)
    return item_vectors, list_loss(queries, list_ids, labels, every)


def solution(mesh):
    return jax.shard_map(
        functools.partial(local, mesh.shape["dp"], mesh.shape["groups"]),
        mesh=mesh,
        in_specs=(
            P(("groups", "dp"), None),
            P(("groups", "dp")),
            P(),
            P(),
            P(),
            P(None, None, "dp"),
            P("dp", None),
            P(),
            P(("groups", "dp"), None),
            P(("groups", "dp")),
            P(("groups", "dp"), None),
        ),
        out_specs=(P(("groups", "dp"), None), P(("groups", "dp"))),
        check_vma=False,
    )
```

```python
import functools

import jax
import jax.numpy as jnp
from jax import lax
from jax.experimental import pallas as pl
from jax.experimental.pallas import tpu as pltpu
from jax.sharding import PartitionSpec as P

D = 768
HEAD = 64
LISTS = 2
OUTER = 4
CHUNK = 256

SCORE_SCALE = HEAD ** (-0.5) * 1.4426950408889634
epsilon = 1e-06
score_scale = 32.0
MIB = 1024 * 1024
SHORT = pl.CostEstimate(flops=1000, bytes_accessed=1000, transcendentals=0)
LONG = pl.CostEstimate(flops=40_000_000_000, bytes_accessed=1000, transcendentals=0)


def inverse_rms(widened):
    return lax.rsqrt(jnp.mean(widened * widened, axis=-1, keepdims=True) + epsilon)


def nt_dot(left, right):
    return lax.dot_general(
        left, right, (((1,), (1,)), ((), ())), preferred_element_type=jnp.float32
    )


LANES = 128


def pack_kernel(expand, contract, packed, done):
    copies = [
        pltpu.make_async_copy(expand.at[which], packed.at[which], done.at[which])
        for which in range(2)
    ]
    for piece in range(D // LANES):
        columns = slice(piece * LANES, (piece + 1) * LANES)
        source, target = contract.at[:, columns], packed.at[2, columns, :]
        copies.append(pltpu.make_async_copy(source, target, done.at[2 + piece]))
    for copy in copies:
        copy.start()
    for copy in copies:
        copy.wait()


def pack_weights(expand_weight, contract_weight):
    in_place = pl.BlockSpec(memory_space=pltpu.HBM)
    return pl.pallas_call(
        pack_kernel,
        out_shape=jax.ShapeDtypeStruct((3, D, LANES), jnp.bfloat16),
        in_specs=[in_place, in_place],
        out_specs=pl.BlockSpec(memory_space=pltpu.VMEM),
        scratch_shapes=[pltpu.SemaphoreType.DMA((2 + D // LANES,))],
        compiler_params=pltpu.CompilerParams(vmem_limit_bytes=60 * MIB),
        name="pack_weights",
    )(expand_weight, contract_weight)


def row_tile(rows):
    return 256 if rows % 256 == 0 else rows


def live_tiles(items, lengths, tile):
    total = lengths[0]
    for item in range(1, items):
        total = total + lengths[item]
    return (total + tile - 1) // tile


def tile_rows(index, tile):
    return pl.ds(pl.multiple_of(index * tile, tile), tile)


def project_kernel(items, lengths, tokens, gains, weights, out):
    tile = row_tile(tokens.shape[0])

    def body(index, carry):
        here = tile_rows(index, tile)
        widened = tokens[here, :].astype(jnp.float32)
        x = (widened * inverse_rms(widened) * gains[0:1, :]).astype(jnp.bfloat16)
        for which in range(3):
            span = slice(which * D, (which + 1) * D)
            part = jnp.dot(x, weights[:, span], preferred_element_type=jnp.float32)
            if which == 0:
                part = part * SCORE_SCALE
            out[here, span] = part.astype(jnp.bfloat16)
        return carry

    lax.fori_loop(0, live_tiles(items, lengths, tile), body, 0)


def call(kernel, name, scalars, arrays, out_shape, scratch=(), cost=SHORT):
    whole = pl.BlockSpec(memory_space=pltpu.VMEM)
    return pl.pallas_call(
        functools.partial(kernel, scalars[0].shape[0]),
        in_specs=[pl.BlockSpec(memory_space=pltpu.SMEM)] * len(scalars) + [whole] * len(arrays),
        out_specs=jax.tree.map(lambda _: whole, out_shape),
        out_shape=out_shape,
        compiler_params=pltpu.CompilerParams(vmem_limit_bytes=24 * MIB),
        scratch_shapes=scratch,
        cost_estimate=cost,
        name=name,
    )(*scalars, *arrays)


def project(lengths, tokens, norm_gains, query_key_value):
    out = jax.ShapeDtypeStruct((tokens.shape[0], 3 * D), jnp.bfloat16)
    return call(project_kernel, "project", (lengths,), (tokens, norm_gains, query_key_value), out)


def heads_kernel(items, lengths, projected, mixed_heads):
    rows = projected.shape[0]
    tile = row_tile(rows)
    wide = 2 * HEAD
    group = D // 2
    lane = lax.broadcasted_iota(jnp.int32, (1, wide), 1) // HEAD
    ends = []
    end = 0
    for item in range(items):
        end = end + lengths[item]
        ends.append(end)
    tiles = (end + tile - 1) // tile

    def segment(position):
        return sum((position >= end).astype(jnp.int32) for end in ends)

    for keys in range(tile, rows + 1, tile):
        across = segment(lax.broadcasted_iota(jnp.int32, (1, keys), 1))

        def body(index, carry):
            row = index // 2
            here = tile_rows(row, tile)
            offset = pl.multiple_of(index % 2 * group, group)
            down = segment(row * tile + lax.broadcasted_iota(jnp.int32, (tile, 1), 0))
            same = down == across

            def columns(kind, head):
                return pl.ds(kind * D + offset + head // 2 * wide, wide)

            def scores(head):
                q = projected[here, columns(0, head)]
                q = jnp.where(lane == head % 2, q, jnp.bfloat16(0))
                return nt_dot(q, projected[:keys, columns(1, head)])

            count = group // HEAD
            ahead = scores(0)
            for head in range(count):
                logits = jnp.where(same, ahead, -1e30)
                if head + 1 < count:
                    ahead = scores(head + 1)
                highest = jnp.max(logits, axis=1, keepdims=True)
                weights = jnp.exp2((logits - highest).astype(jnp.bfloat16))
                mine = lane == head % 2
                v = jnp.where(mine, projected[:keys, columns(2, head)], jnp.bfloat16(1))
                out = jnp.dot(weights, v, preferred_element_type=jnp.float32)
                other = (1 - head % 2) * HEAD
                out = out * (1.0 / out[:, other : other + 1])
                mixed = out if head % 2 == 0 else jnp.where(mine, out, mixed)
                if head % 2 == 1:
                    mixed_heads[here, columns(0, head)] = mixed.astype(jnp.bfloat16)
            return carry

        count = keys // tile
        lax.fori_loop(0, jnp.where(tiles == count, 2 * count, 0), body, 0)


def heads(lengths, projected):
    out = jax.ShapeDtypeStruct((projected.shape[0], D), jnp.bfloat16)
    return call(heads_kernel, "heads", (lengths,), (projected,), out)


def join_kernel(items, lengths, tokens, gains, wo, mixed_heads, residual, normed):
    tile = row_tile(tokens.shape[0])

    def body(index, carry):
        here = tile_rows(index, tile)
        total = tokens[here, :].astype(jnp.float32)
        total += jnp.dot(mixed_heads[here, :], wo[...], preferred_element_type=jnp.float32)
        rounded = total.astype(jnp.bfloat16)
        residual[here, :] = rounded
        widened = rounded.astype(jnp.float32)
        normed[here, :] = (widened * inverse_rms(widened) * gains[1:2, :]).astype(jnp.bfloat16)
        return carry

    lax.fori_loop(0, live_tiles(items, lengths, tile), body, 0)


def join_heads(lengths, *arrays):
    rows = jax.ShapeDtypeStruct(arrays[0].shape, jnp.bfloat16)
    return call(join_kernel, "join_heads", (lengths,), arrays, (rows, rows))


def grow(block_group, which):
    return jnp.concatenate([block[which] for block in block_group], axis=1)


def shrink(block_group):
    rows = []
    for block in block_group:
        pieces = [block[2, i : i + LANES, :] for i in range(0, D, LANES)]
        rows.append(jnp.concatenate(pieces, axis=1))
    return jnp.concatenate(rows, axis=0)


def hidden_units(here, blocks):
    each = CHUNK // LANES
    grown = None
    for start in range(0, len(blocks), each):
        group = blocks[start : start + each]
        gate = jnp.dot(here, grow(group, 0), preferred_element_type=jnp.float32)
        up = jnp.dot(here, grow(group, 1), preferred_element_type=jnp.float32)
        active = (jax.nn.gelu(gate, approximate=True) * up).astype(jnp.bfloat16)
        term = jnp.dot(active, shrink(group), preferred_element_type=jnp.float32)
        grown = term if grown is None else grown + term
    return grown


def all_tiles(tiles, every, tile, one_tile):
    def body(index, carry):
        one_tile(tile_rows(index, tile))
        return carry

    lax.fori_loop(0, jnp.where(tiles == every, 0, tiles), body, 0)

    @pl.when(tiles == every)
    def _():
        for index in range(every):
            one_tile(slice(index * tile, (index + 1) * tile))


def first_kernel(items, lengths, x, *refs):
    blocks, total = refs[:-1], refs[-1]
    tile = row_tile(x.shape[0])

    def one_tile(span):
        total[span, :] = hidden_units(x[span, :], blocks)

    all_tiles(live_tiles(items, lengths, tile), x.shape[0] // tile, tile, one_tile)


def first_units(lengths, normed, blocks):
    out = jax.ShapeDtypeStruct(normed.shape, jnp.float32)
    return call(first_kernel, "first_units", (lengths,), (normed, *blocks), out, cost=LONG)


def more_kernel(items, lengths, their_lengths, *refs):
    sides, blocks, totals = refs[:4], refs[4:-2], refs[-2:]
    tile = row_tile(sides[0].shape[0])
    every = sides[0].shape[0] // tile
    for side, counts in enumerate((lengths, their_lengths)):
        rows, before, total = sides[side], sides[2 + side], totals[side]

        def one_tile(span):
            total[span, :] = before[span, :] + hidden_units(rows[span, :], blocks)

        all_tiles(live_tiles(items, counts, tile), every, tile, one_tile)


def more_units(lengths, their_lengths, normed, their_normed, own, theirs, blocks):
    total = jax.ShapeDtypeStruct(normed.shape, jnp.float32)
    arrays = (normed, their_normed, own, theirs, *blocks)
    return call(more_kernel, "more_units", (lengths, their_lengths), arrays, (total, total))


def last_kernel(items, lengths, their_lengths, normed, their_normed, own, theirs, *refs):
    blocks, (own_total, their_total) = refs[:-2], refs[-2:]
    tile = row_tile(normed.shape[0])
    every = normed.shape[0] // tile
    tiles = live_tiles(items, lengths, tile)
    their_tiles = live_tiles(items, their_lengths, tile)

    def one_tile(span):
        grown = theirs[span, :] + hidden_units(their_normed[span, :], blocks)
        their_total[span, :] = grown.astype(jnp.bfloat16)

    all_tiles(their_tiles, every, tile, one_tile)

    def own_tile(span):
        own_total[span, :] = own[span, :] + hidden_units(normed[span, :], blocks)

    all_tiles(jnp.where(tiles > their_tiles, tiles, 0), every, tile, own_tile)


def last_units(lengths, their_lengths, normed, their_normed, own, theirs, blocks):
    out = (
        jax.ShapeDtypeStruct(normed.shape, jnp.float32),
        jax.ShapeDtypeStruct(normed.shape, jnp.bfloat16),
    )
    arrays = (normed, their_normed, own, theirs, *blocks)
    return call(last_kernel, "last_units", (lengths, their_lengths), arrays, out)


def pool_kernel(
    items, lengths, their_lengths, gains, residual, pool, normed, own, own_total, back, *refs
):
    blocks, (vectors, candidates), total = refs[:-3], refs[-3:-1], refs[-1]
    tile = row_tile(residual.shape[0])
    tiles = live_tiles(items, lengths, tile)
    done = tiles > live_tiles(items, their_lengths, tile)
    slots = 16
    slot = lax.broadcasted_iota(jnp.int32, (slots, 1), 0)
    first = jnp.zeros((slots, 1), jnp.int32)
    last = jnp.zeros((slots, 1), jnp.int32)
    begin = 0
    for item in range(items):
        end = begin + lengths[item]
        first = jnp.where(slot == item, begin, first)
        last = jnp.where(slot == item, end, last)
        begin = end

    def body(index, summed):
        here = tile_rows(index, tile)

        @pl.when(done)
        def _():
            total[...] = own_total[here, :]

        @pl.when(jnp.logical_not(done))
        def _():
            total[...] = own[here, :] + hidden_units(normed[here, :], blocks)

        finished = residual[here, :].astype(jnp.float32) + total[...]
        finished += back[here, :].astype(jnp.float32)
        finished = finished.astype(jnp.bfloat16).astype(jnp.float32)
        final_rows = (finished * inverse_rms(finished) * gains[2:3, :]).astype(jnp.bfloat16)
        across = index * tile + lax.broadcasted_iota(jnp.int32, (slots, tile), 1)
        member = jnp.where((across >= first) & (across < last), 1.0, 0.0)
        return summed + jnp.dot(
            member.astype(jnp.bfloat16), final_rows, preferred_element_type=jnp.float32
        )

    summed = lax.fori_loop(0, tiles, body, jnp.zeros((slots, D), jnp.float32))
    counts = jnp.maximum(last - first, 1).astype(jnp.float32)
    pooled = (summed / counts).astype(jnp.bfloat16)
    e = jnp.dot(pooled, pool[...], preferred_element_type=jnp.float32)
    e = e * inverse_rms(e)
    vectors[...] = e[:items, :]
    mine = e[:items, :].astype(jnp.bfloat16)
    for device in range(candidates.shape[0]):
        candidates[device] = mine


def pool_items(devices, lengths, their_lengths, *arrays):
    items = lengths.shape[0]
    out = (
        jax.ShapeDtypeStruct((items, D), jnp.float32),
        jax.ShapeDtypeStruct((devices, items, D), jnp.bfloat16),
    )
    tile = row_tile(arrays[1].shape[0])
    scratch = [pltpu.VMEM((tile, D), jnp.float32)]
    return call(pool_kernel, "pool_items", (lengths, their_lengths), arrays, out, scratch)


def loss_kernel(queries, list_ids, labels, candidates, loss):
    widened = queries[...].astype(jnp.float32)
    query_unit = (widened * inverse_rms(widened)).astype(jnp.bfloat16)
    each = labels.shape[0]
    chosen = None
    for which in range(LISTS):
        scores = nt_dot(candidates[which * each : (which + 1) * each, :], query_unit)
        if chosen is None:
            chosen = scores
        else:
            chosen = jnp.where(list_ids[...] == which, scores, chosen)
    chosen = chosen * (score_scale / D)
    target = jnp.exp(labels[...].astype(jnp.float32))
    target = target / jnp.sum(target, axis=0, keepdims=True)
    log_total = jnp.log(jnp.sum(jnp.exp(chosen), axis=0, keepdims=True))
    loss[...] = log_total - jnp.sum(target * chosen, axis=0, keepdims=True)


def list_loss(queries, list_ids, labels, candidates):
    count = queries.shape[0]
    return pl.pallas_call(
        loss_kernel,
        out_shape=jax.ShapeDtypeStruct((1, count), jnp.float32),
        compiler_params=pltpu.CompilerParams(vmem_limit_bytes=16 * MIB),
        name="list_loss",
    )(queries, list_ids.reshape(1, count), labels.T, candidates).reshape(count)


def swapped(value, count, bit):
    return lax.ppermute(value, "dp", [(i, i ^ bit) for i in range(count)])


def after(value, *earlier):
    return lax.optimization_barrier((value, earlier))[0]


def local(
    count,
    planes,
    tokens,
    lengths,
    norm_gains,
    query_key_value,
    attention_out,
    expand_weight,
    contract_weight,
    pool_weight,
    queries,
    list_ids,
    labels,
):
    inner = count // OUTER
    their_lengths = swapped(lengths, count, 1)

    def attend(turn):
        projected = turn(0, project(lengths, tokens, norm_gains, query_key_value))
        mixed_heads = heads(lengths, projected)
        residual, normed = join_heads(lengths, tokens, norm_gains, attention_out, mixed_heads)
        return residual, turn(1, normed), swapped(normed, count, 1)

    same_core = [list(range(first, count, 2)) for first in range(2)]
    if planes == 2 and inner == 4 and contract_weight.shape[0] == LANES:

        def hop(value, same, across, crossed):
            pairs = []
            for here in range(planes * count):
                y, place = divmod(here, count)
                z, x, c = place // inner, place % inner // 2, place % 2
                role = 0 if c == y else 1
                link = across if role else same
                if link == "y":
                    y = 1 - y
                elif link == "x":
                    x = 1 - x
                else:
                    z = (z + (1 if link == "up" else OUTER - 1)) % OUTER
                role = 1 - role if crossed else role
                pairs.append((here, y * count + z * inner + x * 2 + (1 - y if role else y)))
            return lax.ppermute(value, ("groups", "dp"), pairs)

        v = [pack_weights(expand_weight, contract_weight)]
        v.append(hop(v[0], "x", "up", True))

        def turn(number, value):
            if number == 0:
                v[1], value = after((v[1], value))
                v.append(hop(v[1], "up", "down", False))
                v.append(hop(v[1], "x", "y", False))
                v.append(hop(v[1], "y", "up", False))
            else:
                v[2], value = after((v[2], value))
                v.append(hop(v[2], "up", "y", False))
                v.append(hop(v[2], "x", "x", False))
            return value

        residual, normed, theirs = attend(turn)
        own_sum = first_units(lengths, normed, v[:4])
        v[2] = after(v[2], own_sum)
        v.append(hop(v[2], "y", "down", False))
    else:
        grown = lax.all_gather(
            expand_weight, "dp", axis=2, tiled=True, axis_index_groups=same_core
        )
        shrunk = lax.all_gather(
            contract_weight, "dp", axis=0, tiled=True, axis_index_groups=same_core
        )
        grown = grown.reshape(2, D, -1, LANES).transpose(2, 0, 1, 3)
        shrunk = shrunk.reshape(-1, LANES, D // LANES, LANES).transpose(0, 2, 1, 3)
        v = jnp.concatenate([grown, shrunk.reshape(-1, 1, D, LANES)], axis=1)
        residual, normed, theirs = attend(lambda number, value: value)
        own_sum = first_units(lengths, normed, v[:4])

    their_sum = first_units(their_lengths, theirs, v[:4])
    counts = (lengths, their_lengths)
    own_sum, their_sum = more_units(*counts, normed, theirs, own_sum, their_sum, v[4:6])
    own_total, their_total = last_units(*counts, normed, theirs, own_sum, their_sum, v[6:])
    back = swapped(their_total, count, 1)
    item_vectors, candidates = pool_items(
        count,
        *counts,
        norm_gains,
        residual,
        pool_weight,
        normed,
        own_sum,
        own_total,
        back,
        *v[6:],
    )
    every = lax.all_to_all(candidates, "dp", 0, 0, tiled=True)
    every = every.reshape(count * lengths.shape[0], D)
    return item_vectors, list_loss(queries, list_ids, labels, every)


def solution(mesh):
    return jax.shard_map(
        functools.partial(local, mesh.shape["dp"], mesh.shape["groups"]),
        mesh=mesh,
        in_specs=(
            P(("groups", "dp"), None),
            P(("groups", "dp")),
            P(),
            P(),
            P(),
            P(None, None, "dp"),
            P("dp", None),
            P(),
            P(("groups", "dp"), None),
            P(("groups", "dp")),
            P(("groups", "dp"), None),
        ),
        out_specs=(P(("groups", "dp"), None), P(("groups", "dp"))),
        check_vma=False,
    )
```

```python
import functools

import jax
import jax.numpy as jnp
from jax import lax
from jax.experimental import pallas as pl
from jax.experimental.pallas import tpu as pltpu
from jax.sharding import PartitionSpec as P

D = 768
HEAD = 64
LISTS = 2
OUTER = 4
CHUNK = 256

SCORE_SCALE = HEAD ** (-0.5) * 1.4426950408889634
epsilon = 1e-06
score_scale = 32.0
MIB = 1024 * 1024
SHORT = pl.CostEstimate(flops=1000, bytes_accessed=1000, transcendentals=0)
LONG = pl.CostEstimate(flops=40_000_000_000, bytes_accessed=1000, transcendentals=0)


def inverse_rms(widened):
    return lax.rsqrt(jnp.mean(widened * widened, axis=-1, keepdims=True) + epsilon)


def nt_dot(left, right):
    return lax.dot_general(
        left, right, (((1,), (1,)), ((), ())), preferred_element_type=jnp.float32
    )


LANES = 128


def pack_kernel(expand, contract, packed, stage, come, gone):
    arrivals = [
        pltpu.make_async_copy(expand.at[which], stage.at[which], come.at[which])
        for which in range(2)
    ]
    for piece in range(D // LANES):
        columns = slice(piece * LANES, (piece + 1) * LANES)
        source, target = contract.at[:, columns], stage.at[2, columns, :]
        arrivals.append(pltpu.make_async_copy(source, target, come.at[2 + piece]))
    leavings = [
        pltpu.make_async_copy(stage.at[which], packed.at[which], gone.at[which])
        for which in range(3)
    ]
    for copy in arrivals:
        copy.start()
    for which in range(3):
        for copy in arrivals[2:] if which == 2 else arrivals[which : which + 1]:
            copy.wait()
        leavings[which].start()
    for copy in leavings:
        copy.wait()


def pack_weights(expand_weight, contract_weight):
    in_place = pl.BlockSpec(memory_space=pltpu.HBM)
    block = jax.ShapeDtypeStruct((3, D, LANES), jnp.bfloat16)
    return pl.pallas_call(
        pack_kernel,
        out_shape=block,
        in_specs=[in_place, in_place],
        out_specs=in_place,
        scratch_shapes=[
            pltpu.VMEM(block.shape, block.dtype),
            pltpu.SemaphoreType.DMA((2 + D // LANES,)),
            pltpu.SemaphoreType.DMA((3,)),
        ],
        compiler_params=pltpu.CompilerParams(vmem_limit_bytes=60 * MIB),
        name="pack_weights",
    )(expand_weight, contract_weight)


def row_tile(rows):
    return 256 if rows % 256 == 0 else rows


def live_tiles(items, lengths, tile):
    total = lengths[0]
    for item in range(1, items):
        total = total + lengths[item]
    return (total + tile - 1) // tile


def tile_rows(index, tile):
    return pl.ds(pl.multiple_of(index * tile, tile), tile)


def project_kernel(items, lengths, tokens, gains, weights, out):
    tile = row_tile(tokens.shape[0])

    def body(index, carry):
        here = tile_rows(index, tile)
        widened = tokens[here, :].astype(jnp.float32)
        x = (widened * inverse_rms(widened) * gains[0:1, :]).astype(jnp.bfloat16)
        for which in range(3):
            span = slice(which * D, (which + 1) * D)
            part = jnp.dot(x, weights[:, span], preferred_element_type=jnp.float32)
            if which == 0:
                part = part * SCORE_SCALE
            out[here, span] = part.astype(jnp.bfloat16)
        return carry

    lax.fori_loop(0, live_tiles(items, lengths, tile), body, 0)


def call(kernel, name, scalars, arrays, out_shape, cost=SHORT):
    whole = pl.BlockSpec(memory_space=pltpu.VMEM)
    return pl.pallas_call(
        functools.partial(kernel, scalars[0].shape[0]),
        in_specs=[pl.BlockSpec(memory_space=pltpu.SMEM)] * len(scalars) + [whole] * len(arrays),
        out_specs=jax.tree.map(lambda _: whole, out_shape),
        out_shape=out_shape,
        compiler_params=pltpu.CompilerParams(vmem_limit_bytes=24 * MIB),
        cost_estimate=cost,
        name=name,
    )(*scalars, *arrays)


def project(lengths, tokens, norm_gains, query_key_value):
    out = jax.ShapeDtypeStruct((tokens.shape[0], 3 * D), jnp.bfloat16)
    return call(project_kernel, "project", (lengths,), (tokens, norm_gains, query_key_value), out)


def heads_kernel(items, lengths, projected, mixed_heads):
    rows = projected.shape[0]
    tile = row_tile(rows)
    wide = 2 * HEAD
    group = D // 2
    lane = lax.broadcasted_iota(jnp.int32, (1, wide), 1) // HEAD
    ends = []
    end = 0
    for item in range(items):
        end = end + lengths[item]
        ends.append(end)
    tiles = (end + tile - 1) // tile

    def segment(position):
        return sum((position >= end).astype(jnp.int32) for end in ends)

    for keys in range(tile, rows + 1, tile):
        across = segment(lax.broadcasted_iota(jnp.int32, (1, keys), 1))

        def body(index, carry):
            row = index // 2
            here = tile_rows(row, tile)
            offset = pl.multiple_of(index % 2 * group, group)
            down = segment(row * tile + lax.broadcasted_iota(jnp.int32, (tile, 1), 0))
            same = down == across

            def columns(kind, head):
                return pl.ds(kind * D + offset + head // 2 * wide, wide)

            def scores(head):
                q = projected[here, columns(0, head)]
                q = jnp.where(lane == head % 2, q, jnp.bfloat16(0))
                return nt_dot(q, projected[:keys, columns(1, head)])

            count = group // HEAD
            ahead = scores(0)
            for head in range(count):
                logits = jnp.where(same, ahead, -1e30)
                if head + 1 < count:
                    ahead = scores(head + 1)
                highest = jnp.max(logits, axis=1, keepdims=True)
                weights = jnp.exp2((logits - highest).astype(jnp.bfloat16))
                mine = lane == head % 2
                v = jnp.where(mine, projected[:keys, columns(2, head)], jnp.bfloat16(1))
                out = jnp.dot(weights, v, preferred_element_type=jnp.float32)
                other = (1 - head % 2) * HEAD
                out = out * (1.0 / out[:, other : other + 1])
                mixed = out if head % 2 == 0 else jnp.where(mine, out, mixed)
                if head % 2 == 1:
                    mixed_heads[here, columns(0, head)] = mixed.astype(jnp.bfloat16)
            return carry

        count = keys // tile
        lax.fori_loop(0, jnp.where(tiles == count, 2 * count, 0), body, 0)


def heads(lengths, projected):
    out = jax.ShapeDtypeStruct((projected.shape[0], D), jnp.bfloat16)
    return call(heads_kernel, "heads", (lengths,), (projected,), out)


def join_kernel(items, lengths, tokens, gains, wo, mixed_heads, residual, normed):
    tile = row_tile(tokens.shape[0])

    def body(index, carry):
        here = tile_rows(index, tile)
        total = tokens[here, :].astype(jnp.float32)
        total += jnp.dot(mixed_heads[here, :], wo[...], preferred_element_type=jnp.float32)
        rounded = total.astype(jnp.bfloat16)
        residual[here, :] = rounded
        widened = rounded.astype(jnp.float32)
        normed[here, :] = (widened * inverse_rms(widened) * gains[1:2, :]).astype(jnp.bfloat16)
        return carry

    lax.fori_loop(0, live_tiles(items, lengths, tile), body, 0)


def join_heads(lengths, *arrays):
    rows = jax.ShapeDtypeStruct(arrays[0].shape, jnp.bfloat16)
    return call(join_kernel, "join_heads", (lengths,), arrays, (rows, rows))


def grow(block_group, which):
    return jnp.concatenate([block[which] for block in block_group], axis=1)


def shrink(block_group):
    rows = []
    for block in block_group:
        pieces = [block[2, i : i + LANES, :] for i in range(0, D, LANES)]
        rows.append(jnp.concatenate(pieces, axis=1))
    return jnp.concatenate(rows, axis=0)


def hidden_units(here, blocks):
    each = CHUNK // LANES
    grown = None
    for start in range(0, len(blocks), each):
        group = blocks[start : start + each]
        if len(group) == each:
            gate = jnp.dot(here, grow(group, 0), preferred_element_type=jnp.float32)
            up = jnp.dot(here, grow(group, 1), preferred_element_type=jnp.float32)
        else:
            both = jnp.concatenate([block[which] for which in range(2) for block in group], axis=1)
            both = jnp.dot(here, both, preferred_element_type=jnp.float32)
            gate, up = jnp.split(both, 2, axis=1)
        active = (jax.nn.gelu(gate, approximate=True) * up).astype(jnp.bfloat16)
        term = jnp.dot(active, shrink(group), preferred_element_type=jnp.float32)
        grown = term if grown is None else grown + term
    return grown


def all_tiles(tiles, every, tile, one_tile):
    def body(index, carry):
        one_tile(tile_rows(index, tile))
        return carry

    lax.fori_loop(0, jnp.where(tiles == every, 0, tiles), body, 0)

    @pl.when(tiles == every)
    def _():
        for index in range(every):
            one_tile(slice(index * tile, (index + 1) * tile))


def first_kernel(items, lengths, x, *refs):
    blocks, total = refs[:-1], refs[-1]
    tile = row_tile(x.shape[0])

    def one_tile(span):
        total[span, :] = hidden_units(x[span, :], blocks)

    all_tiles(live_tiles(items, lengths, tile), x.shape[0] // tile, tile, one_tile)


def first_units(lengths, normed, blocks):
    out = jax.ShapeDtypeStruct(normed.shape, jnp.float32)
    return call(first_kernel, "first_units", (lengths,), (normed, *blocks), out, cost=LONG)


def last_kernel(
    items, lengths, their_lengths, residual, normed, their_normed, own, theirs, *refs
):
    blocks, (own_total, their_total) = refs[:-2], refs[-2:]
    tile = row_tile(normed.shape[0])
    every = normed.shape[0] // tile
    tiles = live_tiles(items, lengths, tile)
    their_tiles = live_tiles(items, their_lengths, tile)

    def one_tile(span):
        grown = theirs[span, :] + hidden_units(their_normed[span, :], blocks)
        their_total[span, :] = grown.astype(jnp.bfloat16)

    all_tiles(their_tiles, every, tile, one_tile)

    def own_tile(span):
        kept = own[span, :] + residual[span, :].astype(jnp.float32)
        own_total[span, :] = kept + hidden_units(normed[span, :], blocks)

    all_tiles(jnp.where(tiles > their_tiles, tiles, 0), every, tile, own_tile)


def last_units(lengths, their_lengths, residual, normed, their_normed, own, theirs, blocks):
    out = (
        jax.ShapeDtypeStruct(normed.shape, jnp.float32),
        jax.ShapeDtypeStruct(normed.shape, jnp.bfloat16),
    )
    arrays = (residual, normed, their_normed, own, theirs, *blocks)
    return call(last_kernel, "last_units", (lengths, their_lengths), arrays, out)


def pool_kernel(
    items, lengths, their_lengths, gains, residual, pool, normed, own, own_total, back, *refs
):
    blocks, (vectors, candidates) = refs[:-2], refs[-2:]
    tile = row_tile(residual.shape[0])
    tiles = live_tiles(items, lengths, tile)
    done = tiles > live_tiles(items, their_lengths, tile)
    slots = 16
    slot = lax.broadcasted_iota(jnp.int32, (slots, 1), 0)
    first = jnp.zeros((slots, 1), jnp.int32)
    last = jnp.zeros((slots, 1), jnp.int32)
    begin = 0
    for item in range(items):
        end = begin + lengths[item]
        first = jnp.where(slot == item, begin, first)
        last = jnp.where(slot == item, end, last)
        begin = end

    def pool_tile(here, index, total, summed):
        total = total + back[here, :].astype(jnp.float32)
        finished = total.astype(jnp.bfloat16).astype(jnp.float32)
        final_rows = (finished * inverse_rms(finished) * gains[2:3, :]).astype(jnp.bfloat16)
        across = index * tile + lax.broadcasted_iota(jnp.int32, (slots, tile), 1)
        member = jnp.where((across >= first) & (across < last), 1.0, 0.0)
        return summed + jnp.dot(
            member.astype(jnp.bfloat16), final_rows, preferred_element_type=jnp.float32
        )

    def finished_tile(index, summed):
        here = tile_rows(index, tile)
        return pool_tile(here, index, own_total[here, :], summed)

    def other_tile(index, summed):
        here = tile_rows(index, tile)
        total = own[here, :] + residual[here, :].astype(jnp.float32)
        total = total + hidden_units(normed[here, :], blocks)
        return pool_tile(here, index, total, summed)

    summed = jnp.zeros((slots, D), jnp.float32)
    summed = lax.fori_loop(0, jnp.where(done, tiles, 0), finished_tile, summed)
    summed = lax.fori_loop(0, jnp.where(done, 0, tiles), other_tile, summed)
    counts = jnp.maximum(last - first, 1).astype(jnp.float32)
    pooled = (summed / counts).astype(jnp.bfloat16)
    e = jnp.dot(pooled, pool[...], preferred_element_type=jnp.float32)
    e = e * inverse_rms(e)
    vectors[...] = e[:items, :]
    mine = e[:items, :].astype(jnp.bfloat16)
    for device in range(candidates.shape[0]):
        candidates[device] = mine


def pool_items(devices, lengths, their_lengths, *arrays):
    items = lengths.shape[0]
    out = (
        jax.ShapeDtypeStruct((items, D), jnp.float32),
        jax.ShapeDtypeStruct((devices, items, D), jnp.bfloat16),
    )
    return call(pool_kernel, "pool_items", (lengths, their_lengths), arrays, out)


def loss_kernel(queries, list_ids, labels, candidates, loss):
    widened = queries[...].astype(jnp.float32)
    query_unit = (widened * inverse_rms(widened)).astype(jnp.bfloat16)
    each = labels.shape[0]
    chosen = None
    for which in range(LISTS):
        scores = nt_dot(candidates[which * each : (which + 1) * each, :], query_unit)
        if chosen is None:
            chosen = scores
        else:
            chosen = jnp.where(list_ids[...] == which, scores, chosen)
    chosen = chosen * (score_scale / D)
    target = jnp.exp(labels[...].astype(jnp.float32))
    target = target / jnp.sum(target, axis=0, keepdims=True)
    log_total = jnp.log(jnp.sum(jnp.exp(chosen), axis=0, keepdims=True))
    loss[...] = log_total - jnp.sum(target * chosen, axis=0, keepdims=True)


def list_loss(queries, list_ids, labels, candidates):
    count = queries.shape[0]
    return pl.pallas_call(
        loss_kernel,
        out_shape=jax.ShapeDtypeStruct((1, count), jnp.float32),
        compiler_params=pltpu.CompilerParams(vmem_limit_bytes=16 * MIB),
        name="list_loss",
    )(queries, list_ids.reshape(1, count), labels.T, candidates).reshape(count)


def swapped(value, count, bit):
    return lax.ppermute(value, "dp", [(i, i ^ bit) for i in range(count)])


def after(value, *earlier):
    return lax.optimization_barrier((value, earlier))[0]


def local(
    count,
    planes,
    tokens,
    lengths,
    norm_gains,
    query_key_value,
    attention_out,
    expand_weight,
    contract_weight,
    pool_weight,
    queries,
    list_ids,
    labels,
):
    inner = count // OUTER
    their_lengths = swapped(lengths, count, 1)

    def attend(turn):
        projected = turn(0, project(lengths, tokens, norm_gains, query_key_value))
        mixed_heads = heads(lengths, projected)
        residual, normed = join_heads(lengths, tokens, norm_gains, attention_out, mixed_heads)
        return residual, turn(1, normed), swapped(normed, count, 1)

    same_core = [list(range(first, count, 2)) for first in range(2)]
    if planes == 2 and inner == 4 and contract_weight.shape[0] == LANES:

        def hop(value, same, across, crossed):
            pairs = []
            for here in range(planes * count):
                y, place = divmod(here, count)
                z, x, c = place // inner, place % inner // 2, place % 2
                role = 0 if c == y else 1
                link = across if role else same
                if link == "y":
                    y = 1 - y
                elif link == "x":
                    x = 1 - x
                else:
                    z = (z + (1 if link == "up" else OUTER - 1)) % OUTER
                role = 1 - role if crossed else role
                pairs.append((here, y * count + z * inner + x * 2 + (1 - y if role else y)))
            return lax.ppermute(value, ("groups", "dp"), pairs)

        v = [pack_weights(expand_weight, contract_weight)]
        v.append(hop(v[0], "x", "up", True))

        def turn(number, value):
            if number == 0:
                v[1], value = after((v[1], value))
                v.append(hop(v[1], "up", "down", False))
                v.append(hop(v[1], "y", "up", False))
                v.append(hop(v[1], "x", "y", False))
            else:
                v[2], value = after((v[2], value))
                v.append(hop(v[2], "up", "y", False))
                v.append(hop(v[2], "x", "x", False))
                v.append(hop(v[2], "y", "down", False))
            return value

        residual, normed, theirs = attend(turn)
        first = tuple(v[:5])
        third = tuple(v[5:8])
        own_sum = first_units(lengths, normed, first)
    else:
        grown = lax.all_gather(
            expand_weight, "dp", axis=2, tiled=True, axis_index_groups=same_core
        )
        shrunk = lax.all_gather(
            contract_weight, "dp", axis=0, tiled=True, axis_index_groups=same_core
        )
        grown = grown.reshape(2, D, -1, LANES).transpose(2, 0, 1, 3)
        shrunk = shrunk.reshape(-1, LANES, D // LANES, LANES).transpose(0, 2, 1, 3)
        v = jnp.concatenate([grown, shrunk.reshape(-1, 1, D, LANES)], axis=1)
        residual, normed, theirs = attend(lambda number, value: value)
        first = tuple(v[:5])
        third = tuple(v[5:])
        own_sum = first_units(lengths, normed, first)

    their_sum = first_units(their_lengths, theirs, first)
    counts = (lengths, their_lengths)
    own_total, their_total = last_units(
        *counts, residual, normed, theirs, own_sum, their_sum, third
    )
    back = swapped(their_total, count, 1)
    item_vectors, candidates = pool_items(
        count,
        *counts,
        norm_gains,
        residual,
        pool_weight,
        normed,
        own_sum,
        own_total,
        back,
        *third,
    )
    every = lax.all_to_all(candidates, "dp", 0, 0, tiled=True)
    every = every.reshape(count * lengths.shape[0], D)
    return item_vectors, list_loss(queries, list_ids, labels, every)


def solution(mesh):
    return jax.shard_map(
        functools.partial(local, mesh.shape["dp"], mesh.shape["groups"]),
        mesh=mesh,
        in_specs=(
            P(("groups", "dp"), None),
            P(("groups", "dp")),
            P(),
            P(),
            P(),
            P(None, None, "dp"),
            P("dp", None),
            P(),
            P(("groups", "dp"), None),
            P(("groups", "dp")),
            P(("groups", "dp"), None),
        ),
        out_specs=(P(("groups", "dp"), None), P(("groups", "dp"))),
        check_vma=False,
    )
```

```python
import functools

import jax
import jax.numpy as jnp
from jax import lax
from jax.experimental import pallas as pl
from jax.experimental.pallas import tpu as pltpu
from jax.sharding import PartitionSpec as P

D = 768
HEAD = 64
LISTS = 2
OUTER = 4
CHUNK = 256

SCORE_SCALE = HEAD ** (-0.5) * 1.4426950408889634
epsilon = 1e-06
score_scale = 32.0
MIB = 1024 * 1024
SHORT = pl.CostEstimate(flops=1000, bytes_accessed=1000, transcendentals=0)
LONG = pl.CostEstimate(flops=40_000_000_000, bytes_accessed=1000, transcendentals=0)


def inverse_rms(widened):
    return lax.rsqrt(jnp.mean(widened * widened, axis=-1, keepdims=True) + epsilon)


def nt_dot(left, right):
    return lax.dot_general(
        left, right, (((1,), (1,)), ((), ())), preferred_element_type=jnp.float32
    )


LANES = 128


def pack_kernel(expand, contract, packed, stage, come, gone):
    arrivals = [
        pltpu.make_async_copy(expand.at[which], stage.at[which], come.at[which])
        for which in range(2)
    ]
    for piece in range(D // LANES):
        columns = slice(piece * LANES, (piece + 1) * LANES)
        source, target = contract.at[:, columns], stage.at[2, columns, :]
        arrivals.append(pltpu.make_async_copy(source, target, come.at[2 + piece]))
    leavings = [
        pltpu.make_async_copy(stage.at[which], packed.at[which], gone.at[which])
        for which in range(3)
    ]
    for copy in arrivals:
        copy.start()
    for which in range(3):
        for copy in arrivals[2:] if which == 2 else arrivals[which : which + 1]:
            copy.wait()
        leavings[which].start()
    for copy in leavings:
        copy.wait()


def pack_weights(expand_weight, contract_weight):
    in_place = pl.BlockSpec(memory_space=pltpu.HBM)
    block = jax.ShapeDtypeStruct((3, D, LANES), jnp.bfloat16)
    return pl.pallas_call(
        pack_kernel,
        out_shape=block,
        in_specs=[in_place, in_place],
        out_specs=in_place,
        scratch_shapes=[
            pltpu.VMEM(block.shape, block.dtype),
            pltpu.SemaphoreType.DMA((2 + D // LANES,)),
            pltpu.SemaphoreType.DMA((3,)),
        ],
        compiler_params=pltpu.CompilerParams(vmem_limit_bytes=60 * MIB),
        name="pack_weights",
    )(expand_weight, contract_weight)


def row_tile(rows):
    return 256 if rows % 256 == 0 else rows


def live_tiles(items, lengths, tile):
    total = lengths[0]
    for item in range(1, items):
        total = total + lengths[item]
    return (total + tile - 1) // tile


def tile_rows(index, tile):
    return pl.ds(pl.multiple_of(index * tile, tile), tile)


def project_kernel(items, lengths, tokens, gains, weights, out):
    tile = row_tile(tokens.shape[0])

    def body(index, carry):
        here = tile_rows(index, tile)
        widened = tokens[here, :].astype(jnp.float32)
        x = (widened * inverse_rms(widened) * gains[0:1, :]).astype(jnp.bfloat16)
        for which in range(3):
            span = slice(which * D, (which + 1) * D)
            part = jnp.dot(x, weights[:, span], preferred_element_type=jnp.float32)
            if which == 0:
                part = part * SCORE_SCALE
            out[here, span] = part.astype(jnp.bfloat16)
        return carry

    lax.fori_loop(0, live_tiles(items, lengths, tile), body, 0)


def call(kernel, name, scalars, arrays, out_shape, cost=SHORT):
    whole = pl.BlockSpec(memory_space=pltpu.VMEM)
    return pl.pallas_call(
        functools.partial(kernel, scalars[0].shape[0]),
        in_specs=[pl.BlockSpec(memory_space=pltpu.SMEM)] * len(scalars) + [whole] * len(arrays),
        out_specs=jax.tree.map(lambda _: whole, out_shape),
        out_shape=out_shape,
        compiler_params=pltpu.CompilerParams(vmem_limit_bytes=24 * MIB),
        cost_estimate=cost,
        name=name,
    )(*scalars, *arrays)


def project(lengths, tokens, norm_gains, query_key_value):
    out = jax.ShapeDtypeStruct((tokens.shape[0], 3 * D), jnp.bfloat16)
    return call(project_kernel, "project", (lengths,), (tokens, norm_gains, query_key_value), out)


def heads_kernel(items, lengths, projected, mixed_heads):
    rows = projected.shape[0]
    tile = row_tile(rows)
    wide = 2 * HEAD
    group = D // 2
    lane = lax.broadcasted_iota(jnp.int32, (1, wide), 1) // HEAD
    ends = []
    end = 0
    for item in range(items):
        end = end + lengths[item]
        ends.append(end)
    tiles = (end + tile - 1) // tile

    def segment(position):
        return sum((position >= end).astype(jnp.int32) for end in ends)

    for keys in range(tile, rows + 1, tile):
        across = segment(lax.broadcasted_iota(jnp.int32, (1, keys), 1))

        def body(index, carry):
            row = index // 2
            here = tile_rows(row, tile)
            offset = pl.multiple_of(index % 2 * group, group)
            down = segment(row * tile + lax.broadcasted_iota(jnp.int32, (tile, 1), 0))
            same = down == across

            def columns(kind, head):
                return pl.ds(kind * D + offset + head // 2 * wide, wide)

            def scores(head):
                q = projected[here, columns(0, head)]
                q = jnp.where(lane == head % 2, q, jnp.bfloat16(0))
                return nt_dot(q, projected[:keys, columns(1, head)])

            count = group // HEAD
            ahead = scores(0)
            for head in range(count):
                logits = jnp.where(same, ahead, -1e30)
                if head + 1 < count:
                    ahead = scores(head + 1)
                highest = jnp.max(logits, axis=1, keepdims=True)
                weights = jnp.exp2((logits - highest).astype(jnp.bfloat16))
                mine = lane == head % 2
                v = jnp.where(mine, projected[:keys, columns(2, head)], jnp.bfloat16(1))
                out = jnp.dot(weights, v, preferred_element_type=jnp.float32)
                other = (1 - head % 2) * HEAD
                out = out * (1.0 / out[:, other : other + 1])
                mixed = out if head % 2 == 0 else jnp.where(mine, out, mixed)
                if head % 2 == 1:
                    mixed_heads[here, columns(0, head)] = mixed.astype(jnp.bfloat16)
            return carry

        count = keys // tile
        lax.fori_loop(0, jnp.where(tiles == count, 2 * count, 0), body, 0)


def heads(lengths, projected):
    out = jax.ShapeDtypeStruct((projected.shape[0], D), jnp.bfloat16)
    return call(heads_kernel, "heads", (lengths,), (projected,), out)


def join_kernel(items, lengths, tokens, gains, wo, mixed_heads, residual, normed):
    tile = row_tile(tokens.shape[0])

    def body(index, carry):
        here = tile_rows(index, tile)
        total = tokens[here, :].astype(jnp.float32)
        total += jnp.dot(mixed_heads[here, :], wo[...], preferred_element_type=jnp.float32)
        rounded = total.astype(jnp.bfloat16)
        residual[here, :] = rounded
        widened = rounded.astype(jnp.float32)
        normed[here, :] = (widened * inverse_rms(widened) * gains[1:2, :]).astype(jnp.bfloat16)
        return carry

    lax.fori_loop(0, live_tiles(items, lengths, tile), body, 0)


def join_heads(lengths, *arrays):
    rows = jax.ShapeDtypeStruct(arrays[0].shape, jnp.bfloat16)
    return call(join_kernel, "join_heads", (lengths,), arrays, (rows, rows))


def grow(block_group, which):
    return jnp.concatenate([block[which] for block in block_group], axis=1)


def shrink(block_group):
    rows = []
    for block in block_group:
        pieces = [block[2, i : i + LANES, :] for i in range(0, D, LANES)]
        rows.append(jnp.concatenate(pieces, axis=1))
    return jnp.concatenate(rows, axis=0)


def hidden_units(rows, blocks, finish):
    each = CHUNK // LANES
    groups = [blocks[start : start + each] for start in range(0, len(blocks), each)]
    work = [(tile, group) for tile in range(len(rows)) for group in range(len(groups))]

    def expand(tile, group):
        gate = jnp.dot(rows[tile], grow(groups[group], 0), preferred_element_type=jnp.float32)
        up = jnp.dot(rows[tile], grow(groups[group], 1), preferred_element_type=jnp.float32)
        return gate, up

    ahead = expand(*work[0])
    for number, (tile, group) in enumerate(work):
        gate, up = ahead
        if number + 1 < len(work):
            ahead = expand(*work[number + 1])
        active = (jax.nn.gelu(gate, approximate=True) * up).astype(jnp.bfloat16)
        term = jnp.dot(active, shrink(groups[group]), preferred_element_type=jnp.float32)
        grown = term if group == 0 else grown + term
        if group == len(groups) - 1:
            finish(tile, grown)


def all_tiles(tiles, every, tile, run):
    def body(index, carry):
        run([tile_rows(index, tile)])
        return carry

    lax.fori_loop(0, jnp.where(tiles == every, 0, tiles), body, 0)

    @pl.when(tiles == every)
    def _():
        run([slice(index * tile, (index + 1) * tile) for index in range(every)])


def first_kernel(items, lengths, x, *refs):
    blocks, total = refs[:-1], refs[-1]
    tile = row_tile(x.shape[0])

    def run(spans):
        def finish(number, grown):
            total[spans[number], :] = grown

        hidden_units([x[span, :] for span in spans], blocks, finish)

    all_tiles(live_tiles(items, lengths, tile), x.shape[0] // tile, tile, run)


def first_units(lengths, normed, blocks):
    out = jax.ShapeDtypeStruct(normed.shape, jnp.float32)
    return call(first_kernel, "first_units", (lengths,), (normed, *blocks), out, cost=LONG)


def last_kernel(
    items, lengths, their_lengths, residual, normed, their_normed, own, theirs, *refs
):
    blocks, (own_total, their_total) = refs[:-2], refs[-2:]
    tile = row_tile(normed.shape[0])
    every = normed.shape[0] // tile
    tiles = live_tiles(items, lengths, tile)
    their_tiles = live_tiles(items, their_lengths, tile)

    def run_theirs(spans):
        def finish(number, grown):
            span = spans[number]
            their_total[span, :] = (theirs[span, :] + grown).astype(jnp.bfloat16)

        hidden_units([their_normed[span, :] for span in spans], blocks, finish)

    def run_own(spans):
        def finish(number, grown):
            span = spans[number]
            kept = own[span, :] + residual[span, :].astype(jnp.float32)
            own_total[span, :] = kept + grown

        hidden_units([normed[span, :] for span in spans], blocks, finish)

    all_tiles(their_tiles, every, tile, run_theirs)
    all_tiles(jnp.where(tiles > their_tiles, tiles, 0), every, tile, run_own)


def last_units(lengths, their_lengths, residual, normed, their_normed, own, theirs, blocks):
    out = (
        jax.ShapeDtypeStruct(normed.shape, jnp.float32),
        jax.ShapeDtypeStruct(normed.shape, jnp.bfloat16),
    )
    arrays = (residual, normed, their_normed, own, theirs, *blocks)
    return call(last_kernel, "last_units", (lengths, their_lengths), arrays, out)


def pool_kernel(
    items, lengths, their_lengths, gains, residual, pool, normed, own, own_total, back, *refs
):
    blocks, (vectors, candidates) = refs[:-2], refs[-2:]
    tile = row_tile(residual.shape[0])
    tiles = live_tiles(items, lengths, tile)
    done = tiles > live_tiles(items, their_lengths, tile)
    slots = 16
    slot = lax.broadcasted_iota(jnp.int32, (slots, 1), 0)
    first = jnp.zeros((slots, 1), jnp.int32)
    last = jnp.zeros((slots, 1), jnp.int32)
    begin = 0
    for item in range(items):
        end = begin + lengths[item]
        first = jnp.where(slot == item, begin, first)
        last = jnp.where(slot == item, end, last)
        begin = end

    def pool_tile(here, index, total, summed):
        total = total + back[here, :].astype(jnp.float32)
        finished = total.astype(jnp.bfloat16).astype(jnp.float32)
        final_rows = (finished * inverse_rms(finished) * gains[2:3, :]).astype(jnp.bfloat16)
        across = index * tile + lax.broadcasted_iota(jnp.int32, (slots, tile), 1)
        member = jnp.where((across >= first) & (across < last), 1.0, 0.0)
        return summed + jnp.dot(
            member.astype(jnp.bfloat16), final_rows, preferred_element_type=jnp.float32
        )

    def finished_tile(index, summed):
        here = tile_rows(index, tile)
        return pool_tile(here, index, own_total[here, :], summed)

    def other_tile(index, summed):
        here = tile_rows(index, tile)
        parts = []
        hidden_units([normed[here, :]], blocks, lambda number, grown: parts.append(grown))
        total = own[here, :] + residual[here, :].astype(jnp.float32) + parts[0]
        return pool_tile(here, index, total, summed)

    summed = jnp.zeros((slots, D), jnp.float32)
    summed = lax.fori_loop(0, jnp.where(done, tiles, 0), finished_tile, summed)
    summed = lax.fori_loop(0, jnp.where(done, 0, tiles), other_tile, summed)
    counts = jnp.maximum(last - first, 1).astype(jnp.float32)
    pooled = (summed / counts).astype(jnp.bfloat16)
    e = jnp.dot(pooled, pool[...], preferred_element_type=jnp.float32)
    e = e * inverse_rms(e)
    vectors[...] = e[:items, :]
    mine = e[:items, :].astype(jnp.bfloat16)
    for device in range(candidates.shape[0]):
        candidates[device] = mine


def pool_items(devices, lengths, their_lengths, *arrays):
    items = lengths.shape[0]
    out = (
        jax.ShapeDtypeStruct((items, D), jnp.float32),
        jax.ShapeDtypeStruct((devices, items, D), jnp.bfloat16),
    )
    return call(pool_kernel, "pool_items", (lengths, their_lengths), arrays, out)


def loss_kernel(queries, list_ids, labels, candidates, loss):
    widened = queries[...].astype(jnp.float32)
    query_unit = (widened * inverse_rms(widened)).astype(jnp.bfloat16)
    each = labels.shape[0]
    chosen = None
    for which in range(LISTS):
        scores = nt_dot(candidates[which * each : (which + 1) * each, :], query_unit)
        if chosen is None:
            chosen = scores
        else:
            chosen = jnp.where(list_ids[...] == which, scores, chosen)
    chosen = chosen * (score_scale / D)
    target = jnp.exp(labels[...].astype(jnp.float32))
    target = target / jnp.sum(target, axis=0, keepdims=True)
    log_total = jnp.log(jnp.sum(jnp.exp(chosen), axis=0, keepdims=True))
    loss[...] = log_total - jnp.sum(target * chosen, axis=0, keepdims=True)


def list_loss(queries, list_ids, labels, candidates):
    count = queries.shape[0]
    return pl.pallas_call(
        loss_kernel,
        out_shape=jax.ShapeDtypeStruct((1, count), jnp.float32),
        compiler_params=pltpu.CompilerParams(vmem_limit_bytes=16 * MIB),
        name="list_loss",
    )(queries, list_ids.reshape(1, count), labels.T, candidates).reshape(count)


def swapped(value, count, bit):
    return lax.ppermute(value, "dp", [(i, i ^ bit) for i in range(count)])


def after(value, *earlier):
    return lax.optimization_barrier((value, earlier))[0]


def local(
    count,
    planes,
    tokens,
    lengths,
    norm_gains,
    query_key_value,
    attention_out,
    expand_weight,
    contract_weight,
    pool_weight,
    queries,
    list_ids,
    labels,
):
    inner = count // OUTER
    counts = [lengths, swapped(lengths, count, 1)]

    def attend(turn):
        projected = project(lengths, tokens, norm_gains, query_key_value)
        projected, counts[1] = turn(0, (projected, counts[1]))
        mixed_heads = heads(lengths, projected)
        residual, normed = join_heads(lengths, tokens, norm_gains, attention_out, mixed_heads)
        return residual, turn(1, normed), swapped(normed, count, 1)

    same_core = [list(range(first, count, 2)) for first in range(2)]
    if planes == 2 and inner == 4 and contract_weight.shape[0] == LANES:

        def hop(value, same, across, crossed):
            pairs = []
            for here in range(planes * count):
                y, place = divmod(here, count)
                z, x, c = place // inner, place % inner // 2, place % 2
                role = 0 if c == y else 1
                link = across if role else same
                if link == "y":
                    y = 1 - y
                elif link == "x":
                    x = 1 - x
                else:
                    z = (z + (1 if link == "up" else OUTER - 1)) % OUTER
                role = 1 - role if crossed else role
                pairs.append((here, y * count + z * inner + x * 2 + (1 - y if role else y)))
            return lax.ppermute(value, ("groups", "dp"), pairs)

        v = [pack_weights(expand_weight, contract_weight)]
        v.append(hop(v[0], "x", "up", True))

        def turn(number, value):
            if number == 0:
                v[1], value = after((v[1], value))
                v.append(hop(v[1], "up", "down", False))
                v.append(hop(v[1], "y", "up", False))
                v.append(hop(v[1], "x", "y", False))
            else:
                v[2], value = after((v[2], value))
                v.append(hop(v[2], "up", "y", False))
                v.append(hop(v[2], "x", "x", False))
                v.append(hop(v[2], "y", "down", False))
            return value

        residual, normed, theirs = attend(turn)
        first = tuple(v[:5])
        third = tuple(v[5:8])
        own_sum = first_units(lengths, normed, first)
    else:
        grown = lax.all_gather(
            expand_weight, "dp", axis=2, tiled=True, axis_index_groups=same_core
        )
        shrunk = lax.all_gather(
            contract_weight, "dp", axis=0, tiled=True, axis_index_groups=same_core
        )
        grown = grown.reshape(2, D, -1, LANES).transpose(2, 0, 1, 3)
        shrunk = shrunk.reshape(-1, LANES, D // LANES, LANES).transpose(0, 2, 1, 3)
        v = jnp.concatenate([grown, shrunk.reshape(-1, 1, D, LANES)], axis=1)
        residual, normed, theirs = attend(lambda number, value: value)
        first = tuple(v[:5])
        third = tuple(v[5:])
        own_sum = first_units(lengths, normed, first)

    their_sum = first_units(counts[1], theirs, first)
    own_total, their_total = last_units(
        *counts, residual, normed, theirs, own_sum, their_sum, third
    )
    back = swapped(their_total, count, 1)
    item_vectors, candidates = pool_items(
        count,
        *counts,
        norm_gains,
        residual,
        pool_weight,
        normed,
        own_sum,
        own_total,
        back,
        *third,
    )
    every = lax.all_to_all(candidates, "dp", 0, 0, tiled=True)
    every = every.reshape(count * lengths.shape[0], D)
    return item_vectors, list_loss(queries, list_ids, labels, every)


def solution(mesh):
    return jax.shard_map(
        functools.partial(local, mesh.shape["dp"], mesh.shape["groups"]),
        mesh=mesh,
        in_specs=(
            P(("groups", "dp"), None),
            P(("groups", "dp")),
            P(),
            P(),
            P(),
            P(None, None, "dp"),
            P("dp", None),
            P(),
            P(("groups", "dp"), None),
            P(("groups", "dp")),
            P(("groups", "dp"), None),
        ),
        out_specs=(P(("groups", "dp"), None), P(("groups", "dp"))),
        check_vma=False,
    )
```

```python
import functools

import jax
import jax.numpy as jnp
from jax import lax
from jax.experimental import pallas as pl
from jax.experimental.pallas import tpu as pltpu
from jax.sharding import PartitionSpec as P

D = 768
HEAD = 64
LISTS = 2
OUTER = 4
CHUNK = 256

SCORE_SCALE = HEAD ** (-0.5) * 1.4426950408889634
epsilon = 1e-06
score_scale = 32.0
MIB = 1024 * 1024
SHORT = pl.CostEstimate(flops=1000, bytes_accessed=1000, transcendentals=0)
LONG = pl.CostEstimate(flops=40_000_000_000, bytes_accessed=1000, transcendentals=0)


def inverse_rms(widened):
    return lax.rsqrt(jnp.mean(widened * widened, axis=-1, keepdims=True) + epsilon)


def nt_dot(left, right):
    return lax.dot_general(
        left, right, (((1,), (1,)), ((), ())), preferred_element_type=jnp.float32
    )


LANES = 128


def pack_kernel(expand, contract, packed, stage, come, gone):
    arrivals = [
        pltpu.make_async_copy(expand.at[which], stage.at[which], come.at[which])
        for which in range(2)
    ]
    for piece in range(D // LANES):
        columns = slice(piece * LANES, (piece + 1) * LANES)
        source, target = contract.at[:, columns], stage.at[2, columns, :]
        arrivals.append(pltpu.make_async_copy(source, target, come.at[2 + piece]))
    leavings = [
        pltpu.make_async_copy(stage.at[which], packed.at[which], gone.at[which])
        for which in range(3)
    ]
    for copy in arrivals:
        copy.start()
    for which in range(3):
        for copy in arrivals[2:] if which == 2 else arrivals[which : which + 1]:
            copy.wait()
        leavings[which].start()
    for copy in leavings:
        copy.wait()


def pack_weights(expand_weight, contract_weight):
    in_place = pl.BlockSpec(memory_space=pltpu.HBM)
    block = jax.ShapeDtypeStruct((3, D, LANES), jnp.bfloat16)
    return pl.pallas_call(
        pack_kernel,
        out_shape=block,
        in_specs=[in_place, in_place],
        out_specs=in_place,
        scratch_shapes=[
            pltpu.VMEM(block.shape, block.dtype),
            pltpu.SemaphoreType.DMA((2 + D // LANES,)),
            pltpu.SemaphoreType.DMA((3,)),
        ],
        compiler_params=pltpu.CompilerParams(vmem_limit_bytes=60 * MIB),
        name="pack_weights",
    )(expand_weight, contract_weight)


def row_tile(rows):
    return 256 if rows % 256 == 0 else rows


def live_tiles(items, lengths, tile):
    total = lengths[0]
    for item in range(1, items):
        total = total + lengths[item]
    return (total + tile - 1) // tile


def tile_rows(index, tile):
    return pl.ds(pl.multiple_of(index * tile, tile), tile)


def project_kernel(items, lengths, tokens, gains, weights, out):
    tile = row_tile(tokens.shape[0])

    def body(index, carry):
        here = tile_rows(index, tile)
        widened = tokens[here, :].astype(jnp.float32)
        x = (widened * inverse_rms(widened) * gains[0:1, :]).astype(jnp.bfloat16)
        for which in range(3):
            span = slice(which * D, (which + 1) * D)
            part = jnp.dot(x, weights[:, span], preferred_element_type=jnp.float32)
            if which == 0:
                part = part * SCORE_SCALE
            out[here, span] = part.astype(jnp.bfloat16)
        return carry

    lax.fori_loop(0, live_tiles(items, lengths, tile), body, 0)


def call(kernel, name, scalars, arrays, out_shape, scratch=(), cost=SHORT):
    whole = pl.BlockSpec(memory_space=pltpu.VMEM)
    return pl.pallas_call(
        functools.partial(kernel, scalars[0].shape[0]),
        in_specs=[pl.BlockSpec(memory_space=pltpu.SMEM)] * len(scalars) + [whole] * len(arrays),
        out_specs=jax.tree.map(lambda _: whole, out_shape),
        out_shape=out_shape,
        compiler_params=pltpu.CompilerParams(vmem_limit_bytes=24 * MIB),
        scratch_shapes=scratch,
        cost_estimate=cost,
        name=name,
    )(*scalars, *arrays)


def project(lengths, tokens, norm_gains, query_key_value):
    out = jax.ShapeDtypeStruct((tokens.shape[0], 3 * D), jnp.bfloat16)
    return call(project_kernel, "project", (lengths,), (tokens, norm_gains, query_key_value), out)


def heads_kernel(items, lengths, projected, mixed_heads):
    rows = projected.shape[0]
    tile = row_tile(rows)
    wide = 2 * HEAD
    group = D // 2
    lane = lax.broadcasted_iota(jnp.int32, (1, wide), 1) // HEAD
    ends = []
    end = 0
    for item in range(items):
        end = end + lengths[item]
        ends.append(end)
    tiles = (end + tile - 1) // tile

    def segment(position):
        return sum((position >= end).astype(jnp.int32) for end in ends)

    for keys in range(tile, rows + 1, tile):
        across = segment(lax.broadcasted_iota(jnp.int32, (1, keys), 1))

        def body(index, carry):
            row = index // 2
            here = tile_rows(row, tile)
            offset = pl.multiple_of(index % 2 * group, group)
            down = segment(row * tile + lax.broadcasted_iota(jnp.int32, (tile, 1), 0))
            same = down == across

            def columns(kind, head):
                return pl.ds(kind * D + offset + head // 2 * wide, wide)

            def scores(head):
                q = projected[here, columns(0, head)]
                q = jnp.where(lane == head % 2, q, jnp.bfloat16(0))
                return nt_dot(q, projected[:keys, columns(1, head)])

            count = group // HEAD
            ahead = scores(0)
            for head in range(count):
                logits = jnp.where(same, ahead, -1e30)
                if head + 1 < count:
                    ahead = scores(head + 1)
                highest = jnp.max(logits, axis=1, keepdims=True)
                weights = jnp.exp2((logits - highest).astype(jnp.bfloat16))
                mine = lane == head % 2
                v = jnp.where(mine, projected[:keys, columns(2, head)], jnp.bfloat16(1))
                out = jnp.dot(weights, v, preferred_element_type=jnp.float32)
                other = (1 - head % 2) * HEAD
                out = out * (1.0 / out[:, other : other + 1])
                mixed = out if head % 2 == 0 else jnp.where(mine, out, mixed)
                if head % 2 == 1:
                    mixed_heads[here, columns(0, head)] = mixed.astype(jnp.bfloat16)
            return carry

        count = keys // tile
        lax.fori_loop(0, jnp.where(tiles == count, 2 * count, 0), body, 0)


def heads(lengths, projected):
    out = jax.ShapeDtypeStruct((projected.shape[0], D), jnp.bfloat16)
    return call(heads_kernel, "heads", (lengths,), (projected,), out)


def join_kernel(items, lengths, tokens, gains, wo, mixed_heads, residual, normed):
    tile = row_tile(tokens.shape[0])

    def body(index, carry):
        here = tile_rows(index, tile)
        total = tokens[here, :].astype(jnp.float32)
        total += jnp.dot(mixed_heads[here, :], wo[...], preferred_element_type=jnp.float32)
        rounded = total.astype(jnp.bfloat16)
        residual[here, :] = rounded
        widened = rounded.astype(jnp.float32)
        normed[here, :] = (widened * inverse_rms(widened) * gains[1:2, :]).astype(jnp.bfloat16)
        return carry

    lax.fori_loop(0, live_tiles(items, lengths, tile), body, 0)


def join_heads(lengths, *arrays):
    rows = jax.ShapeDtypeStruct(arrays[0].shape, jnp.bfloat16)
    return call(join_kernel, "join_heads", (lengths,), arrays, (rows, rows))


def grow(block_group, which):
    return jnp.concatenate([block[which] for block in block_group], axis=1)


def shrink(block_group):
    rows = []
    for block in block_group:
        pieces = [block[2, i : i + LANES, :] for i in range(0, D, LANES)]
        rows.append(jnp.concatenate(pieces, axis=1))
    return jnp.concatenate(rows, axis=0)


def hidden_units(rows, blocks, finish):
    each = CHUNK // LANES
    groups = [blocks[start : start + each] for start in range(0, len(blocks), each)]
    work = [(tile, group) for tile in range(len(rows)) for group in range(len(groups))]

    def expand(tile, group):
        gate = jnp.dot(rows[tile], grow(groups[group], 0), preferred_element_type=jnp.float32)
        up = jnp.dot(rows[tile], grow(groups[group], 1), preferred_element_type=jnp.float32)
        return gate, up

    ahead = expand(*work[0])
    for number, (tile, group) in enumerate(work):
        gate, up = ahead
        if number + 1 < len(work):
            ahead = expand(*work[number + 1])
        active = (jax.nn.gelu(gate, approximate=True) * up).astype(jnp.bfloat16)
        term = jnp.dot(active, shrink(groups[group]), preferred_element_type=jnp.float32)
        grown = term if group == 0 else grown + term
        if group == len(groups) - 1:
            finish(tile, grown)


def all_tiles(tiles, every, tile, run):
    def body(index, carry):
        run([tile_rows(index, tile)])
        return carry

    lax.fori_loop(0, jnp.where(tiles == every, 0, tiles), body, 0)

    @pl.when(tiles == every)
    def _():
        run([slice(index * tile, (index + 1) * tile) for index in range(every)])


def first_kernel(items, lengths, x, *refs):
    blocks, total = refs[:-1], refs[-1]
    tile = row_tile(x.shape[0])

    def run(spans):
        def finish(number, grown):
            total[spans[number], :] = grown

        hidden_units([x[span, :] for span in spans], blocks, finish)

    all_tiles(live_tiles(items, lengths, tile), x.shape[0] // tile, tile, run)


def first_units(lengths, normed, blocks):
    out = jax.ShapeDtypeStruct(normed.shape, jnp.float32)
    return call(first_kernel, "first_units", (lengths,), (normed, *blocks), out, cost=LONG)


def their_last_kernel(items, lengths, x, before, *refs):
    blocks, total = refs[:-1], refs[-1]
    tile = row_tile(x.shape[0])

    def run(spans):
        def finish(number, grown):
            span = spans[number]
            total[span, :] = (before[span, :] + grown).astype(jnp.bfloat16)

        hidden_units([x[span, :] for span in spans], blocks, finish)

    all_tiles(live_tiles(items, lengths, tile), x.shape[0] // tile, tile, run)


def their_last_units(lengths, normed, before, blocks):
    out = jax.ShapeDtypeStruct(normed.shape, jnp.bfloat16)
    return call(their_last_kernel, "their_last_units", (lengths,), (normed, before, *blocks), out)


def own_last_kernel(items, lengths, residual, x, before, *refs):
    blocks, total = refs[:-1], refs[-1]
    tile = row_tile(x.shape[0])

    def run(spans):
        def finish(number, grown):
            span = spans[number]
            total[span, :] = before[span, :] + residual[span, :].astype(jnp.float32) + grown

        hidden_units([x[span, :] for span in spans], blocks, finish)

    all_tiles(live_tiles(items, lengths, tile), x.shape[0] // tile, tile, run)


def own_last_units(lengths, residual, normed, before, blocks):
    out = jax.ShapeDtypeStruct(normed.shape, jnp.float32)
    arrays = (residual, normed, before, *blocks)
    return call(own_last_kernel, "own_last_units", (lengths,), arrays, out)


def pool_kernel(items, lengths, gains, pool, own_total, back, vectors, candidates, summed):
    tile = row_tile(own_total.shape[0])
    every = own_total.shape[0] // tile
    tiles = live_tiles(items, lengths, tile)
    slots = 16
    slot = lax.broadcasted_iota(jnp.int32, (slots, 1), 0)
    first = jnp.zeros((slots, 1), jnp.int32)
    last = jnp.zeros((slots, 1), jnp.int32)
    begin = 0
    for item in range(items):
        end = begin + lengths[item]
        first = jnp.where(slot == item, begin, first)
        last = jnp.where(slot == item, end, last)
        begin = end

    def pool_tile(index):
        here = tile_rows(index, tile)
        total = own_total[here, :] + back[here, :].astype(jnp.float32)
        finished = total.astype(jnp.bfloat16).astype(jnp.float32)
        final_rows = (finished * inverse_rms(finished) * gains[2:3, :]).astype(jnp.bfloat16)
        across = index * tile + lax.broadcasted_iota(jnp.int32, (slots, tile), 1)
        member = jnp.where((across >= first) & (across < last), 1.0, 0.0)
        return jnp.dot(member.astype(jnp.bfloat16), final_rows, preferred_element_type=jnp.float32)

    def body(index, carry):
        summed[...] += pool_tile(index)
        return carry

    @pl.when(tiles < every)
    def _():
        summed[...] = jnp.zeros((slots, D), jnp.float32)

    lax.fori_loop(0, jnp.where(tiles < every, tiles, 0), body, 0)

    @pl.when(tiles == every)
    def _():
        summed[...] = sum(pool_tile(index) for index in range(every))

    counts = jnp.maximum(last - first, 1).astype(jnp.float32)
    pooled = (summed[...] / counts).astype(jnp.bfloat16)
    e = jnp.dot(pooled, pool[...], preferred_element_type=jnp.float32)
    e = e * inverse_rms(e)
    vectors[...] = e[:items, :]
    mine = e[:items, :].astype(jnp.bfloat16)
    for device in range(candidates.shape[0]):
        candidates[device] = mine


def pool_items(devices, lengths, *arrays):
    items = lengths.shape[0]
    out = (
        jax.ShapeDtypeStruct((items, D), jnp.float32),
        jax.ShapeDtypeStruct((devices, items, D), jnp.bfloat16),
    )
    scratch = [pltpu.VMEM((16, D), jnp.float32)]
    return call(pool_kernel, "pool_items", (lengths,), arrays, out, scratch)


def loss_kernel(queries, list_ids, labels, candidates, loss):
    widened = queries[...].astype(jnp.float32)
    query_unit = (widened * inverse_rms(widened)).astype(jnp.bfloat16)
    each = labels.shape[0]
    chosen = None
    for which in range(LISTS):
        scores = nt_dot(candidates[which * each : (which + 1) * each, :], query_unit)
        if chosen is None:
            chosen = scores
        else:
            chosen = jnp.where(list_ids[...] == which, scores, chosen)
    chosen = chosen * (score_scale / D)
    target = jnp.exp(labels[...].astype(jnp.float32))
    target = target / jnp.sum(target, axis=0, keepdims=True)
    log_total = jnp.log(jnp.sum(jnp.exp(chosen), axis=0, keepdims=True))
    loss[...] = log_total - jnp.sum(target * chosen, axis=0, keepdims=True)


def list_loss(queries, list_ids, labels, candidates):
    count = queries.shape[0]
    return pl.pallas_call(
        loss_kernel,
        out_shape=jax.ShapeDtypeStruct((1, count), jnp.float32),
        compiler_params=pltpu.CompilerParams(vmem_limit_bytes=16 * MIB),
        name="list_loss",
    )(queries, list_ids.reshape(1, count), labels.T, candidates).reshape(count)


def swapped(value, count, bit):
    return lax.ppermute(value, "dp", [(i, i ^ bit) for i in range(count)])


def after(value, *earlier):
    return lax.optimization_barrier((value, earlier))[0]


def local(
    count,
    planes,
    tokens,
    lengths,
    norm_gains,
    query_key_value,
    attention_out,
    expand_weight,
    contract_weight,
    pool_weight,
    queries,
    list_ids,
    labels,
):
    inner = count // OUTER
    counts = [lengths, swapped(lengths, count, 1)]

    def attend(turn):
        projected = project(lengths, tokens, norm_gains, query_key_value)
        projected, counts[1] = turn(0, (projected, counts[1]))
        mixed_heads = heads(lengths, projected)
        residual, normed = join_heads(lengths, tokens, norm_gains, attention_out, mixed_heads)
        return residual, turn(1, normed), swapped(normed, count, 1)

    same_core = [list(range(first, count, 2)) for first in range(2)]
    if planes == 2 and inner == 4 and contract_weight.shape[0] == LANES:

        def hop(value, same, across, crossed):
            pairs = []
            for here in range(planes * count):
                y, place = divmod(here, count)
                z, x, c = place // inner, place % inner // 2, place % 2
                role = 0 if c == y else 1
                link = across if role else same
                if link == "y":
                    y = 1 - y
                elif link == "x":
                    x = 1 - x
                else:
                    z = (z + (1 if link == "up" else OUTER - 1)) % OUTER
                role = 1 - role if crossed else role
                pairs.append((here, y * count + z * inner + x * 2 + (1 - y if role else y)))
            return lax.ppermute(value, ("groups", "dp"), pairs)

        v = [pack_weights(expand_weight, contract_weight)]
        v.append(hop(v[0], "x", "up", True))

        def turn(number, value):
            if number == 0:
                v[1], value = after((v[1], value))
                v.append(hop(v[1], "up", "down", False))
                v.append(hop(v[1], "y", "up", False))
                v.append(hop(v[1], "x", "y", False))
            else:
                v[2], value = after((v[2], value))
                v.append(hop(v[2], "up", "y", False))
                v.append(hop(v[2], "x", "x", False))
                v.append(hop(v[2], "y", "down", False))
            return value

        residual, normed, theirs = attend(turn)
        first = tuple(v[:5])
        third = tuple(v[5:8])
        own_sum = first_units(lengths, normed, first)
    else:
        grown = lax.all_gather(
            expand_weight, "dp", axis=2, tiled=True, axis_index_groups=same_core
        )
        shrunk = lax.all_gather(
            contract_weight, "dp", axis=0, tiled=True, axis_index_groups=same_core
        )
        grown = grown.reshape(2, D, -1, LANES).transpose(2, 0, 1, 3)
        shrunk = shrunk.reshape(-1, LANES, D // LANES, LANES).transpose(0, 2, 1, 3)
        v = jnp.concatenate([grown, shrunk.reshape(-1, 1, D, LANES)], axis=1)
        residual, normed, theirs = attend(lambda number, value: value)
        first = tuple(v[:5])
        third = tuple(v[5:])
        own_sum = first_units(lengths, normed, first)

    their_sum = first_units(counts[1], theirs, first)
    third, their_sum = after((third, their_sum), own_sum)
    their_total = their_last_units(counts[1], theirs, their_sum, third)
    back = swapped(their_total, count, 1)
    normed, _ = after((normed, their_total))
    own_total = own_last_units(lengths, residual, normed, own_sum, third)
    item_vectors, candidates = pool_items(
        count, lengths, norm_gains, pool_weight, own_total, back
    )
    every = lax.all_to_all(candidates, "dp", 0, 0, tiled=True)
    every = every.reshape(count * lengths.shape[0], D)
    return item_vectors, list_loss(queries, list_ids, labels, every)


def solution(mesh):
    return jax.shard_map(
        functools.partial(local, mesh.shape["dp"], mesh.shape["groups"]),
        mesh=mesh,
        in_specs=(
            P(("groups", "dp"), None),
            P(("groups", "dp")),
            P(),
            P(),
            P(),
            P(None, None, "dp"),
            P("dp", None),
            P(),
            P(("groups", "dp"), None),
            P(("groups", "dp")),
            P(("groups", "dp"), None),
        ),
        out_specs=(P(("groups", "dp"), None), P(("groups", "dp"))),
        check_vma=False,
    )
```

```python
import functools

import jax
import jax.numpy as jnp
from jax import lax
from jax.experimental import pallas as pl
from jax.experimental.pallas import tpu as pltpu
from jax.sharding import PartitionSpec as P

D = 768
HEAD = 64
LISTS = 2
OUTER = 4
CHUNK = 256

SCORE_SCALE = HEAD ** (-0.5) * 1.4426950408889634
epsilon = 1e-06
score_scale = 32.0
MIB = 1024 * 1024
SHORT = pl.CostEstimate(flops=1000, bytes_accessed=1000, transcendentals=0)
LONG = pl.CostEstimate(flops=40_000_000_000, bytes_accessed=1000, transcendentals=0)


def inverse_rms(widened):
    return lax.rsqrt(jnp.mean(widened * widened, axis=-1, keepdims=True) + epsilon)


def nt_dot(left, right):
    return lax.dot_general(
        left, right, (((1,), (1,)), ((), ())), preferred_element_type=jnp.float32
    )


LANES = 128


def pack_kernel(expand, contract, packed, stage, come, gone):
    arrivals = [
        pltpu.make_async_copy(expand.at[which], stage.at[which], come.at[which])
        for which in range(2)
    ]
    for piece in range(D // LANES):
        columns = slice(piece * LANES, (piece + 1) * LANES)
        source, target = contract.at[:, columns], stage.at[2, columns, :]
        arrivals.append(pltpu.make_async_copy(source, target, come.at[2 + piece]))
    leavings = [
        pltpu.make_async_copy(stage.at[which], packed.at[which], gone.at[which])
        for which in range(3)
    ]
    for copy in arrivals:
        copy.start()
    for which in range(3):
        for copy in arrivals[2:] if which == 2 else arrivals[which : which + 1]:
            copy.wait()
        leavings[which].start()
    for copy in leavings:
        copy.wait()


def pack_weights(expand_weight, contract_weight):
    in_place = pl.BlockSpec(memory_space=pltpu.HBM)
    block = jax.ShapeDtypeStruct((3, D, LANES), jnp.bfloat16)
    return pl.pallas_call(
        pack_kernel,
        out_shape=block,
        in_specs=[in_place, in_place],
        out_specs=in_place,
        scratch_shapes=[
            pltpu.VMEM(block.shape, block.dtype),
            pltpu.SemaphoreType.DMA((2 + D // LANES,)),
            pltpu.SemaphoreType.DMA((3,)),
        ],
        compiler_params=pltpu.CompilerParams(vmem_limit_bytes=60 * MIB),
        name="pack_weights",
    )(expand_weight, contract_weight)


def row_tile(rows):
    return 256 if rows % 256 == 0 else rows


def live_tiles(items, lengths, tile):
    total = lengths[0]
    for item in range(1, items):
        total = total + lengths[item]
    return (total + tile - 1) // tile


def tile_rows(index, tile):
    return pl.ds(pl.multiple_of(index * tile, tile), tile)


def project_kernel(items, lengths, tokens, gains, weights, out):
    tile = row_tile(tokens.shape[0])

    def body(index, carry):
        here = tile_rows(index, tile)
        widened = tokens[here, :].astype(jnp.float32)
        x = (widened * inverse_rms(widened) * gains[0:1, :]).astype(jnp.bfloat16)
        for which in range(3):
            span = slice(which * D, (which + 1) * D)
            part = jnp.dot(x, weights[:, span], preferred_element_type=jnp.float32)
            if which == 0:
                part = part * SCORE_SCALE
            out[here, span] = part.astype(jnp.bfloat16)
        return carry

    lax.fori_loop(0, live_tiles(items, lengths, tile), body, 0)


def call(kernel, name, scalars, arrays, out_shape, scratch=(), cost=SHORT):
    whole = pl.BlockSpec(memory_space=pltpu.VMEM)
    return pl.pallas_call(
        functools.partial(kernel, scalars[0].shape[0]),
        in_specs=[pl.BlockSpec(memory_space=pltpu.SMEM)] * len(scalars) + [whole] * len(arrays),
        out_specs=jax.tree.map(lambda _: whole, out_shape),
        out_shape=out_shape,
        compiler_params=pltpu.CompilerParams(vmem_limit_bytes=24 * MIB),
        scratch_shapes=scratch,
        cost_estimate=cost,
        name=name,
    )(*scalars, *arrays)


def project(lengths, tokens, norm_gains, query_key_value):
    out = jax.ShapeDtypeStruct((tokens.shape[0], 3 * D), jnp.bfloat16)
    return call(project_kernel, "project", (lengths,), (tokens, norm_gains, query_key_value), out)


def heads_kernel(items, lengths, projected, mixed_heads):
    rows = projected.shape[0]
    tile = row_tile(rows)
    wide = 2 * HEAD
    group = D // 2
    lane = lax.broadcasted_iota(jnp.int32, (1, wide), 1) // HEAD
    ends = []
    end = 0
    for item in range(items):
        end = end + lengths[item]
        ends.append(end)
    tiles = (end + tile - 1) // tile

    def segment(position):
        return sum((position >= end).astype(jnp.int32) for end in ends)

    for keys in range(tile, rows + 1, tile):
        across = segment(lax.broadcasted_iota(jnp.int32, (1, keys), 1))

        def body(index, carry):
            row = index // 2
            here = tile_rows(row, tile)
            offset = pl.multiple_of(index % 2 * group, group)
            down = segment(row * tile + lax.broadcasted_iota(jnp.int32, (tile, 1), 0))
            same = down == across

            def columns(kind, head):
                return pl.ds(kind * D + offset + head // 2 * wide, wide)

            def scores(head):
                q = projected[here, columns(0, head)]
                q = jnp.where(lane == head % 2, q, jnp.bfloat16(0))
                return nt_dot(q, projected[:keys, columns(1, head)])

            count = group // HEAD
            ahead = scores(0)
            for head in range(count):
                logits = jnp.where(same, ahead, -1e30)
                if head + 1 < count:
                    ahead = scores(head + 1)
                highest = jnp.max(logits, axis=1, keepdims=True)
                weights = jnp.exp2((logits - highest).astype(jnp.bfloat16))
                mine = lane == head % 2
                v = jnp.where(mine, projected[:keys, columns(2, head)], jnp.bfloat16(1))
                out = jnp.dot(weights, v, preferred_element_type=jnp.float32)
                other = (1 - head % 2) * HEAD
                out = out * (1.0 / out[:, other : other + 1])
                mixed = out if head % 2 == 0 else jnp.where(mine, out, mixed)
                if head % 2 == 1:
                    mixed_heads[here, columns(0, head)] = mixed.astype(jnp.bfloat16)
            return carry

        count = keys // tile
        lax.fori_loop(0, jnp.where(tiles == count, 2 * count, 0), body, 0)


def heads(lengths, projected):
    out = jax.ShapeDtypeStruct((projected.shape[0], D), jnp.bfloat16)
    return call(heads_kernel, "heads", (lengths,), (projected,), out)


def join_kernel(items, lengths, tokens, gains, wo, mixed_heads, residual, normed):
    tile = row_tile(tokens.shape[0])

    def body(index, carry):
        here = tile_rows(index, tile)
        total = tokens[here, :].astype(jnp.float32)
        total += jnp.dot(mixed_heads[here, :], wo[...], preferred_element_type=jnp.float32)
        rounded = total.astype(jnp.bfloat16)
        residual[here, :] = rounded
        widened = rounded.astype(jnp.float32)
        normed[here, :] = (widened * inverse_rms(widened) * gains[1:2, :]).astype(jnp.bfloat16)
        return carry

    lax.fori_loop(0, live_tiles(items, lengths, tile), body, 0)


def join_heads(lengths, *arrays):
    rows = jax.ShapeDtypeStruct(arrays[0].shape, jnp.bfloat16)
    return call(join_kernel, "join_heads", (lengths,), arrays, (rows, rows))


def grow(block_group, which):
    return jnp.concatenate([block[which] for block in block_group], axis=1)


def shrink(block_group):
    rows = []
    for block in block_group:
        pieces = [block[2, i : i + LANES, :] for i in range(0, D, LANES)]
        rows.append(jnp.concatenate(pieces, axis=1))
    return jnp.concatenate(rows, axis=0)


def hidden_units(rows, blocks, finish):
    each = CHUNK // LANES
    groups = [blocks[start : start + each] for start in range(0, len(blocks), each)]
    work = [(tile, group) for tile in range(len(rows)) for group in range(len(groups))]

    def expand(tile, group):
        gate = jnp.dot(rows[tile], grow(groups[group], 0), preferred_element_type=jnp.float32)
        up = jnp.dot(rows[tile], grow(groups[group], 1), preferred_element_type=jnp.float32)
        return gate, up

    ahead = expand(*work[0])
    for number, (tile, group) in enumerate(work):
        gate, up = ahead
        if number + 1 < len(work):
            ahead = expand(*work[number + 1])
        active = (jax.nn.gelu(gate, approximate=True) * up).astype(jnp.bfloat16)
        term = jnp.dot(active, shrink(groups[group]), preferred_element_type=jnp.float32)
        grown = term if group == 0 else grown + term
        if group == len(groups) - 1:
            finish(tile, grown)


def all_tiles(tiles, every, tile, run):
    def body(index, carry):
        run([tile_rows(index, tile)])
        return carry

    lax.fori_loop(0, jnp.where(tiles == every, 0, tiles), body, 0)

    @pl.when(tiles == every)
    def _():
        run([slice(index * tile, (index + 1) * tile) for index in range(every)])


def first_kernel(items, lengths, x, *refs):
    blocks, total = refs[:-1], refs[-1]
    tile = row_tile(x.shape[0])

    def run(spans):
        def finish(number, grown):
            total[spans[number], :] = grown

        hidden_units([x[span, :] for span in spans], blocks, finish)

    all_tiles(live_tiles(items, lengths, tile), x.shape[0] // tile, tile, run)


def first_units(lengths, normed, blocks):
    out = jax.ShapeDtypeStruct(normed.shape, jnp.float32)
    return call(first_kernel, "first_units", (lengths,), (normed, *blocks), out, cost=LONG)


def their_last_kernel(items, lengths, x, before, *refs):
    blocks, total = refs[:-1], refs[-1]
    tile = row_tile(x.shape[0])

    def run(spans):
        def finish(number, grown):
            span = spans[number]
            total[span, :] = (before[span, :] + grown).astype(jnp.bfloat16)

        hidden_units([x[span, :] for span in spans], blocks, finish)

    all_tiles(live_tiles(items, lengths, tile), x.shape[0] // tile, tile, run)


def their_last_units(lengths, normed, before, blocks):
    out = jax.ShapeDtypeStruct(normed.shape, jnp.bfloat16)
    return call(their_last_kernel, "their_last_units", (lengths,), (normed, before, *blocks), out)


def own_last_kernel(items, lengths, residual, x, before, *refs):
    blocks, total = refs[:-1], refs[-1]
    tile = row_tile(x.shape[0])

    def run(spans):
        def finish(number, grown):
            span = spans[number]
            total[span, :] = before[span, :] + residual[span, :].astype(jnp.float32) + grown

        hidden_units([x[span, :] for span in spans], blocks, finish)

    all_tiles(live_tiles(items, lengths, tile), x.shape[0] // tile, tile, run)


def own_last_units(lengths, residual, normed, before, blocks):
    out = jax.ShapeDtypeStruct(normed.shape, jnp.float32)
    arrays = (residual, normed, before, *blocks)
    return call(own_last_kernel, "own_last_units", (lengths,), arrays, out)


def pool_kernel(items, lengths, gains, pool, own_total, back, vectors, candidates, summed):
    tile = row_tile(own_total.shape[0])
    every = own_total.shape[0] // tile
    tiles = live_tiles(items, lengths, tile)
    slots = 16
    slot = lax.broadcasted_iota(jnp.int32, (slots, 1), 0)
    first = jnp.zeros((slots, 1), jnp.int32)
    last = jnp.zeros((slots, 1), jnp.int32)
    begin = 0
    for item in range(items):
        end = begin + lengths[item]
        first = jnp.where(slot == item, begin, first)
        last = jnp.where(slot == item, end, last)
        begin = end

    def pool_tile(index):
        here = tile_rows(index, tile)
        total = own_total[here, :] + back[here, :].astype(jnp.float32)
        finished = total.astype(jnp.bfloat16).astype(jnp.float32)
        final_rows = (finished * inverse_rms(finished) * gains[2:3, :]).astype(jnp.bfloat16)
        across = index * tile + lax.broadcasted_iota(jnp.int32, (slots, tile), 1)
        member = jnp.where((across >= first) & (across < last), 1.0, 0.0)
        return jnp.dot(member.astype(jnp.bfloat16), final_rows, preferred_element_type=jnp.float32)

    def body(index, carry):
        summed[...] += pool_tile(index)
        return carry

    @pl.when(tiles < every)
    def _():
        summed[...] = jnp.zeros((slots, D), jnp.float32)

    lax.fori_loop(0, jnp.where(tiles < every, tiles, 0), body, 0)

    @pl.when(tiles == every)
    def _():
        summed[...] = sum(pool_tile(index) for index in range(every))

    counts = jnp.maximum(last - first, 1).astype(jnp.float32)
    pooled = (summed[...] / counts).astype(jnp.bfloat16)
    e = jnp.dot(pooled, pool[...], preferred_element_type=jnp.float32)
    e = e * inverse_rms(e)
    vectors[...] = e[:items, :]
    mine = e[:items, :].astype(jnp.bfloat16)
    for device in range(candidates.shape[0]):
        candidates[device] = mine


def pool_items(devices, lengths, *arrays):
    items = lengths.shape[0]
    out = (
        jax.ShapeDtypeStruct((items, D), jnp.float32),
        jax.ShapeDtypeStruct((devices, items, D), jnp.bfloat16),
    )
    scratch = [pltpu.VMEM((16, D), jnp.float32)]
    return call(pool_kernel, "pool_items", (lengths,), arrays, out, scratch)


def loss_kernel(items, queries, list_ids, labels, candidates, loss):
    widened = queries[...].astype(jnp.float32)
    query_unit = (widened * inverse_rms(widened)).astype(jnp.bfloat16)
    each = labels.shape[0]
    chosen = None
    for which in range(LISTS):
        place = LISTS - 1 - which
        scores = nt_dot(candidates[place * each : (place + 1) * each, :], query_unit)
        if chosen is None:
            chosen = scores
        else:
            chosen = jnp.where(list_ids[...] == which, scores, chosen)
    chosen = chosen * (score_scale / D)
    relevance = labels[...]
    relevance = jnp.concatenate(
        [relevance[start : start + items, :] for start in range(each - items, -1, -items)], axis=0
    )
    target = jnp.exp(relevance.astype(jnp.float32))
    target = target / jnp.sum(target, axis=0, keepdims=True)
    log_total = jnp.log(jnp.sum(jnp.exp(chosen), axis=0, keepdims=True))
    loss[...] = log_total - jnp.sum(target * chosen, axis=0, keepdims=True)


def list_loss(items, queries, list_ids, labels, candidates):
    count = queries.shape[0]
    return pl.pallas_call(
        functools.partial(loss_kernel, items),
        out_shape=jax.ShapeDtypeStruct((1, count), jnp.float32),
        compiler_params=pltpu.CompilerParams(vmem_limit_bytes=16 * MIB),
        name="list_loss",
    )(queries, list_ids.reshape(1, count), labels.T, candidates).reshape(count)


def swapped(value, count, bit):
    return lax.ppermute(value, "dp", [(i, i ^ bit) for i in range(count)])


def after(value, *earlier):
    return lax.optimization_barrier((value, earlier))[0]


def local(
    count,
    planes,
    tokens,
    lengths,
    norm_gains,
    query_key_value,
    attention_out,
    expand_weight,
    contract_weight,
    pool_weight,
    queries,
    list_ids,
    labels,
):
    inner = count // OUTER
    counts = [lengths, swapped(lengths, count, 1)]

    def attend(turn):
        projected = project(lengths, tokens, norm_gains, query_key_value)
        projected, counts[1] = turn(0, (projected, counts[1]))
        mixed_heads = heads(lengths, projected)
        residual, normed = join_heads(lengths, tokens, norm_gains, attention_out, mixed_heads)
        return residual, turn(1, normed), swapped(normed, count, 1)

    same_core = [list(range(first, count, 2)) for first in range(2)]
    if planes == 2 and inner == 4 and contract_weight.shape[0] == LANES:

        def hop(value, same, across, crossed):
            pairs = []
            for here in range(planes * count):
                y, place = divmod(here, count)
                z, x, c = place // inner, place % inner // 2, place % 2
                role = 0 if c == y else 1
                link = across if role else same
                if link == "y":
                    y = 1 - y
                elif link == "x":
                    x = 1 - x
                else:
                    z = (z + (1 if link == "up" else OUTER - 1)) % OUTER
                role = 1 - role if crossed else role
                pairs.append((here, y * count + z * inner + x * 2 + (1 - y if role else y)))
            return lax.ppermute(value, ("groups", "dp"), pairs)

        v = [pack_weights(expand_weight, contract_weight)]
        v.append(hop(v[0], "x", "up", True))

        def turn(number, value):
            if number == 0:
                v[1], value = after((v[1], value))
                v.append(hop(v[1], "up", "down", False))
                v.append(hop(v[1], "y", "up", False))
                v.append(hop(v[1], "x", "y", False))
            else:
                v[2], value = after((v[2], value))
                v.append(hop(v[2], "up", "y", False))
                v.append(hop(v[2], "x", "x", False))
                v.append(hop(v[2], "y", "down", False))
            return value

        residual, normed, theirs = attend(turn)
        first = tuple(v[:5])
        third = tuple(v[5:8])
        own_sum = first_units(lengths, normed, first)
    else:
        grown = lax.all_gather(
            expand_weight, "dp", axis=2, tiled=True, axis_index_groups=same_core
        )
        shrunk = lax.all_gather(
            contract_weight, "dp", axis=0, tiled=True, axis_index_groups=same_core
        )
        grown = grown.reshape(2, D, -1, LANES).transpose(2, 0, 1, 3)
        shrunk = shrunk.reshape(-1, LANES, D // LANES, LANES).transpose(0, 2, 1, 3)
        v = jnp.concatenate([grown, shrunk.reshape(-1, 1, D, LANES)], axis=1)
        residual, normed, theirs = attend(lambda number, value: value)
        first = tuple(v[:5])
        third = tuple(v[5:])
        own_sum = first_units(lengths, normed, first)

    their_sum = first_units(counts[1], theirs, first)
    third, their_sum = after((third, their_sum), own_sum)
    their_total = their_last_units(counts[1], theirs, their_sum, third)
    back = swapped(their_total, count, 1)
    normed, _ = after((normed, their_total))
    own_total = own_last_units(lengths, residual, normed, own_sum, third)
    item_vectors, candidates = pool_items(
        count, lengths, norm_gains, pool_weight, own_total, back
    )
    backwards = [list(range(count - 1, -1, -1))]
    every = lax.all_to_all(
        candidates, "dp", 0, 0, tiled=True, axis_index_groups=backwards
    )
    every = every.reshape(count * lengths.shape[0], D)
    return item_vectors, list_loss(lengths.shape[0], queries, list_ids, labels, every)


def solution(mesh):
    return jax.shard_map(
        functools.partial(local, mesh.shape["dp"], mesh.shape["groups"]),
        mesh=mesh,
        in_specs=(
            P(("groups", "dp"), None),
            P(("groups", "dp")),
            P(),
            P(),
            P(),
            P(None, None, "dp"),
            P("dp", None),
            P(),
            P(("groups", "dp"), None),
            P(("groups", "dp")),
            P(("groups", "dp"), None),
        ),
        out_specs=(P(("groups", "dp"), None), P(("groups", "dp"))),
        check_vma=False,
    )
```

```python
import functools

import jax
import jax.numpy as jnp
from jax import lax
from jax.experimental import pallas as pl
from jax.experimental.pallas import tpu as pltpu
from jax.sharding import PartitionSpec as P

D = 768
HEAD = 64
LISTS = 2
OUTER = 4
CHUNK = 256

SCORE_SCALE = HEAD ** (-0.5) * 1.4426950408889634
epsilon = 1e-06
score_scale = 32.0
MIB = 1024 * 1024
SHORT = pl.CostEstimate(flops=1000, bytes_accessed=1000, transcendentals=0)
LONG = pl.CostEstimate(flops=40_000_000_000, bytes_accessed=1000, transcendentals=0)


def inverse_rms(widened):
    return lax.rsqrt(jnp.mean(widened * widened, axis=-1, keepdims=True) + epsilon)


def nt_dot(left, right):
    return lax.dot_general(
        left, right, (((1,), (1,)), ((), ())), preferred_element_type=jnp.float32
    )


LANES = 128


def pack_kernel(expand, contract, packed, stage, come, gone):
    arrivals = [
        pltpu.make_async_copy(expand.at[which], stage.at[which], come.at[which])
        for which in range(2)
    ]
    for piece in range(D // LANES):
        columns = slice(piece * LANES, (piece + 1) * LANES)
        source, target = contract.at[:, columns], stage.at[2, columns, :]
        arrivals.append(pltpu.make_async_copy(source, target, come.at[2 + piece]))
    leavings = [
        pltpu.make_async_copy(stage.at[which], packed.at[which], gone.at[which])
        for which in range(3)
    ]
    for copy in arrivals:
        copy.start()
    for which in range(3):
        for copy in arrivals[2:] if which == 2 else arrivals[which : which + 1]:
            copy.wait()
        leavings[which].start()
    for copy in leavings:
        copy.wait()


def pack_weights(expand_weight, contract_weight):
    in_place = pl.BlockSpec(memory_space=pltpu.HBM)
    block = jax.ShapeDtypeStruct((3, D, LANES), jnp.bfloat16)
    return pl.pallas_call(
        pack_kernel,
        out_shape=block,
        in_specs=[in_place, in_place],
        out_specs=in_place,
        scratch_shapes=[
            pltpu.VMEM(block.shape, block.dtype),
            pltpu.SemaphoreType.DMA((2 + D // LANES,)),
            pltpu.SemaphoreType.DMA((3,)),
        ],
        compiler_params=pltpu.CompilerParams(vmem_limit_bytes=60 * MIB),
        name="pack_weights",
    )(expand_weight, contract_weight)


def row_tile(rows):
    return 256 if rows % 256 == 0 else rows


def live_tiles(items, lengths, tile):
    total = lengths[0]
    for item in range(1, items):
        total = total + lengths[item]
    return (total + tile - 1) // tile


def tile_rows(index, tile):
    return pl.ds(pl.multiple_of(index * tile, tile), tile)


def project_kernel(items, lengths, tokens, gains, weights, out):
    tile = row_tile(tokens.shape[0])

    def body(index, carry):
        here = tile_rows(index, tile)
        widened = tokens[here, :].astype(jnp.float32)
        x = (widened * inverse_rms(widened) * gains[0:1, :]).astype(jnp.bfloat16)
        for which in range(3):
            span = slice(which * D, (which + 1) * D)
            part = jnp.dot(x, weights[:, span], preferred_element_type=jnp.float32)
            if which == 0:
                part = part * SCORE_SCALE
            out[here, span] = part.astype(jnp.bfloat16)
        return carry

    lax.fori_loop(0, live_tiles(items, lengths, tile), body, 0)


def call(kernel, name, scalars, arrays, out_shape, scratch=(), cost=SHORT):
    whole = pl.BlockSpec(memory_space=pltpu.VMEM)
    return pl.pallas_call(
        functools.partial(kernel, scalars[0].shape[0]),
        in_specs=[pl.BlockSpec(memory_space=pltpu.SMEM)] * len(scalars) + [whole] * len(arrays),
        out_specs=jax.tree.map(lambda _: whole, out_shape),
        out_shape=out_shape,
        compiler_params=pltpu.CompilerParams(vmem_limit_bytes=24 * MIB),
        scratch_shapes=scratch,
        cost_estimate=cost,
        name=name,
    )(*scalars, *arrays)


def project(lengths, tokens, norm_gains, query_key_value):
    out = jax.ShapeDtypeStruct((tokens.shape[0], 3 * D), jnp.bfloat16)
    return call(project_kernel, "project", (lengths,), (tokens, norm_gains, query_key_value), out)


def heads_kernel(items, lengths, projected, mixed_heads):
    rows = projected.shape[0]
    tile = row_tile(rows)
    wide = 2 * HEAD
    group = D // 2
    lane = lax.broadcasted_iota(jnp.int32, (1, wide), 1) // HEAD
    ends = []
    end = 0
    for item in range(items):
        end = end + lengths[item]
        ends.append(end)
    tiles = (end + tile - 1) // tile

    def segment(position):
        return sum((position >= end).astype(jnp.int32) for end in ends)

    for keys in range(tile, rows + 1, tile):
        across = segment(lax.broadcasted_iota(jnp.int32, (1, keys), 1))

        def body(index, carry):
            row = index // 2
            here = tile_rows(row, tile)
            offset = pl.multiple_of(index % 2 * group, group)
            down = segment(row * tile + lax.broadcasted_iota(jnp.int32, (tile, 1), 0))
            same = down == across

            def columns(kind, head):
                return pl.ds(kind * D + offset + head // 2 * wide, wide)

            def scores(head):
                q = projected[here, columns(0, head)]
                q = jnp.where(lane == head % 2, q, jnp.bfloat16(0))
                return nt_dot(q, projected[:keys, columns(1, head)])

            count = group // HEAD
            ahead = scores(0)
            for head in range(count):
                logits = jnp.where(same, ahead, -1e30)
                if head + 1 < count:
                    ahead = scores(head + 1)
                highest = jnp.max(logits, axis=1, keepdims=True)
                weights = jnp.exp2((logits - highest).astype(jnp.bfloat16))
                mine = lane == head % 2
                v = jnp.where(mine, projected[:keys, columns(2, head)], jnp.bfloat16(1))
                out = jnp.dot(weights, v, preferred_element_type=jnp.float32)
                other = (1 - head % 2) * HEAD
                out = out * (1.0 / out[:, other : other + 1])
                mixed = out if head % 2 == 0 else jnp.where(mine, out, mixed)
                if head % 2 == 1:
                    mixed_heads[here, columns(0, head)] = mixed.astype(jnp.bfloat16)
            return carry

        count = keys // tile
        lax.fori_loop(0, jnp.where(tiles == count, 2 * count, 0), body, 0)


def heads(lengths, projected):
    out = jax.ShapeDtypeStruct((projected.shape[0], D), jnp.bfloat16)
    return call(heads_kernel, "heads", (lengths,), (projected,), out)


def join_kernel(items, lengths, tokens, gains, wo, mixed_heads, residual, normed):
    tile = row_tile(tokens.shape[0])

    def body(index, carry):
        here = tile_rows(index, tile)
        total = tokens[here, :].astype(jnp.float32)
        total += jnp.dot(mixed_heads[here, :], wo[...], preferred_element_type=jnp.float32)
        rounded = total.astype(jnp.bfloat16)
        residual[here, :] = rounded
        widened = rounded.astype(jnp.float32)
        normed[here, :] = (widened * inverse_rms(widened) * gains[1:2, :]).astype(jnp.bfloat16)
        return carry

    lax.fori_loop(0, live_tiles(items, lengths, tile), body, 0)


def join_heads(lengths, *arrays):
    rows = jax.ShapeDtypeStruct(arrays[0].shape, jnp.bfloat16)
    return call(join_kernel, "join_heads", (lengths,), arrays, (rows, rows))


def grow(block_group, which):
    return jnp.concatenate([block[which] for block in block_group], axis=1)


def shrink(block_group):
    rows = []
    for block in block_group:
        pieces = [block[2, i : i + LANES, :] for i in range(0, D, LANES)]
        rows.append(jnp.concatenate(pieces, axis=1))
    return jnp.concatenate(rows, axis=0)


def hidden_units(rows, blocks, finish):
    each = CHUNK // LANES
    groups = [blocks[start : start + each] for start in range(0, len(blocks), each)]
    work = [(tile, group) for tile in range(len(rows)) for group in range(len(groups))]

    def expand(tile, group):
        gate = jnp.dot(rows[tile], grow(groups[group], 0), preferred_element_type=jnp.float32)
        up = jnp.dot(rows[tile], grow(groups[group], 1), preferred_element_type=jnp.float32)
        return gate, up

    ahead = expand(*work[0])
    for number, (tile, group) in enumerate(work):
        gate, up = ahead
        if number + 1 < len(work):
            ahead = expand(*work[number + 1])
        active = (jax.nn.gelu(gate, approximate=True) * up).astype(jnp.bfloat16)
        term = jnp.dot(active, shrink(groups[group]), preferred_element_type=jnp.float32)
        grown = term if group == 0 else grown + term
        if group == len(groups) - 1:
            finish(tile, grown)


def all_tiles(tiles, every, tile, run):
    def body(index, carry):
        run([tile_rows(index, tile)])
        return carry

    lax.fori_loop(0, jnp.where(tiles == every, 0, tiles), body, 0)

    @pl.when(tiles == every)
    def _():
        run([slice(index * tile, (index + 1) * tile) for index in range(every)])


def first_kernel(items, lengths, x, *refs):
    blocks, total = refs[:-1], refs[-1]
    tile = row_tile(x.shape[0])

    def run(spans):
        def finish(number, grown):
            total[spans[number], :] = grown

        hidden_units([x[span, :] for span in spans], blocks, finish)

    all_tiles(live_tiles(items, lengths, tile), x.shape[0] // tile, tile, run)


def first_units(lengths, normed, blocks):
    out = jax.ShapeDtypeStruct(normed.shape, jnp.float32)
    return call(first_kernel, "first_units", (lengths,), (normed, *blocks), out, cost=LONG)


def their_last_kernel(items, lengths, x, before, *refs):
    blocks, total = refs[:-1], refs[-1]
    tile = row_tile(x.shape[0])

    def run(spans):
        def finish(number, grown):
            span = spans[number]
            total[span, :] = (before[span, :] + grown).astype(jnp.bfloat16)

        hidden_units([x[span, :] for span in spans], blocks, finish)

    all_tiles(live_tiles(items, lengths, tile), x.shape[0] // tile, tile, run)


def their_last_units(lengths, normed, before, blocks):
    out = jax.ShapeDtypeStruct(normed.shape, jnp.bfloat16)
    return call(their_last_kernel, "their_last_units", (lengths,), (normed, before, *blocks), out)


def own_last_kernel(items, lengths, residual, x, before, *refs):
    blocks, total = refs[:-1], refs[-1]
    tile = row_tile(x.shape[0])

    def run(spans):
        def finish(number, grown):
            span = spans[number]
            total[span, :] = before[span, :] + residual[span, :].astype(jnp.float32) + grown

        hidden_units([x[span, :] for span in spans], blocks, finish)

    all_tiles(live_tiles(items, lengths, tile), x.shape[0] // tile, tile, run)


def own_last_units(lengths, residual, normed, before, blocks):
    out = jax.ShapeDtypeStruct(normed.shape, jnp.float32)
    arrays = (residual, normed, before, *blocks)
    return call(own_last_kernel, "own_last_units", (lengths,), arrays, out)


def pool_kernel(items, lengths, gains, pool, own_total, back, vectors, candidates, summed):
    tile = row_tile(own_total.shape[0])
    every = own_total.shape[0] // tile
    tiles = live_tiles(items, lengths, tile)
    slots = 16
    slot = lax.broadcasted_iota(jnp.int32, (slots, 1), 0)
    first = jnp.zeros((slots, 1), jnp.int32)
    last = jnp.zeros((slots, 1), jnp.int32)
    begin = 0
    for item in range(items):
        end = begin + lengths[item]
        first = jnp.where(slot == item, begin, first)
        last = jnp.where(slot == item, end, last)
        begin = end

    def pool_tile(index):
        here = tile_rows(index, tile)
        total = own_total[here, :] + back[here, :].astype(jnp.float32)
        finished = total.astype(jnp.bfloat16).astype(jnp.float32)
        final_rows = (finished * inverse_rms(finished) * gains[2:3, :]).astype(jnp.bfloat16)
        across = index * tile + lax.broadcasted_iota(jnp.int32, (slots, tile), 1)
        member = jnp.where((across >= first) & (across < last), 1.0, 0.0)
        return jnp.dot(member.astype(jnp.bfloat16), final_rows, preferred_element_type=jnp.float32)

    def body(index, carry):
        summed[...] += pool_tile(index)
        return carry

    @pl.when(tiles < every)
    def _():
        summed[...] = jnp.zeros((slots, D), jnp.float32)

    lax.fori_loop(0, jnp.where(tiles < every, tiles, 0), body, 0)

    @pl.when(tiles == every)
    def _():
        summed[...] = sum(pool_tile(index) for index in range(every))

    counts = jnp.maximum(last - first, 1).astype(jnp.float32)
    pooled = (summed[...] / counts).astype(jnp.bfloat16)
    e = jnp.dot(pooled, pool[...], preferred_element_type=jnp.float32)
    e = e * inverse_rms(e)
    vectors[...] = e[:items, :]
    mine = e[:items, :].astype(jnp.bfloat16)
    for device in range(candidates.shape[0]):
        candidates[device] = mine


def pool_items(devices, lengths, *arrays):
    items = lengths.shape[0]
    out = (
        jax.ShapeDtypeStruct((items, D), jnp.float32),
        jax.ShapeDtypeStruct((devices, items, D), jnp.bfloat16),
    )
    scratch = [pltpu.VMEM((16, D), jnp.float32)]
    return call(pool_kernel, "pool_items", (lengths,), arrays, out, scratch)


def loss_kernel(items, queries, list_ids, labels, candidates, loss):
    widened = queries[...].astype(jnp.float32)
    query_unit = (widened * inverse_rms(widened)).astype(jnp.bfloat16)
    each = labels.shape[0]
    chosen = None
    for which in range(LISTS):
        place = LISTS - 1 - which
        scores = nt_dot(candidates[place * each : (place + 1) * each, :], query_unit)
        if chosen is None:
            chosen = scores
        else:
            chosen = jnp.where(list_ids[...] == which, scores, chosen)
    chosen = chosen * (score_scale / D)
    relevance = labels[...]
    relevance = jnp.concatenate(
        [relevance[start : start + items, :] for start in range(each - items, -1, -items)], axis=0
    )
    target = jnp.exp(relevance.astype(jnp.float32))
    target = target / jnp.sum(target, axis=0, keepdims=True)
    log_total = jnp.log(jnp.sum(jnp.exp(chosen), axis=0, keepdims=True))
    loss[...] = log_total - jnp.sum(target * chosen, axis=0, keepdims=True)


def list_loss(items, queries, list_ids, labels, candidates):
    count = queries.shape[0]
    return pl.pallas_call(
        functools.partial(loss_kernel, items),
        out_shape=jax.ShapeDtypeStruct((1, count), jnp.float32),
        compiler_params=pltpu.CompilerParams(vmem_limit_bytes=16 * MIB),
        name="list_loss",
    )(queries, list_ids.reshape(1, count), labels.T, candidates).reshape(count)


def swapped(value, count, bit):
    return lax.ppermute(value, "dp", [(i, i ^ bit) for i in range(count)])


def after(value, *earlier):
    return lax.optimization_barrier((value, earlier))[0]


def local(
    count,
    planes,
    tokens,
    lengths,
    norm_gains,
    query_key_value,
    attention_out,
    expand_weight,
    contract_weight,
    pool_weight,
    queries,
    list_ids,
    labels,
):
    inner = count // OUTER
    counts = [lengths, swapped(lengths, count, 1)]

    def attend(turn):
        projected = project(lengths, tokens, norm_gains, query_key_value)
        projected, counts[1] = turn(0, (projected, counts[1]))
        mixed_heads = heads(lengths, projected)
        residual, normed = join_heads(lengths, tokens, norm_gains, attention_out, mixed_heads)
        return residual, turn(1, normed), swapped(normed, count, 1)

    same_core = [list(range(first, count, 2)) for first in range(2)]
    if planes == 2 and inner == 4 and contract_weight.shape[0] == LANES:

        def hop(value, same, across, crossed):
            pairs = []
            for here in range(planes * count):
                y, place = divmod(here, count)
                z, x, c = place // inner, place % inner // 2, place % 2
                role = 0 if c == y else 1
                link = across if role else same
                if link == "y":
                    y = 1 - y
                elif link == "x":
                    x = 1 - x
                else:
                    z = (z + (1 if link == "up" else OUTER - 1)) % OUTER
                role = 1 - role if crossed else role
                pairs.append((here, y * count + z * inner + x * 2 + (1 - y if role else y)))
            return lax.ppermute(value, ("groups", "dp"), pairs)

        v = [pack_weights(expand_weight, contract_weight)]
        v.append(hop(v[0], "x", "down", True))

        def turn(number, value):
            if number == 0:
                v[1], value = after((v[1], value))
                v.append(hop(v[1], "down", "up", False))
                v.append(hop(v[1], "y", "down", False))
                v.append(hop(v[1], "x", "y", False))
            else:
                v[2], value = after((v[2], value))
                v.append(hop(v[2], "down", "y", False))
                v.append(hop(v[2], "x", "x", False))
                v.append(hop(v[2], "y", "up", False))
            return value

        residual, normed, theirs = attend(turn)
        first = tuple(v[:5])
        third = tuple(v[5:8])
        own_sum = first_units(lengths, normed, first)
    else:
        grown = lax.all_gather(
            expand_weight, "dp", axis=2, tiled=True, axis_index_groups=same_core
        )
        shrunk = lax.all_gather(
            contract_weight, "dp", axis=0, tiled=True, axis_index_groups=same_core
        )
        grown = grown.reshape(2, D, -1, LANES).transpose(2, 0, 1, 3)
        shrunk = shrunk.reshape(-1, LANES, D // LANES, LANES).transpose(0, 2, 1, 3)
        v = jnp.concatenate([grown, shrunk.reshape(-1, 1, D, LANES)], axis=1)
        residual, normed, theirs = attend(lambda number, value: value)
        first = tuple(v[:5])
        third = tuple(v[5:])
        own_sum = first_units(lengths, normed, first)

    their_sum = first_units(counts[1], theirs, first)
    third, their_sum = after((third, their_sum), own_sum)
    their_total = their_last_units(counts[1], theirs, their_sum, third)
    back = swapped(their_total, count, 1)
    normed, _ = after((normed, their_total))
    own_total = own_last_units(lengths, residual, normed, own_sum, third)
    item_vectors, candidates = pool_items(
        count, lengths, norm_gains, pool_weight, own_total, back
    )
    backwards = [list(range(count - 1, -1, -1))]
    every = lax.all_to_all(
        candidates, "dp", 0, 0, tiled=True, axis_index_groups=backwards
    )
    every = every.reshape(count * lengths.shape[0], D)
    return item_vectors, list_loss(lengths.shape[0], queries, list_ids, labels, every)


def solution(mesh):
    return jax.shard_map(
        functools.partial(local, mesh.shape["dp"], mesh.shape["groups"]),
        mesh=mesh,
        in_specs=(
            P(("groups", "dp"), None),
            P(("groups", "dp")),
            P(),
            P(),
            P(),
            P(None, None, "dp"),
            P("dp", None),
            P(),
            P(("groups", "dp"), None),
            P(("groups", "dp")),
            P(("groups", "dp"), None),
        ),
        out_specs=(P(("groups", "dp"), None), P(("groups", "dp"))),
        check_vma=False,
    )
```

```python
import functools

import jax
import jax.numpy as jnp
from jax import lax
from jax.experimental import pallas as pl
from jax.experimental.pallas import tpu as pltpu
from jax.sharding import PartitionSpec as P

D = 768
HEAD = 64
LISTS = 2
OUTER = 4
CHUNK = 256

SCORE_SCALE = HEAD ** (-0.5) * 1.4426950408889634
epsilon = 1e-06
score_scale = 32.0
MIB = 1024 * 1024
SHORT = pl.CostEstimate(flops=1000, bytes_accessed=1000, transcendentals=0)
LONG = pl.CostEstimate(flops=40_000_000_000, bytes_accessed=1000, transcendentals=0)


def inverse_rms(widened):
    return lax.rsqrt(jnp.mean(widened * widened, axis=-1, keepdims=True) + epsilon)


def nt_dot(left, right):
    return lax.dot_general(
        left, right, (((1,), (1,)), ((), ())), preferred_element_type=jnp.float32
    )


LANES = 128


def pack_kernel(expand, contract, packed, stage, come, gone):
    arrivals = [
        pltpu.make_async_copy(expand.at[which], stage.at[which], come.at[which])
        for which in range(2)
    ]
    for piece in range(D // LANES):
        columns = slice(piece * LANES, (piece + 1) * LANES)
        source, target = contract.at[:, columns], stage.at[2, columns, :]
        arrivals.append(pltpu.make_async_copy(source, target, come.at[2 + piece]))
    leavings = [
        pltpu.make_async_copy(stage.at[which], packed.at[which], gone.at[which])
        for which in range(3)
    ]
    for copy in arrivals:
        copy.start()
    for which in range(3):
        for copy in arrivals[2:] if which == 2 else arrivals[which : which + 1]:
            copy.wait()
        leavings[which].start()
    for copy in leavings:
        copy.wait()


def pack_weights(expand_weight, contract_weight):
    in_place = pl.BlockSpec(memory_space=pltpu.HBM)
    block = jax.ShapeDtypeStruct((3, D, LANES), jnp.bfloat16)
    return pl.pallas_call(
        pack_kernel,
        out_shape=block,
        in_specs=[in_place, in_place],
        out_specs=in_place,
        scratch_shapes=[
            pltpu.VMEM(block.shape, block.dtype),
            pltpu.SemaphoreType.DMA((2 + D // LANES,)),
            pltpu.SemaphoreType.DMA((3,)),
        ],
        compiler_params=pltpu.CompilerParams(vmem_limit_bytes=60 * MIB),
        name="pack_weights",
    )(expand_weight, contract_weight)


def row_tile(rows):
    return 256 if rows % 256 == 0 else rows


def live_tiles(items, lengths, tile):
    total = lengths[0]
    for item in range(1, items):
        total = total + lengths[item]
    return (total + tile - 1) // tile


def tile_rows(index, tile):
    return pl.ds(pl.multiple_of(index * tile, tile), tile)


def project_kernel(items, lengths, tokens, gains, weights, out):
    tile = row_tile(tokens.shape[0])

    def body(index, carry):
        here = tile_rows(index, tile)
        widened = tokens[here, :].astype(jnp.float32)
        x = (widened * inverse_rms(widened) * gains[0:1, :]).astype(jnp.bfloat16)
        for which in range(3):
            span = slice(which * D, (which + 1) * D)
            part = jnp.dot(x, weights[:, span], preferred_element_type=jnp.float32)
            if which == 0:
                part = part * SCORE_SCALE
            out[here, span] = part.astype(jnp.bfloat16)
        return carry

    lax.fori_loop(0, live_tiles(items, lengths, tile), body, 0)


def call(kernel, name, scalars, arrays, out_shape, scratch=(), cost=SHORT):
    whole = pl.BlockSpec(memory_space=pltpu.VMEM)
    return pl.pallas_call(
        functools.partial(kernel, scalars[0].shape[0]),
        in_specs=[pl.BlockSpec(memory_space=pltpu.SMEM)] * len(scalars) + [whole] * len(arrays),
        out_specs=jax.tree.map(lambda _: whole, out_shape),
        out_shape=out_shape,
        compiler_params=pltpu.CompilerParams(vmem_limit_bytes=24 * MIB),
        scratch_shapes=scratch,
        cost_estimate=cost,
        name=name,
    )(*scalars, *arrays)


def project(lengths, tokens, norm_gains, query_key_value):
    out = jax.ShapeDtypeStruct((tokens.shape[0], 3 * D), jnp.bfloat16)
    return call(project_kernel, "project", (lengths,), (tokens, norm_gains, query_key_value), out)


def heads_kernel(items, lengths, projected, mixed_heads):
    rows = projected.shape[0]
    tile = row_tile(rows)
    wide = 2 * HEAD
    group = D // 2
    lane = lax.broadcasted_iota(jnp.int32, (1, wide), 1) // HEAD
    ends = []
    end = 0
    for item in range(items):
        end = end + lengths[item]
        ends.append(end)
    tiles = (end + tile - 1) // tile

    def segment(position):
        return sum((position >= end).astype(jnp.int32) for end in ends)

    for keys in range(tile, rows + 1, tile):
        across = segment(lax.broadcasted_iota(jnp.int32, (1, keys), 1))

        def body(index, carry):
            row = index // 2
            here = tile_rows(row, tile)
            offset = pl.multiple_of(index % 2 * group, group)
            down = segment(row * tile + lax.broadcasted_iota(jnp.int32, (tile, 1), 0))
            same = down == across

            def columns(kind, head):
                return pl.ds(kind * D + offset + head // 2 * wide, wide)

            def scores(head):
                q = projected[here, columns(0, head)]
                q = jnp.where(lane == head % 2, q, jnp.bfloat16(0))
                return nt_dot(q, projected[:keys, columns(1, head)])

            count = group // HEAD
            ahead = scores(0)
            for head in range(count):
                logits = jnp.where(same, ahead, -1e30)
                if head + 1 < count:
                    ahead = scores(head + 1)
                highest = jnp.max(logits, axis=1, keepdims=True)
                weights = jnp.exp2((logits - highest).astype(jnp.bfloat16))
                mine = lane == head % 2
                v = jnp.where(mine, projected[:keys, columns(2, head)], jnp.bfloat16(1))
                out = jnp.dot(weights, v, preferred_element_type=jnp.float32)
                other = (1 - head % 2) * HEAD
                out = out * (1.0 / out[:, other : other + 1])
                mixed = out if head % 2 == 0 else jnp.where(mine, out, mixed)
                if head % 2 == 1:
                    mixed_heads[here, columns(0, head)] = mixed.astype(jnp.bfloat16)
            return carry

        count = keys // tile
        lax.fori_loop(0, jnp.where(tiles == count, 2 * count, 0), body, 0)


def heads(lengths, projected):
    out = jax.ShapeDtypeStruct((projected.shape[0], D), jnp.bfloat16)
    return call(heads_kernel, "heads", (lengths,), (projected,), out)


def join_kernel(items, lengths, tokens, gains, wo, mixed_heads, residual, normed):
    tile = row_tile(tokens.shape[0])

    def run(spans):
        for here in spans:
            total = tokens[here, :].astype(jnp.float32)
            total += jnp.dot(mixed_heads[here, :], wo[...], preferred_element_type=jnp.float32)
            rounded = total.astype(jnp.bfloat16)
            residual[here, :] = rounded
            widened = rounded.astype(jnp.float32)
            scaled = widened * inverse_rms(widened) * gains[1:2, :]
            normed[here, :] = scaled.astype(jnp.bfloat16)

    all_tiles(live_tiles(items, lengths, tile), tokens.shape[0] // tile, tile, run)


def join_heads(lengths, *arrays):
    rows = jax.ShapeDtypeStruct(arrays[0].shape, jnp.bfloat16)
    return call(join_kernel, "join_heads", (lengths,), arrays, (rows, rows))


def grow(block_group, which):
    return jnp.concatenate([block[which] for block in block_group], axis=1)


def shrink(block_group):
    rows = []
    for block in block_group:
        pieces = [block[2, i : i + LANES, :] for i in range(0, D, LANES)]
        rows.append(jnp.concatenate(pieces, axis=1))
    return jnp.concatenate(rows, axis=0)


def hidden_units(rows, blocks, finish):
    each = CHUNK // LANES
    groups = [blocks[start : start + each] for start in range(0, len(blocks), each)]
    work = [(tile, group) for tile in range(len(rows)) for group in range(len(groups))]

    def expand(tile, group):
        gate = jnp.dot(rows[tile], grow(groups[group], 0), preferred_element_type=jnp.float32)
        up = jnp.dot(rows[tile], grow(groups[group], 1), preferred_element_type=jnp.float32)
        return gate, up

    ahead = expand(*work[0])
    for number, (tile, group) in enumerate(work):
        gate, up = ahead
        if number + 1 < len(work):
            ahead = expand(*work[number + 1])
        active = (jax.nn.gelu(gate, approximate=True) * up).astype(jnp.bfloat16)
        term = jnp.dot(active, shrink(groups[group]), preferred_element_type=jnp.float32)
        grown = term if group == 0 else grown + term
        if group == len(groups) - 1:
            finish(tile, grown)


def all_tiles(tiles, every, tile, run):
    def body(index, carry):
        run([tile_rows(index, tile)])
        return carry

    lax.fori_loop(0, jnp.where(tiles == every, 0, tiles), body, 0)

    @pl.when(tiles == every)
    def _():
        run([slice(index * tile, (index + 1) * tile) for index in range(every)])


def first_kernel(items, lengths, x, *refs):
    blocks, total = refs[:-1], refs[-1]
    tile = row_tile(x.shape[0])

    def run(spans):
        def finish(number, grown):
            total[spans[number], :] = grown

        hidden_units([x[span, :] for span in spans], blocks, finish)

    all_tiles(live_tiles(items, lengths, tile), x.shape[0] // tile, tile, run)


def first_units(lengths, normed, blocks):
    out = jax.ShapeDtypeStruct(normed.shape, jnp.float32)
    return call(first_kernel, "first_units", (lengths,), (normed, *blocks), out, cost=LONG)


def their_last_kernel(items, lengths, x, before, *refs):
    blocks, total = refs[:-1], refs[-1]
    tile = row_tile(x.shape[0])

    def run(spans):
        def finish(number, grown):
            span = spans[number]
            total[span, :] = (before[span, :] + grown).astype(jnp.bfloat16)

        hidden_units([x[span, :] for span in spans], blocks, finish)

    all_tiles(live_tiles(items, lengths, tile), x.shape[0] // tile, tile, run)


def their_last_units(lengths, normed, before, blocks):
    out = jax.ShapeDtypeStruct(normed.shape, jnp.bfloat16)
    return call(their_last_kernel, "their_last_units", (lengths,), (normed, before, *blocks), out)


def own_last_kernel(items, lengths, residual, x, before, *refs):
    blocks, total = refs[:-1], refs[-1]
    tile = row_tile(x.shape[0])

    def run(spans):
        def finish(number, grown):
            span = spans[number]
            total[span, :] = before[span, :] + residual[span, :].astype(jnp.float32) + grown

        hidden_units([x[span, :] for span in spans], blocks, finish)

    all_tiles(live_tiles(items, lengths, tile), x.shape[0] // tile, tile, run)


def own_last_units(lengths, residual, normed, before, blocks):
    out = jax.ShapeDtypeStruct(normed.shape, jnp.float32)
    arrays = (residual, normed, before, *blocks)
    return call(own_last_kernel, "own_last_units", (lengths,), arrays, out)


def pool_kernel(items, lengths, gains, pool, own_total, back, vectors, candidates, summed):
    tile = row_tile(own_total.shape[0])
    every = own_total.shape[0] // tile
    tiles = live_tiles(items, lengths, tile)
    slots = 16
    slot = lax.broadcasted_iota(jnp.int32, (slots, 1), 0)
    first = jnp.zeros((slots, 1), jnp.int32)
    last = jnp.zeros((slots, 1), jnp.int32)
    begin = 0
    for item in range(items):
        end = begin + lengths[item]
        first = jnp.where(slot == item, begin, first)
        last = jnp.where(slot == item, end, last)
        begin = end

    def pool_tile(index):
        here = tile_rows(index, tile)
        total = own_total[here, :] + back[here, :].astype(jnp.float32)
        finished = total.astype(jnp.bfloat16).astype(jnp.float32)
        final_rows = (finished * inverse_rms(finished) * gains[2:3, :]).astype(jnp.bfloat16)
        across = index * tile + lax.broadcasted_iota(jnp.int32, (slots, tile), 1)
        member = jnp.where((across >= first) & (across < last), 1.0, 0.0)
        return jnp.dot(member.astype(jnp.bfloat16), final_rows, preferred_element_type=jnp.float32)

    def body(index, carry):
        summed[...] += pool_tile(index)
        return carry

    @pl.when(tiles < every)
    def _():
        summed[...] = jnp.zeros((slots, D), jnp.float32)

    lax.fori_loop(0, jnp.where(tiles < every, tiles, 0), body, 0)

    @pl.when(tiles == every)
    def _():
        summed[...] = sum(pool_tile(index) for index in range(every))

    counts = jnp.maximum(last - first, 1).astype(jnp.float32)
    pooled = (summed[...] / counts).astype(jnp.bfloat16)
    e = jnp.dot(pooled, pool[...], preferred_element_type=jnp.float32)
    e = e * inverse_rms(e)
    vectors[...] = e[:items, :]
    mine = e[:items, :].astype(jnp.bfloat16)
    for device in range(candidates.shape[0]):
        candidates[device] = mine


def pool_items(devices, lengths, *arrays):
    items = lengths.shape[0]
    out = (
        jax.ShapeDtypeStruct((items, D), jnp.float32),
        jax.ShapeDtypeStruct((devices, items, D), jnp.bfloat16),
    )
    scratch = [pltpu.VMEM((16, D), jnp.float32)]
    return call(pool_kernel, "pool_items", (lengths,), arrays, out, scratch)


def queries_kernel(items, queries, labels, query_unit, target):
    widened = queries[...].astype(jnp.float32)
    query_unit[...] = (widened * inverse_rms(widened)).astype(jnp.bfloat16)
    relevance = labels[...]
    starts = range(labels.shape[0] - items, -1, -items)
    relevance = jnp.concatenate([relevance[i : i + items, :] for i in starts], axis=0)
    weight = jnp.exp(relevance.astype(jnp.float32))
    target[...] = weight / jnp.sum(weight, axis=0, keepdims=True)


def prepare_queries(items, queries, labels):
    return pl.pallas_call(
        functools.partial(queries_kernel, items),
        out_shape=(
            jax.ShapeDtypeStruct(queries.shape, jnp.bfloat16),
            jax.ShapeDtypeStruct(labels.shape[::-1], jnp.float32),
        ),
        compiler_params=pltpu.CompilerParams(vmem_limit_bytes=16 * MIB),
        cost_estimate=SHORT,
        name="prepare_queries",
    )(queries, labels.T)


def loss_kernel(query_unit, list_ids, target, candidates, loss):
    each = target.shape[0]
    chosen = None
    for which in range(LISTS):
        place = LISTS - 1 - which
        scores = nt_dot(candidates[place * each : (place + 1) * each, :], query_unit[...])
        if chosen is None:
            chosen = scores
        else:
            chosen = jnp.where(list_ids[...] == which, scores, chosen)
    chosen = chosen * (score_scale / D)
    log_total = jnp.log(jnp.sum(jnp.exp(chosen), axis=0, keepdims=True))
    loss[...] = log_total - jnp.sum(target[...] * chosen, axis=0, keepdims=True)


def list_loss(query_unit, list_ids, target, candidates):
    count = query_unit.shape[0]
    return pl.pallas_call(
        loss_kernel,
        out_shape=jax.ShapeDtypeStruct((1, count), jnp.float32),
        compiler_params=pltpu.CompilerParams(vmem_limit_bytes=16 * MIB),
        name="list_loss",
    )(query_unit, list_ids.reshape(1, count), target, candidates).reshape(count)


def swapped(value, count, bit):
    return lax.ppermute(value, "dp", [(i, i ^ bit) for i in range(count)])


def after(value, *earlier):
    return lax.optimization_barrier((value, earlier))[0]


def local(
    count,
    planes,
    tokens,
    lengths,
    norm_gains,
    query_key_value,
    attention_out,
    expand_weight,
    contract_weight,
    pool_weight,
    queries,
    list_ids,
    labels,
):
    inner = count // OUTER
    counts = [lengths, swapped(lengths, count, 1)]

    def attend(turn):
        projected = project(lengths, tokens, norm_gains, query_key_value)
        projected, counts[1] = turn(0, (projected, counts[1]))
        mixed_heads = heads(lengths, projected)
        residual, normed = join_heads(lengths, tokens, norm_gains, attention_out, mixed_heads)
        return residual, turn(1, normed), swapped(normed, count, 1)

    same_core = [list(range(first, count, 2)) for first in range(2)]
    if planes == 2 and inner == 4 and contract_weight.shape[0] == LANES:

        def hop(value, same, across, crossed):
            pairs = []
            for here in range(planes * count):
                y, place = divmod(here, count)
                z, x, c = place // inner, place % inner // 2, place % 2
                role = 0 if c == y else 1
                link = across if role else same
                if link == "y":
                    y = 1 - y
                elif link == "x":
                    x = 1 - x
                else:
                    z = (z + (1 if link == "up" else OUTER - 1)) % OUTER
                role = 1 - role if crossed else role
                pairs.append((here, y * count + z * inner + x * 2 + (1 - y if role else y)))
            return lax.ppermute(value, ("groups", "dp"), pairs)

        v = [pack_weights(expand_weight, contract_weight)]
        v.append(hop(v[0], "x", "up", True))

        def turn(number, value):
            if number == 0:
                v[1], value = after((v[1], value))
                v.append(hop(v[1], "up", "down", False))
                v.append(hop(v[1], "y", "up", False))
                v.append(hop(v[1], "x", "y", False))
            else:
                v[2], value = after((v[2], value))
                v.append(hop(v[2], "up", "y", False))
                v.append(hop(v[2], "x", "x", False))
                v.append(hop(v[2], "y", "down", False))
            return value

        residual, normed, theirs = attend(turn)
        first = tuple(v[:5])
        third = tuple(v[5:8])
        own_sum = first_units(lengths, normed, first)
    else:
        grown = lax.all_gather(
            expand_weight, "dp", axis=2, tiled=True, axis_index_groups=same_core
        )
        shrunk = lax.all_gather(
            contract_weight, "dp", axis=0, tiled=True, axis_index_groups=same_core
        )
        grown = grown.reshape(2, D, -1, LANES).transpose(2, 0, 1, 3)
        shrunk = shrunk.reshape(-1, LANES, D // LANES, LANES).transpose(0, 2, 1, 3)
        v = jnp.concatenate([grown, shrunk.reshape(-1, 1, D, LANES)], axis=1)
        residual, normed, theirs = attend(lambda number, value: value)
        first = tuple(v[:5])
        third = tuple(v[5:])
        own_sum = first_units(lengths, normed, first)

    their_sum = first_units(counts[1], theirs, first)
    query_unit, target = prepare_queries(lengths.shape[0], after(queries, own_sum), labels)
    third, their_sum = after((third, their_sum), own_sum, query_unit, target)
    their_total = their_last_units(counts[1], theirs, their_sum, third)
    back = swapped(their_total, count, 1)
    normed, _ = after((normed, their_total))
    own_total = own_last_units(lengths, residual, normed, own_sum, third)
    item_vectors, candidates = pool_items(
        count, lengths, norm_gains, pool_weight, own_total, back
    )
    backwards = [list(range(count - 1, -1, -1))]
    every = lax.all_to_all(
        candidates, "dp", 0, 0, tiled=True, axis_index_groups=backwards
    )
    every = every.reshape(count * lengths.shape[0], D)
    return item_vectors, list_loss(query_unit, list_ids, target, every)


def solution(mesh):
    return jax.shard_map(
        functools.partial(local, mesh.shape["dp"], mesh.shape["groups"]),
        mesh=mesh,
        in_specs=(
            P(("groups", "dp"), None),
            P(("groups", "dp")),
            P(),
            P(),
            P(),
            P(None, None, "dp"),
            P("dp", None),
            P(),
            P(("groups", "dp"), None),
            P(("groups", "dp")),
            P(("groups", "dp"), None),
        ),
        out_specs=(P(("groups", "dp"), None), P(("groups", "dp"))),
        check_vma=False,
    )
```
